512 devices in a mesh: grp: 32 (over z_lo, y), sp: 16 (over x, z_hi, core).
Axes of the slice: x: 4, y: 4, z: 16 (z_hi: 2, z_lo: 8; z = z_hi * 8 + z_lo), core: 2. Of those that a mesh axis runs over, the one named last changes fastest.
Arguments:
- features: bfloat16 [8, 32, 32, 64, 128], P(None, None, 'sp', 'grp'), may hold values from -6 to 6
- weight_fine: bfloat16 [27, 32, 32], replicated, may hold values from -0.21875 to 0.21875
- weight_down: bfloat16 [8, 64, 32], replicated, may hold values from -0.375 to 0.375
- weight_coarse: bfloat16 [27, 64, 64], replicated, may hold values from -0.15625 to 0.15625
- cotangent: bfloat16 [32, 64, 16, 512], P('grp', None, 'sp'), may hold values from -6 to 6
Outputs:
- coarse_out: bfloat16 [32, 64, 16, 512], P('grp', None, 'sp')
- grad_input: bfloat16 [8, 32, 32, 64, 128], P(None, None, 'sp', 'grp')
- grad_fine: float32 [27, 32, 32], replicated
- grad_down: float32 [8, 64, 32], replicated
- grad_coarse: float32 [27, 64, 64], replicated
The draws below stay inside these ranges and needn't reach their ends.
All inputs are finite; a program needn't handle non-finite values.
Results may differ from the reference program's by a relative error of at most 0.013.
Values may be sent and summed in bfloat16 or wider, within the bound.
No kernel may reach another device: no remote copies, remote signals or barrier semaphores. Data moves between devices by JAX's collectives and lax.ppermute only.
A program may use at most 64 MiB of HBM per device.

```python
import math
import jax
import jax.numpy as jnp
from jax import lax

C2 = 32
C3 = 64
Z2 = 128
QUARTERS = 4
BATCH = 8
X2 = 32
Y2 = 64
X3 = 16
Y3 = 32
Z3 = 64
ZQ3 = 16
YZQ = 512


def levels(stream_key, extent, cuts, least, largest):
    factor_of, own = 1.0, jax.random.fold_in(stream_key, 6)
    for position, parts in cuts:
        heights = jnp.exp(jax.random.uniform(jax.random.fold_in(own, position), (parts,), jnp.float32, least / len(cuts), largest / len(cuts)))
        factor_of = factor_of * jnp.repeat(heights, extent[position] // parts).reshape([-1 if axis == position else 1 for axis in range(len(extent))])
    return factor_of


def centred(rng, dims, scale, most, pieces=(), held_as=jnp.bfloat16):
    values = jax.random.normal(rng, dims, jnp.float32) * scale
    if len(pieces) > 0:
        values = levels(rng, dims, pieces, -0.22, 0.18) * values
    return jnp.clip(values, min=-most, max=most).astype(held_as)


def setup_inputs(seed: int = 0) -> dict:
    key_of = jax.random.split(jax.random.key(seed), 6)
    features = centred(key_of[0], (BATCH, C2, X2, Y2, Z2), 1.0, 6.0, ((2, 16), (3, 32)))
    weight_fine = centred(key_of[1], (27, C2, C2), (27 * C2) ** -0.5, 0.21875)
    weight_down = centred(key_of[2], (8, C3, C2), (8 * C2) ** -0.5, 0.375)
    weight_coarse = centred(key_of[3], (27, C3, C3), (27 * C3) ** -0.5, 0.15625)
    cotangent = centred(key_of[4], (BATCH * QUARTERS, C3, X3, YZQ), 1.0, 6.0, ((0, 32), (2, 16)))
    return {"features": features, "weight_fine": weight_fine, "weight_down": weight_down, "weight_coarse": weight_coarse, "cotangent": cotangent}


def silu_slope(values):
    sigma = jax.nn.sigmoid(values)
    return sigma * (1.0 + values * (1.0 - sigma))

def tap_offsets(offset_index):
    return (offset_index // 9 - 1, offset_index // 3 % 3 - 1, offset_index % 3 - 1)

def convolve(field_volume, weights, transpose):
    padded = jnp.pad(field_volume.astype(jnp.float32), ((0, 0), (1, 1), (1, 1), (1, 1)))
    x_cells, y_cells, z_cells = (field_volume.shape[1], field_volume.shape[2], field_volume.shape[3])
    summed = None
    for offset_index in range(27):
        step_x, step_y, step_z = tap_offsets(offset_index)
        matrix = weights[offset_index].astype(jnp.float32)
        if transpose:
            step_x, step_y, step_z = (-step_x, -step_y, -step_z)
            matrix = matrix.T
        portion = padded[:, 1 + step_x:1 + step_x + x_cells, 1 + step_y:1 + step_y + y_cells, 1 + step_z:1 + step_z + z_cells]
        term = jnp.einsum('oc,cxyz->oxyz', matrix, portion)
        summed = term if summed is None else summed + term
    return summed

def weight_gradient(upstream, field_volume):
    padded = jnp.pad(field_volume.astype(jnp.float32), ((0, 0), (1, 1), (1, 1), (1, 1)))
    x_cells, y_cells, z_cells = (field_volume.shape[1], field_volume.shape[2], field_volume.shape[3])
    upstream = upstream.astype(jnp.float32)
    grads = []
    for offset_index in range(27):
        step_x, step_y, step_z = tap_offsets(offset_index)
        portion = padded[:, 1 + step_x:1 + step_x + x_cells, 1 + step_y:1 + step_y + y_cells, 1 + step_z:1 + step_z + z_cells]
        grads.append(jnp.einsum('oxyz,cxyz->oc', upstream, portion))
    return jnp.stack(grads)

def split_pairs(field_volume):
    chans, x_cells, y_cells, z_cells = field_volume.shape
    return field_volume.astype(jnp.float32).reshape(chans, x_cells // 2, 2, y_cells // 2, 2, z_cells // 2, 2)

def one_sample(features, upstream_block, weight_fine, weight_down, weight_coarse):
    reduction_kernel_taps = weight_down.astype(jnp.float32).reshape(2, 2, 2, C3, C2)
    pre2 = convolve(features, weight_fine, False)
    act2 = jax.nn.silu(pre2).astype(jnp.bfloat16)
    pairs = split_pairs(act2)
    third_level_down = jnp.einsum('ijloc,cxiyjzl->oxyz', reduction_kernel_taps, pairs).astype(jnp.bfloat16)
    pre3 = convolve(third_level_down, weight_coarse, False)
    coarse_out = jax.nn.silu(pre3).astype(jnp.bfloat16)
    upstream = upstream_block.astype(jnp.float32)
    dpre3 = (upstream * silu_slope(pre3)).astype(jnp.bfloat16)
    grad_coarse = weight_gradient(dpre3, third_level_down)
    ddown3 = convolve(dpre3, weight_coarse, True).astype(jnp.bfloat16)
    grad_down = jnp.einsum('oxyz,cxiyjzl->ijloc', ddown3.astype(jnp.float32), pairs).reshape(8, C3, C2)
    dact2 = jnp.einsum('ijloc,oxyz->cxiyjzl', reduction_kernel_taps, ddown3.astype(jnp.float32))
    dact2 = dact2.reshape(C2, X2, Y2, Z2).astype(jnp.bfloat16)
    dpre2 = (dact2.astype(jnp.float32) * silu_slope(pre2)).astype(jnp.bfloat16)
    grad_fine = weight_gradient(dpre2, features)
    grad_input = convolve(dpre2, weight_fine, True).astype(jnp.bfloat16)
    return (coarse_out, grad_input, grad_fine, grad_down, grad_coarse)

def reference(features, weight_fine, weight_down, weight_coarse, cotangent):
    upstream = jnp.roll(cotangent, -(QUARTERS // 2), axis=0)
    upstream = upstream.reshape(BATCH, QUARTERS, C3, X3, Y3, ZQ3)
    upstream = jnp.transpose(upstream, (0, 2, 3, 4, 1, 5)).reshape(BATCH, C3, X3, Y3, Z3)

    def mapped(pair):
        return one_sample(pair[0], pair[1], weight_fine, weight_down, weight_coarse)
    coarse_out, grad_input, grad_fine, grad_down, grad_coarse = lax.map(mapped, (features, upstream))
    coarse_out = coarse_out.reshape(BATCH, C3, X3, Y3, QUARTERS, ZQ3)
    coarse_out = jnp.transpose(coarse_out, (0, 4, 1, 2, 3, 5)).reshape(BATCH * QUARTERS, C3, X3, YZQ)
    coarse_out = jnp.roll(coarse_out, QUARTERS // 2, axis=0)
    fine_scale = 1.0 / math.sqrt(BATCH * X2 * Y2 * Z2)
    coarse_level_scale = 1.0 / math.sqrt(BATCH * X3 * Y3 * Z3)
    grad_fine = lax.optimization_barrier(jnp.sum(grad_fine, axis=0)) * fine_scale
    grad_down = lax.optimization_barrier(jnp.sum(grad_down, axis=0)) * coarse_level_scale
    grad_coarse = lax.optimization_barrier(jnp.sum(grad_coarse, axis=0)) * coarse_level_scale
    return (coarse_out, grad_input, grad_fine, grad_down, grad_coarse)
```

```python
import math
from functools import partial

import jax
import jax.numpy as jnp
import numpy as np
from jax import lax
from jax.experimental import pallas as pl
from jax.experimental.pallas import tpu as pltpu
from jax.sharding import PartitionSpec as P

QUARTERS = 4
LANES = 128
STEPS = (-1, 0, 1)
F32 = jnp.float32
BF16 = jnp.bfloat16
INTERPRET = False


def call(kernel, outs, half, *operands):
    spaces = [pltpu.SMEM] + [pltpu.VMEM] * len(operands)
    return pl.pallas_call(
        kernel,
        out_shape=outs,
        in_specs=[pl.BlockSpec(memory_space=space) for space in spaces],
        compiler_params=pltpu.CompilerParams(vmem_limit_bytes=28 * 1024 * 1024),
        interpret=INTERPRET,
    )(half, *operands)


def arrival(block, step_y, across):
    rows, cols = lax.axis_size("grp"), lax.axis_size("sp")
    pairs = []
    for row in range(rows):
        for col in range(cols):
            if 0 <= row + step_y < rows:
                source = (col + cols // 2) % cols if across else col
                pairs.append(((row + step_y) * cols + source, row * cols + col))
    return lax.ppermute(block, ("grp", "sp"), pairs)


def upper_half():
    return lax.axis_index("sp") // (lax.axis_size("sp") // 2)


def reach():
    return min(4, lax.axis_size("sp") // 2)


def joined(own, other):
    low = jnp.concatenate([own, other], axis=0)
    return jnp.where(upper_half() == 0, low, jnp.concatenate([other, own], axis=0))


def nearest(block, count):
    return jnp.where(upper_half() == 0, block[-count:], block[:count])


def fine_pieces(block):
    return [block, arrival(block[:, 1:], -1, False), arrival(block[:, :1], 1, False)]


def coarse_pieces(block):
    return [block, arrival(block, -1, False), arrival(block, 1, False)]


def silu_slope(values, sigma):
    return sigma * (1.0 + values * (1.0 - sigma))


def dot(left, right):
    return lax.dot_general(left, right, (((1,), (0,)), ((), ())), preferred_element_type=F32)


def dot_lanes(left, right):
    return lax.dot_general(left, right, (((1,), (1,)), ((), ())), preferred_element_type=F32)


def shifted(values, step, span):
    if step == 0:
        return values
    place = lax.broadcasted_iota(jnp.int32, values.shape, 1) % span
    width = values.shape[1]
    moved = pltpu.roll(values, (-step) % width, 1)
    return jnp.where(place == (span - 1 if step > 0 else 0), 0.0, moved)


def fold_taps(products, chans, span):
    total = products[chans : 2 * chans]
    total = total + shifted(products[:chans], -1, span)
    return total + shifted(products[2 * chans :], 1, span)


def fine_stack(refs, column, shift=None):
    center, before, after = refs
    cells = center.shape[0]

    def cell(x, y):
        inside = None
        if shift is not None:
            half, skip, count = shift
            inside = half == 1 if x < 0 else half == 0 if x >= count else None
            x = jnp.clip(x + skip * half, 0, cells - 1)
        elif not 0 <= x < cells:
            return jnp.zeros(center.shape[2:], center.dtype)
        value = before[x, 0] if y < 0 else after[x, 0] if y > 1 else center[x, y]
        return value if inside is None else jnp.where(inside, value, jnp.zeros_like(value))

    return jnp.concatenate(
        [
            jnp.concatenate(
                [cell(2 * column + x + a, y + b) for x in (0, 1) for y in (0, 1)], axis=1
            )
            for a in STEPS
            for b in STEPS
        ],
        axis=0,
    )


def coarse_stack(refs):
    tiles = refs[0].shape[1] // LANES
    low = lax.broadcasted_iota(jnp.int32, (refs[0].shape[0], LANES), 1) < LANES // 2
    lined = []
    for ref in (refs[1], refs[0], refs[2]):
        own = [ref[:, tile * LANES : (tile + 1) * LANES] for tile in range(tiles)]
        first = jnp.where(low, own[-1].astype(F32), 0.0)
        last = jnp.where(low, 0.0, own[0].astype(F32))
        first, last = [pltpu.roll(tile, LANES // 2, 1).astype(BF16) for tile in (first, last)]
        lined.append([first, *own, last])
    return jnp.concatenate(
        [jnp.concatenate(lined[b][a : a + tiles], axis=1) for a in range(3) for b in range(3)],
        axis=0,
    )


def own_lanes(half, extent, shape):
    lane = lax.broadcasted_iota(jnp.int32, shape, 1)
    tiles = shape[1] // LANES
    x = lane // LANES + tiles * (lane % LANES // (LANES // 2)) - (2 * tiles - extent) * half
    return (x >= 0) & (x < extent)


def down_kernel(half, *refs):
    pieces, (weights, down_weights, sort, down, sorted_act, slope) = refs[:3], refs[3:]
    columns, chans = pieces[0].shape[0] // 2, pieces[0].shape[2]
    for tile in range(columns // 2):
        acts = []
        for column in (tile, tile + columns // 2):
            products = dot(weights[...], fine_stack(pieces, column))
            parts = []
            for place in range(4):
                pre = fold_taps(products[:, place * LANES : (place + 1) * LANES], chans, LANES)
                sigma = jax.nn.sigmoid(pre)
                slope[column, place * chans : (place + 1) * chans] = silu_slope(pre, sigma)
                parts.append((pre * sigma).astype(BF16))
            acts.append(jnp.concatenate(parts, axis=0))
        parted = dot(jnp.concatenate(acts, axis=1), sort[...]).astype(BF16)
        stacked = jnp.concatenate([parted[:, :LANES], parted[:, LANES:]], axis=0)
        lanes = slice(tile * LANES, (tile + 1) * LANES)
        sorted_act[:, lanes] = stacked
        down[:, lanes] = dot(down_weights[...], stacked).astype(BF16)


def coarse_kernel(half, *refs):
    pieces, (weights, upstream, out, dpre) = refs[:3], refs[3:]
    chans, width = pieces[0].shape
    pre = fold_taps(dot(weights[...], coarse_stack(pieces)), chans, LANES // 2)
    sigma = jax.nn.sigmoid(pre)
    act = pre * sigma
    slope = silu_slope(pre, sigma)
    tiles = width // LANES
    rows = LANES // 4
    for tile in range(tiles):
        lanes = slice(tile * LANES, (tile + 1) * LANES)
        ends = [tile * rows, (tile + tiles) * rows]
        packed = jnp.concatenate([upstream[end : end + rows] for end in ends], axis=0)
        dpre[:, lanes] = (unpacked(packed.astype(F32)) * slope[:, lanes]).astype(BF16)
        both = packed_cells(act[:, lanes]).astype(BF16)
        for member, end in enumerate(ends):
            out[end : end + rows] = both[member * rows : (member + 1) * rows]


def packed_cells(values):
    turned = jnp.concatenate([values, values], axis=0).T.reshape(LANES // 16, 2, 8, LANES)
    low = lax.broadcasted_iota(jnp.int32, (LANES // 16, 8, LANES), 2) < LANES // 2
    return jnp.where(low, turned[:, 0], turned[:, 1]).reshape(LANES // 2, LANES)


def unpacked(values):
    first = values.reshape(LANES // 16, 1, 8, LANES)
    second = pltpu.roll(values, LANES // 2, 1).reshape(LANES // 16, 1, 8, LANES)
    turned = jnp.concatenate([first, second], axis=1).reshape(LANES, LANES).T
    return turned[: LANES // 2]


def pack_kernel(values, out):
    for tile in range(values.shape[1] // LANES):
        part = values[:, tile * LANES : (tile + 1) * LANES].astype(F32)
        out[tile * LANES // 2 : (tile + 1) * LANES // 2] = packed_cells(part).astype(BF16)


def unpack_kernel(values, out):
    for tile in range(out.shape[1] // LANES):
        part = values[tile * LANES // 2 : (tile + 1) * LANES // 2].astype(F32)
        out[:, tile * LANES : (tile + 1) * LANES] = unpacked(part).astype(BF16)


def tap_stack(values, span):
    values = values.astype(F32)
    return jnp.concatenate([shifted(values, -step, span).astype(BF16) for step in STEPS], axis=0)


def store_tiles(ref, base, values):
    rows, cols = values.shape
    for start in range(0, cols, LANES):
        width = min(LANES, cols - start)
        ref[base : base + rows, :width] = values[:, start : start + width].astype(ref.dtype)
        base += rows
    return base


def coarse_grad_kernel(extent, half, *refs):
    pieces, (dpre, grad) = refs[:3], refs[3:]
    grad[...] = jnp.zeros(grad.shape, grad.dtype)
    own = jnp.where(own_lanes(half[0], extent, dpre.shape), dpre[...].astype(F32), 0.0)
    products = dot_lanes(tap_stack(own, LANES // 2), coarse_stack(pieces))
    store_tiles(grad, 0, products)


def back_kernel(extent, half, *refs):
    pieces, feature_pieces = refs[:3], refs[3:6]
    weights, up_weights, unsort, sorted_act, slope, coarse_grad, dpre2, grads = refs[6:]
    chans3 = pieces[0].shape[0]
    columns, chans = feature_pieces[0].shape[0] // 2, feature_pieces[0].shape[2]
    ddown = fold_taps(dot(weights[...], coarse_stack(pieces)), chans3, LANES // 2)
    own_ddown = jnp.where(own_lanes(half[0], extent, ddown.shape), ddown, 0.0).astype(BF16)
    ddown = ddown.astype(BF16)
    spread = dot(up_weights[...], ddown).astype(BF16)
    rows = spread.shape[0] // 2
    total = None
    for tile in range(columns // 2):
        lanes = slice(tile * LANES, (tile + 1) * LANES)
        both = dot(jnp.concatenate([spread[:rows, lanes], spread[rows:, lanes]], axis=1), unsort[...])
        for member in range(2):
            column = tile + member * (columns // 2)
            dpre = both[:, member * LANES : (member + 1) * LANES] * slope[column]
            dpre = dpre.astype(BF16)
            parts = [dpre[place * chans : (place + 1) * chans] for place in range(4)]
            for place in range(4):
                dpre2[2 * column + place // 2, place % 2] = parts[place]
            place = column - (columns - extent) * half[0]
            inside = (place >= 0) & (place < extent)
            parts = [jnp.where(inside, part.astype(F32), 0.0) for part in parts]
            moved = jnp.concatenate([tap_stack(part, LANES) for part in parts], axis=1)
            term = dot_lanes(moved, fine_stack(feature_pieces, column))
            total = term if total is None else total + term
    base = coarse_grad.shape[0]
    grads[:base] = coarse_grad[...]
    grads[base:] = jnp.zeros((grads.shape[0] - base, LANES), grads.dtype)
    base = store_tiles(grads, base, total)
    store_tiles(grads, base, dot_lanes(own_ddown, sorted_act[...]))


def input_kernel(half, *refs):
    pieces, (weights, out) = refs[:3], refs[3:]
    cells, chans = pieces[0].shape[0], pieces[0].shape[2]
    count = out.shape[0]
    for column in range(count // 2):
        stack = fine_stack(pieces, column, (half[0], cells - count, count))
        products = dot(weights[...], stack)
        for place in range(4):
            total = fold_taps(products[:, place * LANES : (place + 1) * LANES], chans, LANES)
            out[2 * column + place // 2, place % 2] = total.astype(BF16)


def tap_matrix(weights):
    taps, outs, ins = weights.shape
    return jnp.transpose(weights.reshape(9, 3, outs, ins), (1, 2, 0, 3)).reshape(3 * outs, 9 * ins)


def reversed_taps(weights):
    return jnp.transpose(weights[::-1], (0, 2, 1))


def sort_matrix():
    table = np.zeros((2 * LANES, 2 * LANES), np.float32)
    for sample in range(2):
        for z in range(LANES):
            table[sample * LANES + z, (z % 2) * LANES + sample * (LANES // 2) + z // 2] = 1.0
    return table


def trade(parts, axis, groups=None):
    return lax.all_to_all(
        parts, axis, split_axis=0, concat_axis=0, axis_index_groups=groups, tiled=True
    )


def share(part, axis, groups=None):
    count = lax.axis_size(axis) if groups is None else len(groups[0])
    return trade(jnp.broadcast_to(part[None], (count, *part.shape)), axis, groups)


def turned(block, across=False):
    rows, cols = lax.axis_size("grp"), lax.axis_size("sp")
    batch, shift = cols // 2, QUARTERS // 2
    pairs = []
    for row in range(rows):
        major, quarter = divmod((row - shift) % rows, QUARTERS)
        for col in range(cols):
            there = (QUARTERS * (col % batch) + quarter + shift) % rows
            side = 1 - col // batch if across else col // batch
            pairs.append((row * cols + col, there * cols + side * batch + major))
    return lax.ppermute(block, ("grp", "sp"), pairs)


def close_groups():
    cols = lax.axis_size("sp")
    return [[col for col in range(cols) if col // 2 % 2 == far] for far in (0, 1)]


def far_groups():
    rows, cols = lax.axis_size("grp"), lax.axis_size("sp")
    return [
        [row * cols + col + far for row in range(rows) for far in (0, 2)]
        for col in range(cols)
        if col // 2 % 2 == 0
    ]


def local(features, weight_fine, weight_down, weight_coarse, cotangent):
    batch, chans, x_cells, y_cells, z_cells = features.shape
    chans3 = weight_down.shape[1]
    rows, cols = lax.axis_size("grp"), lax.axis_size("sp")
    width = batch * z_cells // 2
    extent = batch + reach()
    wider = extent * z_cells // 2
    fine_scale = 1.0 / math.sqrt(batch * x_cells * cols * y_cells * rows * z_cells)
    coarse_scale = 1.0 / math.sqrt(batch * x_cells * cols * y_cells * rows * z_cells // 8)
    shape = jax.ShapeDtypeStruct
    halves = [list(range(batch)), list(range(batch, cols))]
    near = close_groups()
    unit = len(near[0]) * rows * LANES
    grad_rows = -(-(15 * chans3 + 9 * chans + 2 * chans3) * LANES // unit) * unit // LANES
    half = upper_half().astype(jnp.int32).reshape(1)

    sort = jnp.asarray(sort_matrix(), BF16)
    unsort = jnp.asarray(sort_matrix().T, BF16)
    parted = weight_down.reshape(2, 2, 2, chans3, chans)
    down_matrix = jnp.transpose(parted, (3, 2, 0, 1, 4)).reshape(chans3, 8 * chans)

    own = trade(jnp.transpose(features, (0, 2, 3, 1, 4)), "sp", halves)
    own = own.reshape(batch * x_cells, y_cells, chans, LANES)

    block = (rows, width // 2 // rows, LANES)
    cells = pl.pallas_call(
        pack_kernel, out_shape=shape((width // 2, LANES), BF16), interpret=INTERPRET
    )(cotangent.reshape(chans3, width))
    cells = [turned(cells).reshape(block), turned(cells, True).reshape(block)]
    own, *cells = lax.optimization_barrier((own, *cells))
    own = joined(own, arrival(nearest(own, reach() * x_cells), 0, True))
    cells = jnp.roll(trade(jnp.concatenate(cells, axis=1), "grp"), -(QUARTERS // 2), axis=0)
    cells = [part.reshape(width // 2, LANES) for part in jnp.split(cells, 2, axis=1)]
    count = reach() * QUARTERS * block[1]
    other = jnp.where(upper_half() == 0, cells[1][:count], cells[1][-count:])
    upstream = joined(cells[0], other)

    feature_pieces = fine_pieces(own)
    down, sorted_act, slope = call(
        down_kernel,
        (
            shape((chans3, wider), BF16),
            shape((8 * chans, wider), BF16),
            shape((extent, 4 * chans, LANES), F32),
        ),
        half,
        *feature_pieces,
        tap_matrix(weight_fine),
        down_matrix,
        sort,
    )
    down_pieces = coarse_pieces(down)
    coarse, dpre3 = call(
        coarse_kernel,
        (shape(upstream.shape, BF16), shape((chans3, wider), BF16)),
        half,
        *down_pieces,
        tap_matrix(weight_coarse),
        upstream,
    )
    coarse_grad = call(
        partial(coarse_grad_kernel, batch),
        shape((15 * chans3, LANES), BF16),
        half,
        *down_pieces,
        dpre3,
    )
    dpre_pieces = coarse_pieces(dpre3)
    coarse_grad, *dpre_pieces = lax.optimization_barrier((coarse_grad, *dpre_pieces))

    dpre2, grads = call(
        partial(back_kernel, batch),
        (shape(own.shape, BF16), shape((grad_rows, LANES), BF16)),
        half,
        *dpre_pieces,
        *feature_pieces,
        tap_matrix(reversed_taps(weight_coarse)),
        down_matrix.T,
        unsort,
        sorted_act,
        slope,
        coarse_grad,
    )
    spread = fine_pieces(dpre2)
    part = trade(grads.reshape(len(near[0]), -1, LANES), "sp", near)
    part = jnp.sum(part.astype(F32), axis=0).astype(BF16).reshape(rows, -1, LANES)
    gradient = call(
        input_kernel,
        shape((batch * x_cells, *own.shape[1:]), BF16),
        half,
        *spread,
        tap_matrix(reversed_taps(weight_fine)),
    )
    part, gradient = lax.optimization_barrier((part, gradient))
    kept = part.shape[1]
    wide = -(-kept // 8) * 8
    coarse = jnp.where(upper_half() == 0, coarse[: width // 2], coarse[-(width // 2) :])
    coarse = jnp.roll(coarse.reshape(block), QUARTERS // 2, axis=0)
    blank = jnp.zeros((rows, wide - kept, LANES), BF16)
    mixed = trade(jnp.concatenate([part, blank, coarse], axis=1), "grp")
    part = jnp.sum(mixed[:, :wide].astype(F32), axis=0)
    part = share(part, ("grp", "sp"), far_groups()).reshape(rows, 2, wide, LANES)
    grads = (part[:, 0] + part[:, 1])[:, :kept].reshape(rows * kept, LANES)
    grads = share(grads, "sp", near).reshape(grad_rows, LANES)

    grads, gradient = lax.optimization_barrier((grads, gradient))
    gradient = trade(gradient.reshape(batch, x_cells, y_cells, chans, LANES), "sp", halves)
    grad_input = jnp.transpose(gradient, (0, 3, 1, 2, 4))

    result = pl.pallas_call(
        unpack_kernel, out_shape=shape((chans3, width), BF16), interpret=INTERPRET
    )(turned(mixed[:, wide:].reshape(width // 2, LANES)))
    result = result.reshape(cotangent.shape)

    grad_coarse = grads[: 15 * chans3].reshape(5, 3, chans3, 2, chans3)
    grad_coarse = jnp.transpose(grad_coarse, (0, 3, 1, 2, 4)).reshape(30, chans3, chans3)[:27]
    grads = grads[15 * chans3 :]
    grad_fine = grads[: 9 * chans].reshape(3, 3, chans, 4, chans)
    grad_fine = jnp.transpose(grad_fine, (0, 3, 1, 2, 4)).reshape(36, chans, chans)[:27]
    grad_down = grads[9 * chans : 9 * chans + 2 * chans3].reshape(2, chans3, 4, chans)
    grad_down = jnp.transpose(grad_down, (2, 0, 1, 3)).reshape(8, chans3, chans)
    return (
        result,
        grad_input,
        grad_fine * fine_scale,
        grad_down * coarse_scale,
        grad_coarse * coarse_scale,
    )


def solution(mesh):
    placed = (P(None, None, "sp", "grp", None), P(), P(), P(), P("grp", None, "sp", None))
    return jax.shard_map(
        local,
        mesh=mesh,
        in_specs=placed,
        out_specs=(P("grp", None, "sp", None), P(None, None, "sp", "grp", None), P(), P(), P()),
        check_vma=False,
    )
```

```python
import math
from functools import partial

import jax
import jax.numpy as jnp
import numpy as np
from jax import lax
from jax.experimental import pallas as pl
from jax.experimental.pallas import tpu as pltpu
from jax.sharding import PartitionSpec as P

QUARTERS = 4
LANES = 128
STEPS = (-1, 0, 1)
F32 = jnp.float32
BF16 = jnp.bfloat16
INTERPRET = False


def call(kernel, outs, half, *operands):
    spaces = [pltpu.SMEM] + [pltpu.VMEM] * len(operands)
    return pl.pallas_call(
        kernel,
        out_shape=outs,
        in_specs=[pl.BlockSpec(memory_space=space) for space in spaces],
        compiler_params=pltpu.CompilerParams(vmem_limit_bytes=28 * 1024 * 1024),
        interpret=INTERPRET,
    )(half, *operands)


def arrival(block, step_y, across):
    rows, cols = lax.axis_size("grp"), lax.axis_size("sp")
    pairs = []
    for row in range(rows):
        for col in range(cols):
            if 0 <= row + step_y < rows:
                source = (col + cols // 2) % cols if across else col
                pairs.append(((row + step_y) * cols + source, row * cols + col))
    return lax.ppermute(block, ("grp", "sp"), pairs)


def upper_half():
    return lax.axis_index("sp") // (lax.axis_size("sp") // 2)


def reach():
    return min(4, lax.axis_size("sp") // 2)


def joined(own, other):
    low = jnp.concatenate([own, other], axis=0)
    return jnp.where(upper_half() == 0, low, jnp.concatenate([other, own], axis=0))


def nearest(block, count):
    return jnp.where(upper_half() == 0, block[-count:], block[:count])


def fine_pieces(block):
    return [block, arrival(block[:, 1:], -1, False), arrival(block[:, :1], 1, False)]


def coarse_pieces(block):
    return [block, arrival(block, -1, False), arrival(block, 1, False)]


def silu_slope(values, sigma):
    return sigma * (1.0 + values * (1.0 - sigma))


def dot(left, right):
    return lax.dot_general(left, right, (((1,), (0,)), ((), ())), preferred_element_type=F32)


def dot_lanes(left, right):
    return lax.dot_general(left, right, (((1,), (1,)), ((), ())), preferred_element_type=F32)


def shifted(values, step, span):
    if step == 0:
        return values
    place = lax.broadcasted_iota(jnp.int32, values.shape, 1) % span
    width = values.shape[1]
    moved = pltpu.roll(values, (-step) % width, 1)
    return jnp.where(place == (span - 1 if step > 0 else 0), 0.0, moved)


def fold_taps(products, chans, span):
    total = products[chans : 2 * chans]
    total = total + shifted(products[:chans], -1, span)
    return total + shifted(products[2 * chans :], 1, span)


def fine_stack(refs, column, shift=None):
    center, before, after = refs
    cells = center.shape[0]

    def cell(x, y):
        inside = None
        if shift is not None:
            half, skip, count = shift
            inside = half == 1 if x < 0 else half == 0 if x >= count else None
            x = jnp.clip(x + skip * half, 0, cells - 1)
        elif not 0 <= x < cells:
            return jnp.zeros(center.shape[2:], center.dtype)
        value = before[x, 0] if y < 0 else after[x, 0] if y > 1 else center[x, y]
        return value if inside is None else jnp.where(inside, value, jnp.zeros_like(value))

    return jnp.concatenate(
        [
            jnp.concatenate(
                [cell(2 * column + x + a, y + b) for x in (0, 1) for y in (0, 1)], axis=1
            )
            for a in STEPS
            for b in STEPS
        ],
        axis=0,
    )


def coarse_stack(refs):
    tiles = refs[0].shape[1] // LANES
    low = lax.broadcasted_iota(jnp.int32, (refs[0].shape[0], LANES), 1) < LANES // 2
    lined = []
    for ref in (refs[1], refs[0], refs[2]):
        own = [ref[:, tile * LANES : (tile + 1) * LANES] for tile in range(tiles)]
        first = jnp.where(low, own[-1].astype(F32), 0.0)
        last = jnp.where(low, 0.0, own[0].astype(F32))
        first, last = [pltpu.roll(tile, LANES // 2, 1).astype(BF16) for tile in (first, last)]
        lined.append([first, *own, last])
    return jnp.concatenate(
        [jnp.concatenate(lined[b][a : a + tiles], axis=1) for a in range(3) for b in range(3)],
        axis=0,
    )


def own_lanes(half, extent, shape):
    lane = lax.broadcasted_iota(jnp.int32, shape, 1)
    tiles = shape[1] // LANES
    x = lane // LANES + tiles * (lane % LANES // (LANES // 2)) - (2 * tiles - extent) * half
    return (x >= 0) & (x < extent)


def down_kernel(half, *refs):
    pieces, (weights, down_weights, sort, down, sorted_act, slope) = refs[:3], refs[3:]
    columns, chans = pieces[0].shape[0] // 2, pieces[0].shape[2]
    for tile in range(columns // 2):
        acts = []
        for column in (tile, tile + columns // 2):
            products = dot(weights[...], fine_stack(pieces, column))
            parts = []
            for place in range(4):
                pre = fold_taps(products[:, place * LANES : (place + 1) * LANES], chans, LANES)
                sigma = jax.nn.sigmoid(pre)
                slope[column, place * chans : (place + 1) * chans] = silu_slope(pre, sigma)
                parts.append((pre * sigma).astype(BF16))
            acts.append(jnp.concatenate(parts, axis=0))
        parted = dot(jnp.concatenate(acts, axis=1), sort[...]).astype(BF16)
        stacked = jnp.concatenate([parted[:, :LANES], parted[:, LANES:]], axis=0)
        lanes = slice(tile * LANES, (tile + 1) * LANES)
        sorted_act[:, lanes] = stacked
        down[:, lanes] = dot(down_weights[...], stacked).astype(BF16)


def coarse_kernel(half, *refs):
    pieces, (weights, upstream, out, dpre) = refs[:3], refs[3:]
    chans, width = pieces[0].shape
    pre = fold_taps(dot(weights[...], coarse_stack(pieces)), chans, LANES // 2)
    sigma = jax.nn.sigmoid(pre)
    act = pre * sigma
    slope = silu_slope(pre, sigma)
    tiles = width // LANES
    rows = LANES // 4
    for tile in range(tiles):
        lanes = slice(tile * LANES, (tile + 1) * LANES)
        ends = [tile * rows, (tile + tiles) * rows]
        packed = jnp.concatenate([upstream[end : end + rows] for end in ends], axis=0)
        dpre[:, lanes] = (unpacked(packed.astype(F32)) * slope[:, lanes]).astype(BF16)
        both = packed_cells(act[:, lanes]).astype(BF16)
        for member, end in enumerate(ends):
            out[end : end + rows] = both[member * rows : (member + 1) * rows]


def packed_cells(values):
    turned = jnp.concatenate([values, values], axis=0).T.reshape(LANES // 16, 2, 8, LANES)
    low = lax.broadcasted_iota(jnp.int32, (LANES // 16, 8, LANES), 2) < LANES // 2
    return jnp.where(low, turned[:, 0], turned[:, 1]).reshape(LANES // 2, LANES)


def unpacked(values):
    first = values.reshape(LANES // 16, 1, 8, LANES)
    second = pltpu.roll(values, LANES // 2, 1).reshape(LANES // 16, 1, 8, LANES)
    turned = jnp.concatenate([first, second], axis=1).reshape(LANES, LANES).T
    return turned[: LANES // 2]


def pack_kernel(values, out):
    for tile in range(values.shape[1] // LANES):
        part = values[:, tile * LANES : (tile + 1) * LANES].astype(F32)
        out[tile * LANES // 2 : (tile + 1) * LANES // 2] = packed_cells(part).astype(BF16)


def unpack_kernel(values, out):
    for tile in range(out.shape[1] // LANES):
        part = values[tile * LANES // 2 : (tile + 1) * LANES // 2].astype(F32)
        out[:, tile * LANES : (tile + 1) * LANES] = unpacked(part).astype(BF16)


def tap_stack(values, span):
    values = values.astype(F32)
    return jnp.concatenate([shifted(values, -step, span).astype(BF16) for step in STEPS], axis=0)


def store_tiles(ref, base, values):
    rows, cols = values.shape
    for start in range(0, cols, LANES):
        width = min(LANES, cols - start)
        ref[base : base + rows, :width] = values[:, start : start + width].astype(ref.dtype)
        base += rows
    return base


def coarse_grad_kernel(extent, half, *refs):
    pieces, (dpre, grad) = refs[:3], refs[3:]
    own = jnp.where(own_lanes(half[0], extent, dpre.shape), dpre[...].astype(F32), 0.0)
    products = dot_lanes(tap_stack(own, LANES // 2), coarse_stack(pieces))
    rows, cols = products.shape
    base = store_tiles(grad, 0, products[:, : cols - LANES // 2])
    last = products[:, cols - LANES // 2 :]
    grad[base:] = jnp.concatenate([last[: rows // 2], last[rows // 2 :]], axis=1).astype(grad.dtype)


def back_kernel(extent, half, *refs):
    pieces, feature_pieces = refs[:3], refs[3:6]
    weights, up_weights, unsort, sorted_act, slope, coarse_grad, dpre2, grads = refs[6:]
    chans3 = pieces[0].shape[0]
    columns, chans = feature_pieces[0].shape[0] // 2, feature_pieces[0].shape[2]
    ddown = fold_taps(dot(weights[...], coarse_stack(pieces)), chans3, LANES // 2)
    own_ddown = jnp.where(own_lanes(half[0], extent, ddown.shape), ddown, 0.0).astype(BF16)
    ddown = ddown.astype(BF16)
    spread = dot(up_weights[...], ddown).astype(BF16)
    rows = spread.shape[0] // 2
    total = None
    for tile in range(columns // 2):
        lanes = slice(tile * LANES, (tile + 1) * LANES)
        both = dot(jnp.concatenate([spread[:rows, lanes], spread[rows:, lanes]], axis=1), unsort[...])
        for member in range(2):
            column = tile + member * (columns // 2)
            dpre = both[:, member * LANES : (member + 1) * LANES] * slope[column]
            dpre = dpre.astype(BF16)
            parts = [dpre[place * chans : (place + 1) * chans] for place in range(4)]
            for place in range(4):
                dpre2[2 * column + place // 2, place % 2] = parts[place]
            place = column - (columns - extent) * half[0]
            inside = (place >= 0) & (place < extent)
            parts = [jnp.where(inside, part.astype(F32), 0.0) for part in parts]
            moved = jnp.concatenate([tap_stack(part, LANES) for part in parts], axis=1)
            term = dot_lanes(moved, fine_stack(feature_pieces, column))
            total = term if total is None else total + term
    base = coarse_grad.shape[0]
    grads[:base] = coarse_grad[...]
    grads[base:] = jnp.zeros((grads.shape[0] - base, LANES), grads.dtype)
    base = store_tiles(grads, base, total)
    store_tiles(grads, base, dot_lanes(own_ddown, sorted_act[...]))


def input_kernel(half, *refs):
    pieces, (weights, out) = refs[:3], refs[3:]
    cells, chans = pieces[0].shape[0], pieces[0].shape[2]
    count = out.shape[0]
    for column in range(count // 2):
        stack = fine_stack(pieces, column, (half[0], cells - count, count))
        products = dot(weights[...], stack)
        for place in range(4):
            total = fold_taps(products[:, place * LANES : (place + 1) * LANES], chans, LANES)
            out[2 * column + place // 2, place % 2] = total.astype(BF16)


def tap_matrix(weights):
    taps, outs, ins = weights.shape
    return jnp.transpose(weights.reshape(9, 3, outs, ins), (1, 2, 0, 3)).reshape(3 * outs, 9 * ins)


def reversed_taps(weights):
    return jnp.transpose(weights[::-1], (0, 2, 1))


def sort_matrix():
    table = np.zeros((2 * LANES, 2 * LANES), np.float32)
    for sample in range(2):
        for z in range(LANES):
            table[sample * LANES + z, (z % 2) * LANES + sample * (LANES // 2) + z // 2] = 1.0
    return table


def trade(parts, axis, groups=None):
    return lax.all_to_all(
        parts, axis, split_axis=0, concat_axis=0, axis_index_groups=groups, tiled=True
    )


def share(part, axis, groups=None):
    count = lax.axis_size(axis) if groups is None else len(groups[0])
    return trade(jnp.broadcast_to(part[None], (count, *part.shape)), axis, groups)


def turned(block):
    rows, cols = lax.axis_size("grp"), lax.axis_size("sp")
    batch, shift = cols // 2, QUARTERS // 2
    pairs = []
    for row in range(rows):
        major, quarter = divmod((row - shift) % rows, QUARTERS)
        for col in range(cols):
            there = (QUARTERS * (col % batch) + quarter + shift) % rows
            pairs.append((row * cols + col, there * cols + col // batch * batch + major))
    return lax.ppermute(block, ("grp", "sp"), pairs)


def planes():
    rows, cols = lax.axis_size("grp"), lax.axis_size("sp")
    return [
        [row * cols + col for row in range(start, start + 4) for col in range(cols) if col & 2 == far]
        for start in range(0, rows, 4)
        for far in (0, 2)
    ]


def columns():
    rows, cols = lax.axis_size("grp"), lax.axis_size("sp")
    return [
        [row * cols + col + far for row in range(y, rows, 4) for far in (0, 2)]
        for y in range(4)
        for col in range(cols)
        if col & 2 == 0
    ]


def late():
    return (lax.axis_index("grp") % 4 < 2).astype(jnp.int32)


def for_plane(cells):
    lead = cells.shape[0] // 4
    parts = cells.reshape(lead, 2, 2, QUARTERS, 8, LANES)
    parts = jnp.roll(jnp.transpose(parts, (3, 0, 2, 1, 4, 5)), QUARTERS // 2, axis=0)
    blank = jnp.zeros_like(parts)
    low = upper_half() == 0
    both = [jnp.where(low, parts, blank), jnp.where(low, blank, parts)]
    return jnp.concatenate(both, axis=1).reshape(-1, 16, LANES)


def for_column(got):
    lead = lax.axis_size("sp") // 8
    parts = got.reshape(4, 2, lead, 2, 2, 8, LANES)
    parts = jnp.where(upper_half() == 0, parts[:, 0], parts[:, 1])
    parts = jnp.transpose(parts, (1, 2, 3, 0, 4, 5))
    parts = jnp.stack([parts, jnp.zeros_like(parts)], axis=1).reshape(4 * lead, 2, 32, LANES)
    steps = 4 * lead
    shift = 2 * far_side() + late()
    twice = jnp.concatenate([parts, parts], axis=0)
    return lax.dynamic_slice_in_dim(twice, steps - shift, steps, axis=0).reshape(-1, 32, LANES)


def from_column(got):
    parts = got.reshape(-1, 2, 32, LANES)
    steps = parts.shape[0]
    sample = (lax.axis_index("grp") // 4 - late()) % steps
    return jnp.where(sample // 2 % 2 == 0, parts[:, 0], parts[:, 1]).reshape(-1, LANES)


def far_side():
    return lax.axis_index("sp") // 2 % 2


def far_exchange(parts):
    near = far_side() == 0
    kept = jnp.where(near, parts[:, 0], parts[:, 1])
    sent = jnp.where(near, parts[:, 1], parts[:, 0])
    got = lax.ppermute(sent, "sp", [(col, col ^ 2) for col in range(lax.axis_size("sp"))])
    return jnp.stack([jnp.where(near, kept, got), jnp.where(near, got, kept)], axis=1)


def near_exchange(parts):
    cols = lax.axis_size("sp")
    lead = parts.shape[0]
    groups = [
        [start + 4 * far + core for far in range(lead) for core in (0, 1)]
        for half in range(0, cols, 4 * lead)
        for start in (half, half + 2)
    ]
    rest = parts.shape[3:]
    parts = jnp.swapaxes(parts, 1, 2).reshape(2 * lead, 2, *rest)
    return jnp.swapaxes(trade(parts, "sp", groups).reshape(lead, 2, 2, *rest), 1, 2)


def local(features, weight_fine, weight_down, weight_coarse, cotangent):
    batch, chans, x_cells, y_cells, z_cells = features.shape
    chans3 = weight_down.shape[1]
    rows, cols = lax.axis_size("grp"), lax.axis_size("sp")
    width = batch * z_cells // 2
    extent = batch + reach()
    wider = extent * z_cells // 2
    fine_scale = 1.0 / math.sqrt(batch * x_cells * cols * y_cells * rows * z_cells)
    coarse_scale = 1.0 / math.sqrt(batch * x_cells * cols * y_cells * rows * z_cells // 8)
    shape = jax.ShapeDtypeStruct
    near = planes()
    unit = len(near[0]) * 8
    grad_rows = -(-(27 * chans3 // 2 + 9 * chans + 2 * chans3) // unit) * unit
    half = upper_half().astype(jnp.int32).reshape(1)

    sort = jnp.asarray(sort_matrix(), BF16)
    unsort = jnp.asarray(sort_matrix().T, BF16)
    parted = weight_down.reshape(2, 2, 2, chans3, chans)
    down_matrix = jnp.transpose(parted, (3, 2, 0, 1, 4)).reshape(chans3, 8 * chans)

    halves = [list(range(batch)), list(range(batch, cols))]
    own = trade(jnp.transpose(features, (0, 2, 3, 1, 4)), "sp", halves)
    own = own.reshape(batch * x_cells, y_cells, chans, LANES)

    block = (rows, width // 2 // rows, LANES)
    cells = pl.pallas_call(
        pack_kernel, out_shape=shape((width // 2, LANES), BF16), interpret=INTERPRET
    )(cotangent.reshape(chans3, width))
    cells = turned(cells).reshape(block)
    matrices = [
        tap_matrix(weight_fine),
        tap_matrix(reversed_taps(weight_fine)),
        tap_matrix(weight_coarse),
        tap_matrix(reversed_taps(weight_coarse)),
        down_matrix,
        down_matrix.T,
    ]
    own, cells, *matrices = lax.optimization_barrier((own, cells, *matrices))
    fine_matrix, fine_back, coarse_matrix, coarse_back, down_matrix, up_matrix = matrices
    own = joined(own, arrival(nearest(own, reach() * x_cells), 0, True))
    cells = jnp.roll(trade(cells, "grp"), -(QUARTERS // 2), axis=0).reshape(width // 2, LANES)
    upstream = joined(cells, arrival(nearest(cells, reach() * QUARTERS * block[1]), 0, True))

    feature_pieces = fine_pieces(own)
    down, sorted_act, slope = call(
        down_kernel,
        (
            shape((chans3, wider), BF16),
            shape((8 * chans, wider), BF16),
            shape((extent, 4 * chans, LANES), F32),
        ),
        half,
        *feature_pieces,
        fine_matrix,
        down_matrix,
        sort,
    )
    down_pieces = coarse_pieces(down)
    coarse, dpre3 = call(
        coarse_kernel,
        (shape(upstream.shape, BF16), shape((chans3, wider), BF16)),
        half,
        *down_pieces,
        coarse_matrix,
        upstream,
    )
    coarse_grad = call(
        partial(coarse_grad_kernel, batch),
        shape((27 * chans3 // 2, LANES), BF16),
        half,
        *down_pieces,
        dpre3,
    )
    dpre_pieces = coarse_pieces(dpre3)
    coarse_grad, *dpre_pieces = lax.optimization_barrier((coarse_grad, *dpre_pieces))

    dpre2, grads = call(
        partial(back_kernel, batch),
        (shape(own.shape, BF16), shape((grad_rows, LANES), BF16)),
        half,
        *dpre_pieces,
        *feature_pieces,
        coarse_back,
        up_matrix,
        unsort,
        sorted_act,
        slope,
        coarse_grad,
    )
    coarse = jnp.where(upper_half() == 0, coarse[: width // 2], coarse[-(width // 2) :])
    grads = grads.reshape(len(near[0]), -1, LANES)
    kept = grads.shape[1]
    coarse = for_plane(coarse.reshape(batch, QUARTERS, 8, LANES))
    mixed = trade(jnp.concatenate([grads, coarse], axis=1), ("grp", "sp"), near)
    part = jnp.sum(mixed[:, :kept].astype(F32), axis=0).astype(BF16)
    coarse = for_column(mixed[:, kept:])
    gradient = call(
        input_kernel,
        shape((batch * x_cells, *own.shape[1:]), BF16),
        half,
        *fine_pieces(dpre2),
        fine_back,
    )
    part, gradient, coarse = lax.optimization_barrier((part, gradient, coarse))
    gradient = far_exchange(gradient.reshape(batch // 4, 2, 2, x_cells, y_cells, chans, LANES))
    part = jnp.broadcast_to(part[None], (coarse.shape[0], *part.shape))
    mixed = trade(jnp.concatenate([part, coarse], axis=1), ("grp", "sp"), columns())
    part = jnp.sum(mixed[:, :kept].astype(F32), axis=0)
    coarse = from_column(mixed[:, kept:])
    grads = share(part, ("grp", "sp"), near).reshape(grad_rows, LANES)
    grads, gradient = lax.optimization_barrier((grads, gradient))
    gradient = near_exchange(gradient).reshape(batch, x_cells, y_cells, chans, LANES)
    grad_input = jnp.transpose(gradient, (0, 3, 1, 2, 4))

    result = pl.pallas_call(
        unpack_kernel, out_shape=shape((chans3, width), BF16), interpret=INTERPRET
    )(coarse)
    result = result.reshape(cotangent.shape)

    grad_coarse = grads[: 12 * chans3].reshape(4, 3, chans3, 2, chans3)
    grad_coarse = jnp.transpose(grad_coarse, (0, 3, 1, 2, 4)).reshape(24, chans3, chans3)
    last = grads[12 * chans3 : 27 * chans3 // 2].reshape(-1, 2, chans3)
    last = jnp.swapaxes(last, 0, 1).reshape(3, chans3, chans3)
    grad_coarse = jnp.concatenate([grad_coarse, last], axis=0)
    grads = grads[27 * chans3 // 2 :]
    grad_fine = grads[: 9 * chans].reshape(3, 3, chans, 4, chans)
    grad_fine = jnp.transpose(grad_fine, (0, 3, 1, 2, 4)).reshape(36, chans, chans)[:27]
    grad_down = grads[9 * chans : 9 * chans + 2 * chans3].reshape(2, chans3, 4, chans)
    grad_down = jnp.transpose(grad_down, (2, 0, 1, 3)).reshape(8, chans3, chans)
    return (
        result,
        grad_input,
        grad_fine * fine_scale,
        grad_down * coarse_scale,
        grad_coarse * coarse_scale,
    )


def solution(mesh):
    placed = (P(None, None, "sp", "grp", None), P(), P(), P(), P("grp", None, "sp", None))
    return jax.shard_map(
        local,
        mesh=mesh,
        in_specs=placed,
        out_specs=(P("grp", None, "sp", None), P(None, None, "sp", "grp", None), P(), P(), P()),
        check_vma=False,
    )
```

```python
import math
from functools import partial

import jax
import jax.numpy as jnp
import numpy as np
from jax import lax
from jax.experimental import pallas as pl
from jax.experimental.pallas import tpu as pltpu
from jax.sharding import PartitionSpec as P

QUARTERS = 4
LANES = 128
STEPS = (-1, 0, 1)
F32 = jnp.float32
BF16 = jnp.bfloat16
INTERPRET = False


def call(kernel, outs, half, *operands):
    spaces = [pltpu.SMEM] + [pltpu.VMEM] * len(operands)
    return pl.pallas_call(
        kernel,
        out_shape=outs,
        in_specs=[pl.BlockSpec(memory_space=space) for space in spaces],
        compiler_params=pltpu.CompilerParams(vmem_limit_bytes=28 * 1024 * 1024),
        interpret=INTERPRET,
    )(half, *operands)


def arrival(block, step_y, across):
    rows, cols = lax.axis_size("grp"), lax.axis_size("sp")
    pairs = []
    for row in range(rows):
        for col in range(cols):
            if 0 <= row + step_y < rows:
                source = (col + cols // 2) % cols if across else col
                pairs.append(((row + step_y) * cols + source, row * cols + col))
    return lax.ppermute(block, ("grp", "sp"), pairs)


def upper_half():
    return lax.axis_index("sp") // (lax.axis_size("sp") // 2)


def reach():
    return min(4, lax.axis_size("sp") // 2)


def joined(own, other):
    low = jnp.concatenate([own, other], axis=0)
    return jnp.where(upper_half() == 0, low, jnp.concatenate([other, own], axis=0))


def nearest(block, count):
    return jnp.where(upper_half() == 0, block[-count:], block[:count])


def fine_pieces(block):
    return [block, arrival(block[:, 1:], -1, False), arrival(block[:, :1], 1, False)]


def coarse_pieces(block):
    return [block, arrival(block, -1, False), arrival(block, 1, False)]


def silu_slope(values, sigma):
    return sigma * (1.0 + values * (1.0 - sigma))


def dot(left, right):
    return lax.dot_general(left, right, (((1,), (0,)), ((), ())), preferred_element_type=F32)


def dot_lanes(left, right):
    return lax.dot_general(left, right, (((1,), (1,)), ((), ())), preferred_element_type=F32)


def shifted(values, step, span):
    if step == 0:
        return values
    place = lax.broadcasted_iota(jnp.int32, values.shape, 1) % span
    width = values.shape[1]
    moved = pltpu.roll(values, (-step) % width, 1)
    return jnp.where(place == (span - 1 if step > 0 else 0), 0.0, moved)


def fold_taps(products, chans, span):
    total = products[chans : 2 * chans]
    total = total + shifted(products[:chans], -1, span)
    return total + shifted(products[2 * chans :], 1, span)


def fine_stack(refs, column, shift=None):
    center, before, after = refs
    cells = center.shape[0]

    def cell(x, y):
        inside = None
        if shift is not None:
            half, skip, count = shift
            inside = half == 1 if x < 0 else half == 0 if x >= count else None
            x = jnp.clip(x + skip * half, 0, cells - 1)
        elif not 0 <= x < cells:
            return jnp.zeros(center.shape[2:], center.dtype)
        value = before[x, 0] if y < 0 else after[x, 0] if y > 1 else center[x, y]
        return value if inside is None else jnp.where(inside, value, jnp.zeros_like(value))

    return jnp.concatenate(
        [
            jnp.concatenate(
                [cell(2 * column + x + a, y + b) for x in (0, 1) for y in (0, 1)], axis=1
            )
            for a in STEPS
            for b in STEPS
        ],
        axis=0,
    )


def coarse_stack(refs):
    tiles = refs[0].shape[1] // LANES
    low = lax.broadcasted_iota(jnp.int32, (refs[0].shape[0], LANES), 1) < LANES // 2
    lined = []
    for ref in (refs[1], refs[0], refs[2]):
        own = [ref[:, tile * LANES : (tile + 1) * LANES] for tile in range(tiles)]
        first = jnp.where(low, own[-1].astype(F32), 0.0)
        last = jnp.where(low, 0.0, own[0].astype(F32))
        first, last = [pltpu.roll(tile, LANES // 2, 1).astype(BF16) for tile in (first, last)]
        lined.append([first, *own, last])
    return jnp.concatenate(
        [jnp.concatenate(lined[b][a : a + tiles], axis=1) for a in range(3) for b in range(3)],
        axis=0,
    )


def own_lanes(half, extent, shape):
    lane = lax.broadcasted_iota(jnp.int32, shape, 1)
    tiles = shape[1] // LANES
    x = lane // LANES + tiles * (lane % LANES // (LANES // 2)) - (2 * tiles - extent) * half
    return (x >= 0) & (x < extent)


def down_kernel(half, *refs):
    pieces, (weights, down_weights, sort, down, sorted_act, slope) = refs[:3], refs[3:]
    columns, chans = pieces[0].shape[0] // 2, pieces[0].shape[2]
    for tile in range(columns // 2):
        acts = []
        for column in (tile, tile + columns // 2):
            products = dot(weights[...], fine_stack(pieces, column))
            parts = []
            for place in range(4):
                pre = fold_taps(products[:, place * LANES : (place + 1) * LANES], chans, LANES)
                sigma = jax.nn.sigmoid(pre)
                slope[column, place * chans : (place + 1) * chans] = silu_slope(pre, sigma)
                parts.append((pre * sigma).astype(BF16))
            acts.append(jnp.concatenate(parts, axis=0))
        parted = dot(jnp.concatenate(acts, axis=1), sort[...]).astype(BF16)
        stacked = jnp.concatenate([parted[:, :LANES], parted[:, LANES:]], axis=0)
        lanes = slice(tile * LANES, (tile + 1) * LANES)
        sorted_act[:, lanes] = stacked
        down[:, lanes] = dot(down_weights[...], stacked).astype(BF16)


def coarse_kernel(half, *refs):
    pieces, (weights, upstream, out, dpre) = refs[:3], refs[3:]
    chans, width = pieces[0].shape
    pre = fold_taps(dot(weights[...], coarse_stack(pieces)), chans, LANES // 2)
    sigma = jax.nn.sigmoid(pre)
    act = pre * sigma
    slope = silu_slope(pre, sigma)
    tiles = width // LANES
    rows = LANES // 4
    for tile in range(tiles):
        lanes = slice(tile * LANES, (tile + 1) * LANES)
        ends = [tile * rows, (tile + tiles) * rows]
        packed = jnp.concatenate([upstream[end : end + rows] for end in ends], axis=0)
        dpre[:, lanes] = (unpacked(packed.astype(F32)) * slope[:, lanes]).astype(BF16)
        both = packed_cells(act[:, lanes]).astype(BF16)
        for member, end in enumerate(ends):
            out[end : end + rows] = both[member * rows : (member + 1) * rows]


def packed_cells(values):
    turned = jnp.concatenate([values, values], axis=0).T.reshape(LANES // 16, 2, 8, LANES)
    low = lax.broadcasted_iota(jnp.int32, (LANES // 16, 8, LANES), 2) < LANES // 2
    return jnp.where(low, turned[:, 0], turned[:, 1]).reshape(LANES // 2, LANES)


def unpacked(values):
    first = values.reshape(LANES // 16, 1, 8, LANES)
    second = pltpu.roll(values, LANES // 2, 1).reshape(LANES // 16, 1, 8, LANES)
    turned = jnp.concatenate([first, second], axis=1).reshape(LANES, LANES).T
    return turned[: LANES // 2]


def pack_kernel(values, out):
    for tile in range(values.shape[1] // LANES):
        part = values[:, tile * LANES : (tile + 1) * LANES].astype(F32)
        out[tile * LANES // 2 : (tile + 1) * LANES // 2] = packed_cells(part).astype(BF16)


def unpack_kernel(values, out):
    for tile in range(out.shape[1] // LANES):
        part = values[tile * LANES // 2 : (tile + 1) * LANES // 2].astype(F32)
        out[:, tile * LANES : (tile + 1) * LANES] = unpacked(part).astype(BF16)


def tap_stack(values, span):
    values = values.astype(F32)
    return jnp.concatenate([shifted(values, -step, span).astype(BF16) for step in STEPS], axis=0)


def store_tiles(ref, base, values):
    rows, cols = values.shape
    for start in range(0, cols, LANES):
        width = min(LANES, cols - start)
        ref[base : base + rows, :width] = values[:, start : start + width].astype(ref.dtype)
        base += rows
    return base


def coarse_grad_kernel(extent, half, *refs):
    pieces, (dpre, grad) = refs[:3], refs[3:]
    own = jnp.where(own_lanes(half[0], extent, dpre.shape), dpre[...].astype(F32), 0.0)
    products = dot_lanes(tap_stack(own, LANES // 2), coarse_stack(pieces))
    rows, cols = products.shape
    base = store_tiles(grad, 0, products[:, : cols - LANES // 2])
    last = products[:, cols - LANES // 2 :]
    grad[base:] = jnp.concatenate([last[: rows // 2], last[rows // 2 :]], axis=1).astype(grad.dtype)


def back_kernel(extent, half, *refs):
    pieces, feature_pieces = refs[:3], refs[3:6]
    weights, up_weights, unsort, sorted_act, slope, coarse_grad, dpre2, grads = refs[6:]
    chans3 = pieces[0].shape[0]
    columns, chans = feature_pieces[0].shape[0] // 2, feature_pieces[0].shape[2]
    ddown = fold_taps(dot(weights[...], coarse_stack(pieces)), chans3, LANES // 2)
    own_ddown = jnp.where(own_lanes(half[0], extent, ddown.shape), ddown, 0.0).astype(BF16)
    ddown = ddown.astype(BF16)
    spread = dot(up_weights[...], ddown).astype(BF16)
    rows = spread.shape[0] // 2
    total = None
    for tile in range(columns // 2):
        lanes = slice(tile * LANES, (tile + 1) * LANES)
        both = dot(jnp.concatenate([spread[:rows, lanes], spread[rows:, lanes]], axis=1), unsort[...])
        for member in range(2):
            column = tile + member * (columns // 2)
            dpre = both[:, member * LANES : (member + 1) * LANES] * slope[column]
            dpre = dpre.astype(BF16)
            parts = [dpre[place * chans : (place + 1) * chans] for place in range(4)]
            for place in range(4):
                dpre2[2 * column + place // 2, place % 2] = parts[place]
            place = column - (columns - extent) * half[0]
            inside = (place >= 0) & (place < extent)
            parts = [jnp.where(inside, part.astype(F32), 0.0) for part in parts]
            moved = jnp.concatenate([tap_stack(part, LANES) for part in parts], axis=1)
            term = dot_lanes(moved, fine_stack(feature_pieces, column))
            total = term if total is None else total + term
    base = coarse_grad.shape[0]
    grads[:base] = coarse_grad[...]
    grads[base:] = jnp.zeros((grads.shape[0] - base, LANES), grads.dtype)
    base = store_tiles(grads, base, total)
    store_tiles(grads, base, dot_lanes(own_ddown, sorted_act[...]))


def input_kernel(half, *refs):
    pieces, (weights, out) = refs[:3], refs[3:]
    cells, chans = pieces[0].shape[0], pieces[0].shape[2]
    count = out.shape[0]
    for column in range(count // 2):
        stack = fine_stack(pieces, column, (half[0], cells - count, count))
        products = dot(weights[...], stack)
        for place in range(4):
            total = fold_taps(products[:, place * LANES : (place + 1) * LANES], chans, LANES)
            out[2 * column + place // 2, place % 2] = total.astype(BF16)


def tap_matrix(weights):
    taps, outs, ins = weights.shape
    return jnp.transpose(weights.reshape(9, 3, outs, ins), (1, 2, 0, 3)).reshape(3 * outs, 9 * ins)


def reversed_taps(weights):
    return jnp.transpose(weights[::-1], (0, 2, 1))


def sort_matrix():
    table = np.zeros((2 * LANES, 2 * LANES), np.float32)
    for sample in range(2):
        for z in range(LANES):
            table[sample * LANES + z, (z % 2) * LANES + sample * (LANES // 2) + z // 2] = 1.0
    return table


def trade(parts, axis, groups=None):
    return lax.all_to_all(
        parts, axis, split_axis=0, concat_axis=0, axis_index_groups=groups, tiled=True
    )


def share(part, axis, groups=None):
    count = lax.axis_size(axis) if groups is None else len(groups[0])
    return trade(jnp.broadcast_to(part[None], (count, *part.shape)), axis, groups)


def turned(block):
    rows, cols = lax.axis_size("grp"), lax.axis_size("sp")
    batch, shift = cols // 2, QUARTERS // 2
    pairs = []
    for row in range(rows):
        major, quarter = divmod((row - shift) % rows, QUARTERS)
        for col in range(cols):
            there = (QUARTERS * (col % batch) + quarter + shift) % rows
            pairs.append((row * cols + col, there * cols + col // batch * batch + major))
    return lax.ppermute(block, ("grp", "sp"), pairs)


def planes():
    rows, cols = lax.axis_size("grp"), lax.axis_size("sp")
    return [
        [row * cols + col for row in range(start, start + 4) for col in range(cols) if col & 2 == far]
        for start in range(0, rows, 4)
        for far in (0, 2)
    ]


def columns():
    rows, cols = lax.axis_size("grp"), lax.axis_size("sp")
    return [
        [row * cols + col + far for row in range(y, rows, 4) for far in (0, 2)]
        for y in range(4)
        for col in range(cols)
        if col & 2 == 0
    ]


def late():
    return (lax.axis_index("grp") % 4 < 2).astype(jnp.int32)


def for_plane(cells):
    lead = cells.shape[0] // 4
    parts = cells.reshape(lead, 2, 2, QUARTERS, 8, LANES)
    parts = jnp.roll(jnp.transpose(parts, (3, 0, 2, 1, 4, 5)), QUARTERS // 2, axis=0)
    blank = jnp.zeros_like(parts)
    low = upper_half() == 0
    both = [jnp.where(low, parts, blank), jnp.where(low, blank, parts)]
    return jnp.concatenate(both, axis=1).reshape(-1, 16, LANES)


def for_column(got):
    lead = lax.axis_size("sp") // 8
    parts = got.reshape(4, 2, lead, 2, 2, 8, LANES)
    parts = jnp.where(upper_half() == 0, parts[:, 0], parts[:, 1])
    parts = jnp.transpose(parts, (1, 2, 3, 0, 4, 5))
    parts = jnp.stack([parts, jnp.zeros_like(parts)], axis=1).reshape(4 * lead, 2, 32, LANES)
    steps = 4 * lead
    shift = 2 * far_side() + late()
    twice = jnp.concatenate([parts, parts], axis=0)
    return lax.dynamic_slice_in_dim(twice, steps - shift, steps, axis=0).reshape(-1, 32, LANES)


def from_column(got):
    parts = got.reshape(-1, 2, 32, LANES)
    steps = parts.shape[0]
    sample = (lax.axis_index("grp") // 4 - late()) % steps
    return jnp.where(sample // 2 % 2 == 0, parts[:, 0], parts[:, 1]).reshape(-1, LANES)


def far_side():
    return lax.axis_index("sp") // 2 % 2


def far_exchange(parts):
    near = far_side() == 0
    kept = jnp.where(near, parts[:, 0], parts[:, 1])
    sent = jnp.where(near, parts[:, 1], parts[:, 0])
    got = lax.ppermute(sent, "sp", [(col, col ^ 2) for col in range(lax.axis_size("sp"))])
    return jnp.stack([jnp.where(near, kept, got), jnp.where(near, got, kept)], axis=2)


def matched(parts, far, core):
    if parts.shape[0] > 1:
        parts = jnp.where(far == 0, parts, parts[::-1])
    return jnp.where(core == 0, parts, parts[:, ::-1])


def near_exchange(parts):
    cols, lead = lax.axis_size("sp"), parts.shape[0]
    place = lax.axis_index("sp")
    far, core = place // 4 % lead, place % 2
    parts = matched(parts, far, core)
    got = [
        [
            parts[x, c]
            if x == c == 0
            else lax.ppermute(parts[x, c], "sp", [(col, col ^ (4 * x + c)) for col in range(cols)])
            for c in (0, 1)
        ]
        for x in range(lead)
    ]
    return matched(jnp.stack([jnp.stack(row) for row in got]), far, core)


def local(features, weight_fine, weight_down, weight_coarse, cotangent):
    batch, chans, x_cells, y_cells, z_cells = features.shape
    chans3 = weight_down.shape[1]
    rows, cols = lax.axis_size("grp"), lax.axis_size("sp")
    width = batch * z_cells // 2
    extent = batch + reach()
    wider = extent * z_cells // 2
    fine_scale = 1.0 / math.sqrt(batch * x_cells * cols * y_cells * rows * z_cells)
    coarse_scale = 1.0 / math.sqrt(batch * x_cells * cols * y_cells * rows * z_cells // 8)
    shape = jax.ShapeDtypeStruct
    near = planes()
    unit = len(near[0]) * 8
    grad_rows = -(-(27 * chans3 // 2 + 9 * chans + 2 * chans3) // unit) * unit
    half = upper_half().astype(jnp.int32).reshape(1)

    sort = jnp.asarray(sort_matrix(), BF16)
    unsort = jnp.asarray(sort_matrix().T, BF16)
    parted = weight_down.reshape(2, 2, 2, chans3, chans)
    down_matrix = jnp.transpose(parted, (3, 2, 0, 1, 4)).reshape(chans3, 8 * chans)

    halves = [list(range(batch)), list(range(batch, cols))]
    own = trade(jnp.transpose(features, (0, 2, 3, 1, 4)), "sp", halves)
    own = own.reshape(batch * x_cells, y_cells, chans, LANES)

    block = (rows, width // 2 // rows, LANES)
    cells = pl.pallas_call(
        pack_kernel, out_shape=shape((width // 2, LANES), BF16), interpret=INTERPRET
    )(turned(cotangent.reshape(chans3, width)))
    cells = cells.reshape(block)
    matrices = [
        tap_matrix(weight_fine),
        tap_matrix(reversed_taps(weight_fine)),
        tap_matrix(weight_coarse),
        tap_matrix(reversed_taps(weight_coarse)),
        down_matrix,
        down_matrix.T,
    ]
    own, cells, *matrices = lax.optimization_barrier((own, cells, *matrices))
    fine_matrix, fine_back, coarse_matrix, coarse_back, down_matrix, up_matrix = matrices
    own = joined(own, arrival(nearest(own, reach() * x_cells), 0, True))
    cells = jnp.roll(trade(cells, "grp"), -(QUARTERS // 2), axis=0).reshape(width // 2, LANES)
    upstream = joined(cells, arrival(nearest(cells, reach() * QUARTERS * block[1]), 0, True))

    feature_pieces = fine_pieces(own)
    down, sorted_act, slope = call(
        down_kernel,
        (
            shape((chans3, wider), BF16),
            shape((8 * chans, wider), BF16),
            shape((extent, 4 * chans, LANES), F32),
        ),
        half,
        *feature_pieces,
        fine_matrix,
        down_matrix,
        sort,
    )
    down_pieces = coarse_pieces(down)
    coarse, dpre3 = call(
        coarse_kernel,
        (shape(upstream.shape, BF16), shape((chans3, wider), BF16)),
        half,
        *down_pieces,
        coarse_matrix,
        upstream,
    )
    coarse_grad = call(
        partial(coarse_grad_kernel, batch),
        shape((27 * chans3 // 2, LANES), BF16),
        half,
        *down_pieces,
        dpre3,
    )
    dpre_pieces = coarse_pieces(dpre3)
    coarse_grad, *dpre_pieces = lax.optimization_barrier((coarse_grad, *dpre_pieces))

    dpre2, grads = call(
        partial(back_kernel, batch),
        (shape(own.shape, BF16), shape((grad_rows, LANES), BF16)),
        half,
        *dpre_pieces,
        *feature_pieces,
        coarse_back,
        up_matrix,
        unsort,
        sorted_act,
        slope,
        coarse_grad,
    )
    coarse = jnp.where(upper_half() == 0, coarse[: width // 2], coarse[-(width // 2) :])
    grads = grads.reshape(len(near[0]), -1, LANES)
    kept = grads.shape[1]
    coarse = for_plane(coarse.reshape(batch, QUARTERS, 8, LANES))
    mixed = trade(jnp.concatenate([grads, coarse], axis=1), ("grp", "sp"), near)
    part = jnp.sum(mixed[:, :kept].astype(F32), axis=0).astype(BF16)
    coarse = for_column(mixed[:, kept:])
    gradient = call(
        input_kernel,
        shape((batch * x_cells, *own.shape[1:]), BF16),
        half,
        *fine_pieces(dpre2),
        fine_back,
    )
    part, gradient, coarse = lax.optimization_barrier((part, gradient, coarse))
    gradient = far_exchange(gradient.reshape(batch // 4, 2, 2, x_cells, y_cells, chans, LANES))
    part = jnp.broadcast_to(part[None], (coarse.shape[0], *part.shape))
    mixed = trade(jnp.concatenate([part, coarse], axis=1), ("grp", "sp"), columns())
    part = jnp.sum(mixed[:, :kept].astype(F32), axis=0).astype(BF16)
    coarse = from_column(mixed[:, kept:])
    grads = share(part, ("grp", "sp"), near).reshape(grad_rows, LANES).astype(F32)
    gradient = near_exchange(gradient)
    grads, gradient = lax.optimization_barrier((grads, gradient))
    grad_input = jnp.transpose(gradient, (0, 2, 1, 5, 3, 4, 6)).reshape(features.shape)

    result = pl.pallas_call(
        unpack_kernel, out_shape=shape((chans3, width), BF16), interpret=INTERPRET
    )(coarse)
    result = result.reshape(cotangent.shape)

    grad_coarse = grads[: 12 * chans3].reshape(4, 3, chans3, 2, chans3)
    grad_coarse = jnp.transpose(grad_coarse, (0, 3, 1, 2, 4)).reshape(24, chans3, chans3)
    last = grads[12 * chans3 : 27 * chans3 // 2].reshape(-1, 2, chans3)
    last = jnp.swapaxes(last, 0, 1).reshape(3, chans3, chans3)
    grad_coarse = jnp.concatenate([grad_coarse, last], axis=0)
    grads = grads[27 * chans3 // 2 :]
    grad_fine = grads[: 9 * chans].reshape(3, 3, chans, 4, chans)
    grad_fine = jnp.transpose(grad_fine, (0, 3, 1, 2, 4)).reshape(36, chans, chans)[:27]
    grad_down = grads[9 * chans : 9 * chans + 2 * chans3].reshape(2, chans3, 4, chans)
    grad_down = jnp.transpose(grad_down, (2, 0, 1, 3)).reshape(8, chans3, chans)
    return (
        result,
        grad_input,
        grad_fine * fine_scale,
        grad_down * coarse_scale,
        grad_coarse * coarse_scale,
    )


def solution(mesh):
    placed = (P(None, None, "sp", "grp", None), P(), P(), P(), P("grp", None, "sp", None))
    return jax.shard_map(
        local,
        mesh=mesh,
        in_specs=placed,
        out_specs=(P("grp", None, "sp", None), P(None, None, "sp", "grp", None), P(), P(), P()),
        check_vma=False,
    )
```

```python
import math
from functools import partial

import jax
import jax.numpy as jnp
import numpy as np
from jax import lax
from jax.experimental import pallas as pl
from jax.experimental.pallas import tpu as pltpu
from jax.sharding import PartitionSpec as P

QUARTERS = 4
LANES = 128
STEPS = (-1, 0, 1)
F32 = jnp.float32
BF16 = jnp.bfloat16
INTERPRET = False


def call(kernel, outs, half, *operands):
    spaces = [pltpu.SMEM] + [pltpu.VMEM] * len(operands)
    return pl.pallas_call(
        kernel,
        out_shape=outs,
        in_specs=[pl.BlockSpec(memory_space=space) for space in spaces],
        compiler_params=pltpu.CompilerParams(vmem_limit_bytes=28 * 1024 * 1024),
        interpret=INTERPRET,
    )(half, *operands)


def arrival(block, step_y, across):
    rows, cols = lax.axis_size("grp"), lax.axis_size("sp")
    pairs = []
    for row in range(rows):
        for col in range(cols):
            if 0 <= row + step_y < rows:
                source = (col + cols // 2) % cols if across else col
                pairs.append(((row + step_y) * cols + source, row * cols + col))
    return lax.ppermute(block, ("grp", "sp"), pairs)


def upper_half():
    return lax.axis_index("sp") // (lax.axis_size("sp") // 2)


def reach():
    return min(4, lax.axis_size("sp") // 2)


def joined(own, other):
    low = jnp.concatenate([own, other], axis=0)
    return jnp.where(upper_half() == 0, low, jnp.concatenate([other, own], axis=0))


def nearest(block, count):
    return jnp.where(upper_half() == 0, block[-count:], block[:count])


def fine_pieces(block):
    return [block, arrival(block[:, 1:], -1, False), arrival(block[:, :1], 1, False)]


def coarse_pieces(block):
    return [block, arrival(block, -1, False), arrival(block, 1, False)]


def silu_slope(values, sigma):
    return sigma * (1.0 + values * (1.0 - sigma))


def dot(left, right):
    return lax.dot_general(left, right, (((1,), (0,)), ((), ())), preferred_element_type=F32)


def dot_lanes(left, right):
    return lax.dot_general(left, right, (((1,), (1,)), ((), ())), preferred_element_type=F32)


def shifted(values, step, span):
    if step == 0:
        return values
    place = lax.broadcasted_iota(jnp.int32, values.shape, 1) % span
    width = values.shape[1]
    moved = pltpu.roll(values, (-step) % width, 1)
    return jnp.where(place == (span - 1 if step > 0 else 0), 0.0, moved)


def fold_taps(products, chans, span):
    total = products[chans : 2 * chans]
    total = total + shifted(products[:chans], -1, span)
    return total + shifted(products[2 * chans :], 1, span)


def fine_stack(refs, column, shift=None):
    center, before, after = refs
    cells = center.shape[0]

    def cell(x, y):
        inside = None
        if shift is not None:
            half, skip, count = shift
            inside = half == 1 if x < 0 else half == 0 if x >= count else None
            x = jnp.clip(x + skip * half, 0, cells - 1)
        elif not 0 <= x < cells:
            return jnp.zeros(center.shape[2:], center.dtype)
        value = before[x, 0] if y < 0 else after[x, 0] if y > 1 else center[x, y]
        return value if inside is None else jnp.where(inside, value, jnp.zeros_like(value))

    return jnp.concatenate(
        [
            jnp.concatenate(
                [cell(2 * column + x + a, y + b) for x in (0, 1) for y in (0, 1)], axis=1
            )
            for a in STEPS
            for b in STEPS
        ],
        axis=0,
    )


def coarse_stack(refs):
    tiles = refs[0].shape[1] // LANES
    low = lax.broadcasted_iota(jnp.int32, (refs[0].shape[0], LANES), 1) < LANES // 2
    lined = []
    for ref in (refs[1], refs[0], refs[2]):
        own = [ref[:, tile * LANES : (tile + 1) * LANES] for tile in range(tiles)]
        first = jnp.where(low, own[-1].astype(F32), 0.0)
        last = jnp.where(low, 0.0, own[0].astype(F32))
        first, last = [pltpu.roll(tile, LANES // 2, 1).astype(BF16) for tile in (first, last)]
        lined.append([first, *own, last])
    return jnp.concatenate(
        [jnp.concatenate(lined[b][a : a + tiles], axis=1) for a in range(3) for b in range(3)],
        axis=0,
    )


def own_lanes(half, extent, shape):
    lane = lax.broadcasted_iota(jnp.int32, shape, 1)
    tiles = shape[1] // LANES
    x = lane // LANES + tiles * (lane % LANES // (LANES // 2)) - (2 * tiles - extent) * half
    return (x >= 0) & (x < extent)


def down_kernel(half, *refs):
    pieces, (weights, down_weights, sort, down, sorted_act, slope) = refs[:3], refs[3:]
    columns, chans = pieces[0].shape[0] // 2, pieces[0].shape[2]
    for tile in range(columns // 2):
        acts = []
        for column in (tile, tile + columns // 2):
            products = dot(weights[...], fine_stack(pieces, column))
            parts = []
            for place in range(4):
                pre = fold_taps(products[:, place * LANES : (place + 1) * LANES], chans, LANES)
                sigma = jax.nn.sigmoid(pre)
                slope[column, place * chans : (place + 1) * chans] = silu_slope(pre, sigma)
                parts.append((pre * sigma).astype(BF16))
            acts.append(jnp.concatenate(parts, axis=0))
        parted = dot(jnp.concatenate(acts, axis=1), sort[...]).astype(BF16)
        stacked = jnp.concatenate([parted[:, :LANES], parted[:, LANES:]], axis=0)
        lanes = slice(tile * LANES, (tile + 1) * LANES)
        sorted_act[:, lanes] = stacked
        down[:, lanes] = dot(down_weights[...], stacked).astype(BF16)


def coarse_kernel(half, *refs):
    pieces, (weights, upstream, out, dpre) = refs[:3], refs[3:]
    chans, width = pieces[0].shape
    pre = fold_taps(dot(weights[...], coarse_stack(pieces)), chans, LANES // 2)
    sigma = jax.nn.sigmoid(pre)
    act = pre * sigma
    slope = silu_slope(pre, sigma)
    tiles = width // LANES
    rows = LANES // 4
    for tile in range(tiles):
        lanes = slice(tile * LANES, (tile + 1) * LANES)
        ends = [tile * rows, (tile + tiles) * rows]
        packed = jnp.concatenate([upstream[end : end + rows] for end in ends], axis=0)
        dpre[:, lanes] = (unpacked(packed.astype(F32)) * slope[:, lanes]).astype(BF16)
        both = packed_cells(act[:, lanes]).astype(BF16)
        for member, end in enumerate(ends):
            out[end : end + rows] = both[member * rows : (member + 1) * rows]


def packed_cells(values):
    turned = jnp.concatenate([values, values], axis=0).T.reshape(LANES // 16, 2, 8, LANES)
    low = lax.broadcasted_iota(jnp.int32, (LANES // 16, 8, LANES), 2) < LANES // 2
    return jnp.where(low, turned[:, 0], turned[:, 1]).reshape(LANES // 2, LANES)


def unpacked(values):
    first = values.reshape(LANES // 16, 1, 8, LANES)
    second = pltpu.roll(values, LANES // 2, 1).reshape(LANES // 16, 1, 8, LANES)
    turned = jnp.concatenate([first, second], axis=1).reshape(LANES, LANES).T
    return turned[: LANES // 2]


def pack_kernel(values, out):
    for tile in range(values.shape[1] // LANES):
        part = values[:, tile * LANES : (tile + 1) * LANES].astype(F32)
        out[tile * LANES // 2 : (tile + 1) * LANES // 2] = packed_cells(part).astype(BF16)


def unpack_kernel(values, out):
    for tile in range(out.shape[1] // LANES):
        part = values[tile * LANES // 2 : (tile + 1) * LANES // 2].astype(F32)
        out[:, tile * LANES : (tile + 1) * LANES] = unpacked(part).astype(BF16)


def tap_stack(values, span):
    values = values.astype(F32)
    return jnp.concatenate([shifted(values, -step, span).astype(BF16) for step in STEPS], axis=0)


def store_tiles(ref, base, values):
    rows, cols = values.shape
    for start in range(0, cols, LANES):
        width = min(LANES, cols - start)
        ref[base : base + rows, :width] = values[:, start : start + width].astype(ref.dtype)
        base += rows
    return base


def coarse_grad_kernel(extent, half, *refs):
    pieces, (dpre, grad) = refs[:3], refs[3:]
    own = jnp.where(own_lanes(half[0], extent, dpre.shape), dpre[...].astype(F32), 0.0)
    products = dot_lanes(tap_stack(own, LANES // 2), coarse_stack(pieces))
    rows, cols = products.shape
    base = store_tiles(grad, 0, products[:, : cols - LANES // 2])
    last = products[:, cols - LANES // 2 :]
    grad[base:] = jnp.concatenate([last[: rows // 2], last[rows // 2 :]], axis=1).astype(grad.dtype)


def back_kernel(extent, half, *refs):
    pieces, feature_pieces = refs[:3], refs[3:6]
    weights, up_weights, unsort, sorted_act, slope, coarse_grad, dpre2, grads = refs[6:]
    chans3 = pieces[0].shape[0]
    columns, chans = feature_pieces[0].shape[0] // 2, feature_pieces[0].shape[2]
    ddown = fold_taps(dot(weights[...], coarse_stack(pieces)), chans3, LANES // 2)
    own_ddown = jnp.where(own_lanes(half[0], extent, ddown.shape), ddown, 0.0).astype(BF16)
    ddown = ddown.astype(BF16)
    spread = dot(up_weights[...], ddown).astype(BF16)
    rows = spread.shape[0] // 2
    total = None
    for tile in range(columns // 2):
        lanes = slice(tile * LANES, (tile + 1) * LANES)
        both = dot(jnp.concatenate([spread[:rows, lanes], spread[rows:, lanes]], axis=1), unsort[...])
        for member in range(2):
            column = tile + member * (columns // 2)
            dpre = both[:, member * LANES : (member + 1) * LANES] * slope[column]
            dpre = dpre.astype(BF16)
            parts = [dpre[place * chans : (place + 1) * chans] for place in range(4)]
            for place in range(4):
                dpre2[2 * column + place // 2, place % 2] = parts[place]
            place = column - (columns - extent) * half[0]
            inside = (place >= 0) & (place < extent)
            parts = [jnp.where(inside, part.astype(F32), 0.0) for part in parts]
            moved = jnp.concatenate([tap_stack(part, LANES) for part in parts], axis=1)
            term = dot_lanes(moved, fine_stack(feature_pieces, column))
            total = term if total is None else total + term
    base = coarse_grad.shape[0]
    grads[:base] = coarse_grad[...]
    grads[base:] = jnp.zeros((grads.shape[0] - base, LANES), grads.dtype)
    base = store_tiles(grads, base, total)
    grad_down = dot_lanes(sorted_act[...], own_ddown)
    rows = grad_down.shape[0] // 2
    grads[base : base + rows] = jnp.concatenate(
        [grad_down[:rows], grad_down[rows:]], axis=1
    ).astype(grads.dtype)


def input_kernel(half, *refs):
    pieces, (weights, out) = refs[:3], refs[3:]
    cells, chans = pieces[0].shape[0], pieces[0].shape[2]
    count = out.shape[0]
    for column in range(count // 2):
        stack = fine_stack(pieces, column, (half[0], cells - count, count))
        products = dot(weights[...], stack)
        for place in range(4):
            total = fold_taps(products[:, place * LANES : (place + 1) * LANES], chans, LANES)
            out[2 * column + place // 2, place % 2] = total.astype(BF16)


def assemble_kernel(fine_scale, coarse_scale, rows, fine, down, coarse):
    def pieces(start, count, width, scale):
        tile = rows[start : start + count].astype(F32) * scale
        return [
            (tile if lane == 0 else pltpu.roll(tile, LANES - lane, 1))[:, :width]
            for lane in range(0, LANES, width)
        ]

    chans, chans3 = fine.shape[1], coarse.shape[1]
    for tile in range(4):
        for h, part in enumerate(pieces(3 * tile * chans3, 3 * chans3, chans3, coarse_scale)):
            for c in range(3):
                coarse[6 * tile + 3 * h + c] = part[c * chans3 : (c + 1) * chans3]
    base = 12 * chans3
    low, high = pieces(base, 3 * chans3 // 2, chans3, coarse_scale)
    coarse[24] = low[:chans3]
    coarse[25] = jnp.concatenate([low[chans3:], high[: chans3 // 2]], axis=0)
    coarse[26] = high[chans3 // 2 :]
    base += 3 * chans3 // 2
    for tile in range(3):
        for h, part in enumerate(pieces(base, 3 * chans, chans, fine_scale)):
            for c in range(3):
                if 4 * tile + h < 9:
                    fine[3 * (4 * tile + h) + c] = part[c * chans : (c + 1) * chans]
        base += 3 * chans
    for last, part in enumerate(pieces(base, 4 * chans, chans3, coarse_scale)):
        for first in range(4):
            down[2 * first + last] = part[first * chans : (first + 1) * chans]


def tap_matrix(weights):
    taps, outs, ins = weights.shape
    return jnp.transpose(weights.reshape(9, 3, outs, ins), (1, 2, 0, 3)).reshape(3 * outs, 9 * ins)


def reversed_taps(weights):
    return jnp.transpose(weights[::-1], (0, 2, 1))


def sort_matrix():
    table = np.zeros((2 * LANES, 2 * LANES), np.float32)
    for sample in range(2):
        for z in range(LANES):
            table[sample * LANES + z, (z % 2) * LANES + sample * (LANES // 2) + z // 2] = 1.0
    return table


def trade(parts, axis, groups=None):
    return lax.all_to_all(
        parts, axis, split_axis=0, concat_axis=0, axis_index_groups=groups, tiled=True
    )


def share(part, axis, groups=None):
    count = lax.axis_size(axis) if groups is None else len(groups[0])
    return trade(jnp.broadcast_to(part[None], (count, *part.shape)), axis, groups)


def turned(block):
    rows, cols = lax.axis_size("grp"), lax.axis_size("sp")
    batch, shift = cols // 2, QUARTERS // 2
    pairs = []
    for row in range(rows):
        major, quarter = divmod((row - shift) % rows, QUARTERS)
        for col in range(cols):
            there = (QUARTERS * (col % batch) + quarter + shift) % rows
            pairs.append((row * cols + col, there * cols + col // batch * batch + major))
    return lax.ppermute(block, ("grp", "sp"), pairs)


def planes():
    rows, cols = lax.axis_size("grp"), lax.axis_size("sp")
    return [
        [row * cols + col for row in range(start, start + 4) for col in range(cols) if col & 2 == far]
        for start in range(0, rows, 4)
        for far in (0, 2)
    ]


def columns():
    rows, cols = lax.axis_size("grp"), lax.axis_size("sp")
    return [
        [row * cols + col + far for row in range(y, rows, 4) for far in (0, 2)]
        for y in range(4)
        for col in range(cols)
        if col & 2 == 0
    ]


def late():
    return (lax.axis_index("grp") % 4 < 2).astype(jnp.int32)


def for_plane(cells):
    lead = cells.shape[0] // 4
    parts = cells.reshape(lead, 2, 2, QUARTERS, 8, LANES)
    parts = jnp.roll(jnp.transpose(parts, (3, 0, 2, 1, 4, 5)), QUARTERS // 2, axis=0)
    blank = jnp.zeros_like(parts)
    low = upper_half() == 0
    both = [jnp.where(low, parts, blank), jnp.where(low, blank, parts)]
    return jnp.concatenate(both, axis=1).reshape(-1, 16, LANES)


def for_column(got):
    lead = lax.axis_size("sp") // 8
    parts = got.reshape(4, 2, lead, 2, 2, 8, LANES)
    parts = jnp.where(upper_half() == 0, parts[:, 0], parts[:, 1])
    parts = jnp.transpose(parts, (1, 2, 3, 0, 4, 5))
    parts = jnp.stack([parts, jnp.zeros_like(parts)], axis=1).reshape(4 * lead, 2, 32, LANES)
    steps = 4 * lead
    shift = 2 * far_side() + late()
    twice = jnp.concatenate([parts, parts], axis=0)
    return lax.dynamic_slice_in_dim(twice, steps - shift, steps, axis=0).reshape(-1, 32, LANES)


def from_column(got):
    parts = got.reshape(-1, 2, 32, LANES)
    steps = parts.shape[0]
    sample = (lax.axis_index("grp") // 4 - late()) % steps
    return jnp.where(sample // 2 % 2 == 0, parts[:, 0], parts[:, 1]).reshape(-1, LANES)


def after(value, *others):
    return lax.optimization_barrier((value, *others))[0]


def far_side():
    return lax.axis_index("sp") // 2 % 2


def far_exchange(parts):
    near = far_side() == 0
    kept = jnp.where(near, parts[:, 0], parts[:, 1])
    sent = jnp.where(near, parts[:, 1], parts[:, 0])
    got = lax.ppermute(sent, "sp", [(col, col ^ 2) for col in range(lax.axis_size("sp"))])
    return jnp.stack([jnp.where(near, kept, got), jnp.where(near, got, kept)], axis=2)


def matched(parts, far, core):
    if parts.shape[0] > 1:
        parts = jnp.where(far == 0, parts, parts[::-1])
    return jnp.where(core == 0, parts, parts[:, ::-1])


def near_exchange(parts):
    cols, lead = lax.axis_size("sp"), parts.shape[0]
    place = lax.axis_index("sp")
    far, core = place // 4 % lead, place % 2
    parts = matched(parts, far, core)
    got = [
        [
            parts[x, c]
            if x == c == 0
            else lax.ppermute(parts[x, c], "sp", [(col, col ^ (4 * x + c)) for col in range(cols)])
            for c in (0, 1)
        ]
        for x in range(lead)
    ]
    return matched(jnp.stack([jnp.stack(row) for row in got]), far, core)


def local(features, weight_fine, weight_down, weight_coarse, cotangent):
    batch, chans, x_cells, y_cells, z_cells = features.shape
    chans3 = weight_down.shape[1]
    rows, cols = lax.axis_size("grp"), lax.axis_size("sp")
    width = batch * z_cells // 2
    extent = batch + reach()
    wider = extent * z_cells // 2
    fine_scale = 1.0 / math.sqrt(batch * x_cells * cols * y_cells * rows * z_cells)
    coarse_scale = 1.0 / math.sqrt(batch * x_cells * cols * y_cells * rows * z_cells // 8)
    shape = jax.ShapeDtypeStruct
    near = planes()
    unit = len(near[0]) * 8
    grad_rows = -(-(27 * chans3 // 2 + 9 * chans + 2 * chans3) // unit) * unit
    half = upper_half().astype(jnp.int32).reshape(1)

    sort = jnp.asarray(sort_matrix(), BF16)
    unsort = jnp.asarray(sort_matrix().T, BF16)
    parted = weight_down.reshape(2, 2, 2, chans3, chans)
    down_matrix = jnp.transpose(parted, (3, 2, 0, 1, 4)).reshape(chans3, 8 * chans)

    halves = [list(range(batch)), list(range(batch, cols))]
    own = trade(jnp.transpose(features, (0, 2, 3, 1, 4)), "sp", halves)
    own = own.reshape(batch * x_cells, y_cells, chans, LANES)

    block = (rows, width // 2 // rows, LANES)
    cells = pl.pallas_call(
        pack_kernel, out_shape=shape((width // 2, LANES), BF16), interpret=INTERPRET
    )(turned(cotangent.reshape(chans3, width)))
    cells = cells.reshape(block)
    matrices = [
        tap_matrix(weight_fine),
        tap_matrix(reversed_taps(weight_fine)),
        tap_matrix(weight_coarse),
        tap_matrix(reversed_taps(weight_coarse)),
        down_matrix,
        down_matrix.T,
    ]
    own, *matrices = lax.optimization_barrier((own, *matrices))
    cells = after(cells, own)
    fine_matrix, fine_back, coarse_matrix, coarse_back, down_matrix, up_matrix = matrices
    own = joined(own, arrival(nearest(own, reach() * x_cells), 0, True))
    cells = jnp.roll(trade(cells, "grp"), -(QUARTERS // 2), axis=0).reshape(width // 2, LANES)
    upstream = joined(cells, arrival(nearest(cells, reach() * QUARTERS * block[1]), 0, True))

    feature_pieces = fine_pieces(own)
    down, sorted_act, slope = call(
        down_kernel,
        (
            shape((chans3, wider), BF16),
            shape((8 * chans, wider), BF16),
            shape((extent, 4 * chans, LANES), F32),
        ),
        half,
        *feature_pieces,
        fine_matrix,
        down_matrix,
        sort,
    )
    down_pieces = coarse_pieces(down)
    coarse, dpre3 = call(
        coarse_kernel,
        (shape(upstream.shape, BF16), shape((chans3, wider), BF16)),
        half,
        *down_pieces,
        coarse_matrix,
        upstream,
    )
    coarse_grad = call(
        partial(coarse_grad_kernel, batch),
        shape((27 * chans3 // 2, LANES), BF16),
        half,
        *down_pieces,
        dpre3,
    )
    dpre_pieces = coarse_pieces(dpre3)
    coarse_grad, *dpre_pieces = lax.optimization_barrier((coarse_grad, *dpre_pieces))

    dpre2, grads = call(
        partial(back_kernel, batch),
        (shape(own.shape, BF16), shape((grad_rows, LANES), BF16)),
        half,
        *dpre_pieces,
        *feature_pieces,
        coarse_back,
        up_matrix,
        unsort,
        sorted_act,
        slope,
        coarse_grad,
    )
    coarse = jnp.where(upper_half() == 0, coarse[: width // 2], coarse[-(width // 2) :])
    grads = grads.reshape(len(near[0]), -1, LANES)
    kept = grads.shape[1]
    coarse = for_plane(coarse.reshape(batch, QUARTERS, 8, LANES))
    mixed = trade(jnp.concatenate([grads, coarse], axis=1), ("grp", "sp"), near)
    part = jnp.sum(mixed[:, :kept].astype(F32), axis=0).astype(BF16)
    coarse = for_column(mixed[:, kept:])
    gradient = call(
        input_kernel,
        shape((batch * x_cells, *own.shape[1:]), BF16),
        half,
        *fine_pieces(dpre2),
        fine_back,
    )
    part, coarse = after(part, gradient), after(coarse, gradient)
    gradient = far_exchange(gradient.reshape(batch // 4, 2, 2, x_cells, y_cells, chans, LANES))
    part = jnp.broadcast_to(part[None], (coarse.shape[0], *part.shape))
    mixed = trade(jnp.concatenate([part, coarse], axis=1), ("grp", "sp"), columns())
    part = jnp.sum(mixed[:, :kept].astype(F32), axis=0).astype(BF16)
    coarse = from_column(mixed[:, kept:])
    gradient = after(gradient, part)
    grads = share(part, ("grp", "sp"), near).reshape(grad_rows, LANES)
    gradient = near_exchange(gradient)
    grads, gradient = lax.optimization_barrier((grads, gradient))
    grad_input = jnp.transpose(gradient, (0, 2, 1, 5, 3, 4, 6)).reshape(features.shape)

    result = pl.pallas_call(
        unpack_kernel, out_shape=shape((chans3, width), BF16), interpret=INTERPRET
    )(coarse)
    result = result.reshape(cotangent.shape)

    grad_fine, grad_down, grad_coarse = pl.pallas_call(
        partial(assemble_kernel, fine_scale, coarse_scale),
        out_shape=(
            shape(weight_fine.shape, F32),
            shape((8, chans, chans3), F32),
            shape(weight_coarse.shape, F32),
        ),
        interpret=INTERPRET,
    )(grads)
    return result, grad_input, grad_fine, jnp.swapaxes(grad_down, 1, 2), grad_coarse


def solution(mesh):
    placed = (P(None, None, "sp", "grp", None), P(), P(), P(), P("grp", None, "sp", None))
    return jax.shard_map(
        local,
        mesh=mesh,
        in_specs=placed,
        out_specs=(P("grp", None, "sp", None), P(None, None, "sp", "grp", None), P(), P(), P()),
        check_vma=False,
    )
```

```python
import math
from functools import partial

import jax
import jax.numpy as jnp
import numpy as np
from jax import lax
from jax.experimental import pallas as pl
from jax.experimental.pallas import tpu as pltpu
from jax.sharding import PartitionSpec as P

QUARTERS = 4
LANES = 128
STEPS = (-1, 0, 1)
F32 = jnp.float32
BF16 = jnp.bfloat16
INTERPRET = False


def call(kernel, outs, half, *operands):
    spaces = [pltpu.SMEM] + [pltpu.VMEM] * len(operands)
    return pl.pallas_call(
        kernel,
        out_shape=outs,
        in_specs=[pl.BlockSpec(memory_space=space) for space in spaces],
        compiler_params=pltpu.CompilerParams(vmem_limit_bytes=28 * 1024 * 1024),
        interpret=INTERPRET,
    )(half, *operands)


def arrival(block, step_y, across):
    rows, cols = lax.axis_size("grp"), lax.axis_size("sp")
    pairs = []
    for row in range(rows):
        for col in range(cols):
            if 0 <= row + step_y < rows:
                source = (col + cols // 2) % cols if across else col
                pairs.append(((row + step_y) * cols + source, row * cols + col))
    return lax.ppermute(block, ("grp", "sp"), pairs)


def upper_half():
    return lax.axis_index("sp") // (lax.axis_size("sp") // 2)


def reach():
    return min(4, lax.axis_size("sp") // 2)


def joined(own, other):
    low = jnp.concatenate([own, other], axis=0)
    return jnp.where(upper_half() == 0, low, jnp.concatenate([other, own], axis=0))


def nearest(block, count):
    return jnp.where(upper_half() == 0, block[-count:], block[:count])


def fine_pieces(block):
    return [block, arrival(block[:, 1:], -1, False), arrival(block[:, :1], 1, False)]


def coarse_pieces(block):
    return [block, arrival(block, -1, False), arrival(block, 1, False)]


def silu_slope(values, sigma):
    return sigma * (1.0 + values * (1.0 - sigma))


def dot(left, right):
    return lax.dot_general(left, right, (((1,), (0,)), ((), ())), preferred_element_type=F32)


def dot_lanes(left, right):
    return lax.dot_general(left, right, (((1,), (1,)), ((), ())), preferred_element_type=F32)


def shifted(values, step, span):
    if step == 0:
        return values
    place = lax.broadcasted_iota(jnp.int32, values.shape, 1) % span
    width = values.shape[1]
    moved = pltpu.roll(values, (-step) % width, 1)
    return jnp.where(place == (span - 1 if step > 0 else 0), 0.0, moved)


def fold_taps(products, chans, span):
    total = products[chans : 2 * chans]
    total = total + shifted(products[:chans], -1, span)
    return total + shifted(products[2 * chans :], 1, span)


def fine_stack(refs, column, shift=None):
    center, before, after = refs
    cells = center.shape[0]

    def cell(x, y):
        inside = None
        if shift is not None:
            half, skip, count = shift
            inside = half == 1 if x < 0 else half == 0 if x >= count else None
            x = jnp.clip(x + skip * half, 0, cells - 1)
        elif not 0 <= x < cells:
            return jnp.zeros(center.shape[2:], center.dtype)
        value = before[x, 0] if y < 0 else after[x, 0] if y > 1 else center[x, y]
        return value if inside is None else jnp.where(inside, value, jnp.zeros_like(value))

    return jnp.concatenate(
        [
            jnp.concatenate(
                [cell(2 * column + x + a, y + b) for x in (0, 1) for y in (0, 1)], axis=1
            )
            for a in STEPS
            for b in STEPS
        ],
        axis=0,
    )


def coarse_stack(refs):
    tiles = refs[0].shape[1] // LANES
    low = lax.broadcasted_iota(jnp.int32, (refs[0].shape[0], LANES), 1) < LANES // 2
    lined = []
    for ref in (refs[1], refs[0], refs[2]):
        own = [ref[:, tile * LANES : (tile + 1) * LANES] for tile in range(tiles)]
        first = jnp.where(low, own[-1].astype(F32), 0.0)
        last = jnp.where(low, 0.0, own[0].astype(F32))
        first, last = [pltpu.roll(tile, LANES // 2, 1).astype(BF16) for tile in (first, last)]
        lined.append([first, *own, last])
    return jnp.concatenate(
        [jnp.concatenate(lined[b][a : a + tiles], axis=1) for a in range(3) for b in range(3)],
        axis=0,
    )


def own_lanes(half, extent, shape):
    lane = lax.broadcasted_iota(jnp.int32, shape, 1)
    tiles = shape[1] // LANES
    x = lane // LANES + tiles * (lane % LANES // (LANES // 2)) - (2 * tiles - extent) * half
    return (x >= 0) & (x < extent)


def down_kernel(half, *refs):
    pieces, (weights, down_weights, sort, down, sorted_act, slope) = refs[:3], refs[3:]
    columns, chans = pieces[0].shape[0] // 2, pieces[0].shape[2]
    for tile in range(columns // 2):
        acts = []
        for column in (tile, tile + columns // 2):
            products = dot(weights[...], fine_stack(pieces, column))
            parts = []
            for place in range(4):
                pre = fold_taps(products[:, place * LANES : (place + 1) * LANES], chans, LANES)
                sigma = jax.nn.sigmoid(pre)
                slope[column, place * chans : (place + 1) * chans] = silu_slope(pre, sigma)
                parts.append((pre * sigma).astype(BF16))
            acts.append(jnp.concatenate(parts, axis=0))
        parted = dot(jnp.concatenate(acts, axis=1), sort[...]).astype(BF16)
        stacked = jnp.concatenate([parted[:, :LANES], parted[:, LANES:]], axis=0)
        lanes = slice(tile * LANES, (tile + 1) * LANES)
        sorted_act[:, lanes] = stacked
        down[:, lanes] = dot(down_weights[...], stacked).astype(BF16)


def coarse_kernel(half, *refs):
    pieces, (weights, upstream, out, dpre) = refs[:3], refs[3:]
    chans, width = pieces[0].shape
    pre = fold_taps(dot(weights[...], coarse_stack(pieces)), chans, LANES // 2)
    sigma = jax.nn.sigmoid(pre)
    act = pre * sigma
    slope = silu_slope(pre, sigma)
    tiles = width // LANES
    rows = LANES // 4
    for tile in range(tiles):
        lanes = slice(tile * LANES, (tile + 1) * LANES)
        ends = [tile * rows, (tile + tiles) * rows]
        packed = jnp.concatenate([upstream[end : end + rows] for end in ends], axis=0)
        dpre[:, lanes] = (unpacked(packed.astype(F32)) * slope[:, lanes]).astype(BF16)
        both = packed_cells(act[:, lanes]).astype(BF16)
        for member, end in enumerate(ends):
            out[end : end + rows] = both[member * rows : (member + 1) * rows]


def packed_cells(values):
    turned = jnp.concatenate([values, values], axis=0).T.reshape(LANES // 16, 2, 8, LANES)
    low = lax.broadcasted_iota(jnp.int32, (LANES // 16, 8, LANES), 2) < LANES // 2
    return jnp.where(low, turned[:, 0], turned[:, 1]).reshape(LANES // 2, LANES)


def unpacked(values):
    first = values.reshape(LANES // 16, 1, 8, LANES)
    second = pltpu.roll(values, LANES // 2, 1).reshape(LANES // 16, 1, 8, LANES)
    turned = jnp.concatenate([first, second], axis=1).reshape(LANES, LANES).T
    return turned[: LANES // 2]


def pack_kernel(values, out):
    for tile in range(values.shape[1] // LANES):
        part = values[:, tile * LANES : (tile + 1) * LANES].astype(F32)
        out[tile * LANES // 2 : (tile + 1) * LANES // 2] = packed_cells(part).astype(BF16)


def unpack_kernel(values, out):
    for tile in range(out.shape[1] // LANES):
        part = values[tile * LANES // 2 : (tile + 1) * LANES // 2].astype(F32)
        out[:, tile * LANES : (tile + 1) * LANES] = unpacked(part).astype(BF16)


def tap_stack(values, span):
    values = values.astype(F32)
    return jnp.concatenate([shifted(values, -step, span).astype(BF16) for step in STEPS], axis=0)


def store_tiles(ref, base, values):
    rows, cols = values.shape
    for start in range(0, cols, LANES):
        width = min(LANES, cols - start)
        ref[base : base + rows, :width] = values[:, start : start + width].astype(ref.dtype)
        base += rows
    return base


def coarse_grad_kernel(extent, half, *refs):
    pieces, (dpre, grad) = refs[:3], refs[3:]
    own = jnp.where(own_lanes(half[0], extent, dpre.shape), dpre[...].astype(F32), 0.0)
    products = dot_lanes(tap_stack(own, LANES // 2), coarse_stack(pieces))
    rows, cols = products.shape
    base = store_tiles(grad, 0, products[:, : cols - LANES // 2])
    last = products[:, cols - LANES // 2 :]
    grad[base:] = jnp.concatenate([last[: rows // 2], last[rows // 2 :]], axis=1).astype(grad.dtype)


def back_kernel(extent, half, *refs):
    pieces, feature_pieces = refs[:3], refs[3:6]
    weights, up_weights, unsort, sorted_act, slope, coarse_grad, dpre2, grads = refs[6:]
    chans3 = pieces[0].shape[0]
    columns, chans = feature_pieces[0].shape[0] // 2, feature_pieces[0].shape[2]
    ddown = fold_taps(dot(weights[...], coarse_stack(pieces)), chans3, LANES // 2)
    own_ddown = jnp.where(own_lanes(half[0], extent, ddown.shape), ddown, 0.0).astype(BF16)
    ddown = ddown.astype(BF16)
    spread = dot(up_weights[...], ddown).astype(BF16)
    rows = spread.shape[0] // 2
    total = None
    for tile in range(columns // 2):
        lanes = slice(tile * LANES, (tile + 1) * LANES)
        both = dot(jnp.concatenate([spread[:rows, lanes], spread[rows:, lanes]], axis=1), unsort[...])
        for member in range(2):
            column = tile + member * (columns // 2)
            dpre = both[:, member * LANES : (member + 1) * LANES] * slope[column]
            dpre = dpre.astype(BF16)
            parts = [dpre[place * chans : (place + 1) * chans] for place in range(4)]
            for place in range(4):
                dpre2[2 * column + place // 2, place % 2] = parts[place]
            place = column - (columns - extent) * half[0]
            inside = (place >= 0) & (place < extent)
            parts = [jnp.where(inside, part.astype(F32), 0.0) for part in parts]
            moved = jnp.concatenate([tap_stack(part, LANES) for part in parts], axis=1)
            term = dot_lanes(moved, fine_stack(feature_pieces, column))
            total = term if total is None else total + term
    base = coarse_grad.shape[0]
    grads[:base] = coarse_grad[...]
    grads[base:] = jnp.zeros((grads.shape[0] - base, LANES), grads.dtype)
    base = store_tiles(grads, base, total)
    grad_down = dot_lanes(sorted_act[...], own_ddown)
    rows = grad_down.shape[0] // 2
    grads[base : base + rows] = jnp.concatenate(
        [grad_down[:rows], grad_down[rows:]], axis=1
    ).astype(grads.dtype)


def input_kernel(half, *refs):
    pieces, (weights, out) = refs[:3], refs[3:]
    cells, chans = pieces[0].shape[0], pieces[0].shape[2]
    count = out.shape[0]
    for column in range(count // 2):
        stack = fine_stack(pieces, column, (half[0], cells - count, count))
        products = dot(weights[...], stack)
        for place in range(4):
            total = fold_taps(products[:, place * LANES : (place + 1) * LANES], chans, LANES)
            out[2 * column + place // 2, place % 2] = total.astype(BF16)


def assemble_kernel(fine_scale, coarse_scale, rows, fine, down, coarse):
    def pieces(start, count, width, scale):
        tile = rows[start : start + count].astype(F32) * scale
        return [
            (tile if lane == 0 else pltpu.roll(tile, LANES - lane, 1))[:, :width]
            for lane in range(0, LANES, width)
        ]

    chans, chans3 = fine.shape[1], coarse.shape[1]
    for tile in range(4):
        for h, part in enumerate(pieces(3 * tile * chans3, 3 * chans3, chans3, coarse_scale)):
            for c in range(3):
                coarse[6 * tile + 3 * h + c] = part[c * chans3 : (c + 1) * chans3]
    base = 12 * chans3
    low, high = pieces(base, 3 * chans3 // 2, chans3, coarse_scale)
    coarse[24] = low[:chans3]
    coarse[25] = jnp.concatenate([low[chans3:], high[: chans3 // 2]], axis=0)
    coarse[26] = high[chans3 // 2 :]
    base += 3 * chans3 // 2
    for tile in range(3):
        for h, part in enumerate(pieces(base, 3 * chans, chans, fine_scale)):
            for c in range(3):
                if 4 * tile + h < 9:
                    fine[3 * (4 * tile + h) + c] = part[c * chans : (c + 1) * chans]
        base += 3 * chans
    for last, part in enumerate(pieces(base, 4 * chans, chans3, coarse_scale)):
        for first in range(4):
            down[2 * first + last] = part[first * chans : (first + 1) * chans]


def tap_matrix(weights):
    taps, outs, ins = weights.shape
    return jnp.transpose(weights.reshape(9, 3, outs, ins), (1, 2, 0, 3)).reshape(3 * outs, 9 * ins)


def reversed_taps(weights):
    return jnp.transpose(weights[::-1], (0, 2, 1))


def sort_matrix():
    table = np.zeros((2 * LANES, 2 * LANES), np.float32)
    for sample in range(2):
        for z in range(LANES):
            table[sample * LANES + z, (z % 2) * LANES + sample * (LANES // 2) + z // 2] = 1.0
    return table


def trade(parts, axis, groups=None):
    return lax.all_to_all(
        parts, axis, split_axis=0, concat_axis=0, axis_index_groups=groups, tiled=True
    )


def share(part, axis, groups=None):
    count = lax.axis_size(axis) if groups is None else len(groups[0])
    return trade(jnp.broadcast_to(part[None], (count, *part.shape)), axis, groups)


def turned(block):
    rows, cols = lax.axis_size("grp"), lax.axis_size("sp")
    batch, shift = cols // 2, QUARTERS // 2
    pairs = []
    for row in range(rows):
        major, quarter = divmod((row - shift) % rows, QUARTERS)
        for col in range(cols):
            there = (QUARTERS * (col % batch) + quarter + shift) % rows
            pairs.append((row * cols + col, there * cols + col // batch * batch + major))
    return lax.ppermute(block, ("grp", "sp"), pairs)


def planes():
    rows, cols = lax.axis_size("grp"), lax.axis_size("sp")
    return [
        [row * cols + col for row in range(start, start + 4) for col in range(cols) if col & 2 == far]
        for start in range(0, rows, 4)
        for far in (0, 2)
    ]


def columns():
    rows, cols = lax.axis_size("grp"), lax.axis_size("sp")
    return [
        [row * cols + col + far for row in range(y, rows, 4) for far in (0, 2)]
        for y in range(4)
        for col in range(cols)
        if col & 2 == 0
    ]


def late():
    return (lax.axis_index("grp") % 4 < 2).astype(jnp.int32)


def for_plane(cells):
    lead = cells.shape[0] // 4
    parts = cells.reshape(lead, 2, 2, QUARTERS, 8, LANES)
    parts = jnp.roll(jnp.transpose(parts, (3, 0, 2, 1, 4, 5)), QUARTERS // 2, axis=0)
    blank = jnp.zeros_like(parts)
    low = upper_half() == 0
    both = [jnp.where(low, parts, blank), jnp.where(low, blank, parts)]
    return jnp.concatenate(both, axis=1).reshape(-1, 16, LANES)


def for_column(got):
    lead = lax.axis_size("sp") // 8
    parts = got.reshape(4, 2, lead, 2, 2, 8, LANES)
    parts = jnp.where(upper_half() == 0, parts[:, 0], parts[:, 1])
    parts = jnp.transpose(parts, (1, 2, 3, 0, 4, 5))
    parts = jnp.stack([parts, jnp.zeros_like(parts)], axis=1).reshape(4 * lead, 2, 32, LANES)
    steps = 4 * lead
    shift = 2 * far_side() + late()
    twice = jnp.concatenate([parts, parts], axis=0)
    return lax.dynamic_slice_in_dim(twice, steps - shift, steps, axis=0).reshape(-1, 32, LANES)


def from_column(got):
    parts = got.reshape(-1, 2, 32, LANES)
    steps = parts.shape[0]
    sample = (lax.axis_index("grp") // 4 - late()) % steps
    return jnp.where(sample // 2 % 2 == 0, parts[:, 0], parts[:, 1]).reshape(-1, LANES)


def far_side():
    return lax.axis_index("sp") // 2 % 2


def far_exchange(parts):
    near = far_side() == 0
    kept = jnp.where(near, parts[:, 0], parts[:, 1])
    sent = jnp.where(near, parts[:, 1], parts[:, 0])
    got = lax.ppermute(sent, "sp", [(col, col ^ 2) for col in range(lax.axis_size("sp"))])
    return jnp.stack([jnp.where(near, kept, got), jnp.where(near, got, kept)], axis=2)


def near_exchange(parts):
    cols, lead = lax.axis_size("sp"), parts.shape[0]
    groups = [
        [start + 4 * far + core for far in range(lead) for core in (0, 1)]
        for half in range(0, cols, 4 * lead)
        for start in (half, half + 2)
    ]
    return trade(parts.reshape(2 * lead, *parts.shape[2:]), "sp", groups).reshape(parts.shape)


def local(features, weight_fine, weight_down, weight_coarse, cotangent):
    batch, chans, x_cells, y_cells, z_cells = features.shape
    chans3 = weight_down.shape[1]
    rows, cols = lax.axis_size("grp"), lax.axis_size("sp")
    width = batch * z_cells // 2
    extent = batch + reach()
    wider = extent * z_cells // 2
    fine_scale = 1.0 / math.sqrt(batch * x_cells * cols * y_cells * rows * z_cells)
    coarse_scale = 1.0 / math.sqrt(batch * x_cells * cols * y_cells * rows * z_cells // 8)
    shape = jax.ShapeDtypeStruct
    near = planes()
    unit = len(near[0]) * 8
    grad_rows = -(-(27 * chans3 // 2 + 9 * chans + 2 * chans3) // unit) * unit
    half = upper_half().astype(jnp.int32).reshape(1)

    sort = jnp.asarray(sort_matrix(), BF16)
    unsort = jnp.asarray(sort_matrix().T, BF16)
    parted = weight_down.reshape(2, 2, 2, chans3, chans)
    down_matrix = jnp.transpose(parted, (3, 2, 0, 1, 4)).reshape(chans3, 8 * chans)

    halves = [list(range(batch)), list(range(batch, cols))]
    own = trade(jnp.transpose(features, (0, 2, 3, 1, 4)), "sp", halves)
    own = own.reshape(batch * x_cells, y_cells, chans, LANES)

    block = (rows, width // 2 // rows, LANES)
    cells = pl.pallas_call(
        pack_kernel, out_shape=shape((width // 2, LANES), BF16), interpret=INTERPRET
    )(cotangent.reshape(chans3, width))
    cells = turned(cells).reshape(block)
    matrices = [
        tap_matrix(weight_fine),
        tap_matrix(reversed_taps(weight_fine)),
        tap_matrix(weight_coarse),
        tap_matrix(reversed_taps(weight_coarse)),
        down_matrix,
        down_matrix.T,
    ]
    own, cells, *matrices = lax.optimization_barrier((own, cells, *matrices))
    fine_matrix, fine_back, coarse_matrix, coarse_back, down_matrix, up_matrix = matrices
    own = joined(own, arrival(nearest(own, reach() * x_cells), 0, True))
    cells = jnp.roll(trade(cells, "grp"), -(QUARTERS // 2), axis=0).reshape(width // 2, LANES)
    upstream = joined(cells, arrival(nearest(cells, reach() * QUARTERS * block[1]), 0, True))

    feature_pieces = fine_pieces(own)
    down, sorted_act, slope = call(
        down_kernel,
        (
            shape((chans3, wider), BF16),
            shape((8 * chans, wider), BF16),
            shape((extent, 4 * chans, LANES), F32),
        ),
        half,
        *feature_pieces,
        fine_matrix,
        down_matrix,
        sort,
    )
    down_pieces = coarse_pieces(down)
    coarse, dpre3 = call(
        coarse_kernel,
        (shape(upstream.shape, BF16), shape((chans3, wider), BF16)),
        half,
        *down_pieces,
        coarse_matrix,
        upstream,
    )
    coarse_grad = call(
        partial(coarse_grad_kernel, batch),
        shape((27 * chans3 // 2, LANES), BF16),
        half,
        *down_pieces,
        dpre3,
    )
    dpre_pieces = coarse_pieces(dpre3)
    coarse_grad, *dpre_pieces = lax.optimization_barrier((coarse_grad, *dpre_pieces))

    dpre2, grads = call(
        partial(back_kernel, batch),
        (shape(own.shape, BF16), shape((grad_rows, LANES), BF16)),
        half,
        *dpre_pieces,
        *feature_pieces,
        coarse_back,
        up_matrix,
        unsort,
        sorted_act,
        slope,
        coarse_grad,
    )
    coarse = jnp.where(upper_half() == 0, coarse[: width // 2], coarse[-(width // 2) :])
    grads = grads.reshape(len(near[0]), -1, LANES)
    kept = grads.shape[1]
    coarse = for_plane(coarse.reshape(batch, QUARTERS, 8, LANES))
    mixed = trade(jnp.concatenate([grads, coarse], axis=1), ("grp", "sp"), near)
    part = jnp.sum(mixed[:, :kept].astype(F32), axis=0).astype(BF16)
    coarse = for_column(mixed[:, kept:])
    gradient = call(
        input_kernel,
        shape((batch * x_cells, *own.shape[1:]), BF16),
        half,
        *fine_pieces(dpre2),
        fine_back,
    )
    part, gradient, coarse = lax.optimization_barrier((part, gradient, coarse))
    gradient = far_exchange(gradient.reshape(batch // 4, 2, 2, x_cells, y_cells, chans, LANES))
    part = jnp.broadcast_to(part[None], (coarse.shape[0], *part.shape))
    mixed = trade(jnp.concatenate([part, coarse], axis=1), ("grp", "sp"), columns())
    part = jnp.sum(mixed[:, :kept].astype(F32), axis=0).astype(BF16)
    coarse = from_column(mixed[:, kept:])
    grads = share(part, ("grp", "sp"), near).reshape(grad_rows, LANES)
    grads, gradient = lax.optimization_barrier((grads, gradient))
    gradient = near_exchange(gradient)
    grad_input = jnp.transpose(gradient, (0, 2, 1, 5, 3, 4, 6)).reshape(features.shape)

    result = pl.pallas_call(
        unpack_kernel, out_shape=shape((chans3, width), BF16), interpret=INTERPRET
    )(coarse)
    result = result.reshape(cotangent.shape)

    grad_fine, grad_down, grad_coarse = pl.pallas_call(
        partial(assemble_kernel, fine_scale, coarse_scale),
        out_shape=(
            shape(weight_fine.shape, F32),
            shape((8, chans, chans3), F32),
            shape(weight_coarse.shape, F32),
        ),
        interpret=INTERPRET,
    )(grads)
    return result, grad_input, grad_fine, jnp.swapaxes(grad_down, 1, 2), grad_coarse


def solution(mesh):
    placed = (P(None, None, "sp", "grp", None), P(), P(), P(), P("grp", None, "sp", None))
    return jax.shard_map(
        local,
        mesh=mesh,
        in_specs=placed,
        out_specs=(P("grp", None, "sp", None), P(None, None, "sp", "grp", None), P(), P(), P()),
        check_vma=False,
    )
```

```python
import math
from functools import partial

import jax
import jax.numpy as jnp
import numpy as np
from jax import lax
from jax.experimental import pallas as pl
from jax.experimental.pallas import tpu as pltpu
from jax.sharding import PartitionSpec as P

QUARTERS = 4
LANES = 128
STEPS = (-1, 0, 1)
F32 = jnp.float32
BF16 = jnp.bfloat16
INTERPRET = False


def call(kernel, outs, half, *operands):
    spaces = [pltpu.SMEM] + [pltpu.VMEM] * len(operands)
    return pl.pallas_call(
        kernel,
        out_shape=outs,
        in_specs=[pl.BlockSpec(memory_space=space) for space in spaces],
        compiler_params=pltpu.CompilerParams(vmem_limit_bytes=28 * 1024 * 1024),
        interpret=INTERPRET,
    )(half, *operands)


def arrival(block, step_y, across):
    rows, cols = lax.axis_size("grp"), lax.axis_size("sp")
    pairs = []
    for row in range(rows):
        for col in range(cols):
            if 0 <= row + step_y < rows:
                source = (col + cols // 2) % cols if across else col
                pairs.append(((row + step_y) * cols + source, row * cols + col))
    return lax.ppermute(block, ("grp", "sp"), pairs)


def upper_half():
    return lax.axis_index("sp") // (lax.axis_size("sp") // 2)


def reach():
    return min(4, lax.axis_size("sp") // 2)


def joined(own, other):
    low = jnp.concatenate([own, other], axis=0)
    return jnp.where(upper_half() == 0, low, jnp.concatenate([other, own], axis=0))


def nearest(block, count):
    return jnp.where(upper_half() == 0, block[-count:], block[:count])


def fine_pieces(block):
    return [block, arrival(block[:, 1:], -1, False), arrival(block[:, :1], 1, False)]


def coarse_pieces(block):
    return [block, arrival(block, -1, False), arrival(block, 1, False)]


def silu_slope(values, sigma):
    return sigma * (1.0 + values * (1.0 - sigma))


def dot(left, right):
    return lax.dot_general(left, right, (((1,), (0,)), ((), ())), preferred_element_type=F32)


def dot_lanes(left, right):
    return lax.dot_general(left, right, (((1,), (1,)), ((), ())), preferred_element_type=F32)


def shifted(values, step, span):
    if step == 0:
        return values
    place = lax.broadcasted_iota(jnp.int32, values.shape, 1) % span
    width = values.shape[1]
    moved = pltpu.roll(values, (-step) % width, 1)
    return jnp.where(place == (span - 1 if step > 0 else 0), 0.0, moved)


def fold_taps(products, chans, span):
    total = products[chans : 2 * chans]
    total = total + shifted(products[:chans], -1, span)
    return total + shifted(products[2 * chans :], 1, span)


def fine_stack(refs, column, shift=None):
    center, before, after = refs
    cells = center.shape[0]

    def cell(x, y):
        inside = None
        if shift is not None:
            half, skip, count = shift
            inside = half == 1 if x < 0 else half == 0 if x >= count else None
            x = jnp.clip(x + skip * half, 0, cells - 1)
        elif not 0 <= x < cells:
            return jnp.zeros(center.shape[2:], center.dtype)
        value = before[x, 0] if y < 0 else after[x, 0] if y > 1 else center[x, y]
        return value if inside is None else jnp.where(inside, value, jnp.zeros_like(value))

    return jnp.concatenate(
        [
            jnp.concatenate(
                [cell(2 * column + x + a, y + b) for x in (0, 1) for y in (0, 1)], axis=1
            )
            for a in STEPS
            for b in STEPS
        ],
        axis=0,
    )


def coarse_stack(refs):
    tiles = refs[0].shape[1] // LANES
    low = lax.broadcasted_iota(jnp.int32, (refs[0].shape[0], LANES), 1) < LANES // 2
    lined = []
    for ref in (refs[1], refs[0], refs[2]):
        own = [ref[:, tile * LANES : (tile + 1) * LANES] for tile in range(tiles)]
        first = jnp.where(low, own[-1].astype(F32), 0.0)
        last = jnp.where(low, 0.0, own[0].astype(F32))
        first, last = [pltpu.roll(tile, LANES // 2, 1).astype(BF16) for tile in (first, last)]
        lined.append([first, *own, last])
    return jnp.concatenate(
        [jnp.concatenate(lined[b][a : a + tiles], axis=1) for a in range(3) for b in range(3)],
        axis=0,
    )


def own_lanes(half, extent, shape):
    lane = lax.broadcasted_iota(jnp.int32, shape, 1)
    tiles = shape[1] // LANES
    x = lane // LANES + tiles * (lane % LANES // (LANES // 2)) - (2 * tiles - extent) * half
    return (x >= 0) & (x < extent)


def down_kernel(half, *refs):
    pieces, (weights, down_weights, sort, down, sorted_act, slope) = refs[:3], refs[3:]
    columns, chans = pieces[0].shape[0] // 2, pieces[0].shape[2]
    for tile in range(columns // 2):
        acts = []
        for column in (tile, tile + columns // 2):
            products = dot(weights[...], fine_stack(pieces, column))
            parts = []
            for place in range(4):
                pre = fold_taps(products[:, place * LANES : (place + 1) * LANES], chans, LANES)
                sigma = jax.nn.sigmoid(pre)
                slope[column, place * chans : (place + 1) * chans] = silu_slope(pre, sigma)
                parts.append((pre * sigma).astype(BF16))
            acts.append(jnp.concatenate(parts, axis=0))
        parted = dot(jnp.concatenate(acts, axis=1), sort[...]).astype(BF16)
        stacked = jnp.concatenate([parted[:, :LANES], parted[:, LANES:]], axis=0)
        lanes = slice(tile * LANES, (tile + 1) * LANES)
        sorted_act[:, lanes] = stacked
        down[:, lanes] = dot(down_weights[...], stacked).astype(BF16)


def coarse_kernel(half, *refs):
    pieces, (weights, upstream, out, dpre) = refs[:3], refs[3:]
    chans, width = pieces[0].shape
    pre = fold_taps(dot(weights[...], coarse_stack(pieces)), chans, LANES // 2)
    sigma = jax.nn.sigmoid(pre)
    act = pre * sigma
    slope = silu_slope(pre, sigma)
    tiles = width // LANES
    rows = LANES // 4
    for tile in range(tiles):
        lanes = slice(tile * LANES, (tile + 1) * LANES)
        ends = [tile * rows, (tile + tiles) * rows]
        packed = jnp.concatenate([upstream[end : end + rows] for end in ends], axis=0)
        dpre[:, lanes] = (unpacked(packed.astype(F32)) * slope[:, lanes]).astype(BF16)
        both = packed_cells(act[:, lanes]).astype(BF16)
        for member, end in enumerate(ends):
            out[end : end + rows] = both[member * rows : (member + 1) * rows]


def packed_cells(values):
    turned = jnp.concatenate([values, values], axis=0).T.reshape(LANES // 16, 2, 8, LANES)
    low = lax.broadcasted_iota(jnp.int32, (LANES // 16, 8, LANES), 2) < LANES // 2
    return jnp.where(low, turned[:, 0], turned[:, 1]).reshape(LANES // 2, LANES)


def unpacked(values):
    first = values.reshape(LANES // 16, 1, 8, LANES)
    second = pltpu.roll(values, LANES // 2, 1).reshape(LANES // 16, 1, 8, LANES)
    turned = jnp.concatenate([first, second], axis=1).reshape(LANES, LANES).T
    return turned[: LANES // 2]


def pack_kernel(values, out):
    for tile in range(values.shape[1] // LANES):
        part = values[:, tile * LANES : (tile + 1) * LANES].astype(F32)
        out[tile * LANES // 2 : (tile + 1) * LANES // 2] = packed_cells(part).astype(BF16)


def unpack_kernel(values, out):
    for tile in range(out.shape[1] // LANES):
        part = values[tile * LANES // 2 : (tile + 1) * LANES // 2].astype(F32)
        out[:, tile * LANES : (tile + 1) * LANES] = unpacked(part).astype(BF16)


def tap_stack(values, span):
    values = values.astype(F32)
    return jnp.concatenate([shifted(values, -step, span).astype(BF16) for step in STEPS], axis=0)


def store_tiles(ref, base, values):
    rows, cols = values.shape
    for start in range(0, cols, LANES):
        width = min(LANES, cols - start)
        ref[base : base + rows, :width] = values[:, start : start + width].astype(ref.dtype)
        base += rows
    return base


def coarse_grad_kernel(extent, half, *refs):
    pieces, (dpre, grad) = refs[:3], refs[3:]
    own = jnp.where(own_lanes(half[0], extent, dpre.shape), dpre[...].astype(F32), 0.0)
    products = dot_lanes(tap_stack(own, LANES // 2), coarse_stack(pieces))
    rows, cols = products.shape
    base = store_tiles(grad, 0, products[:, : cols - LANES // 2])
    last = products[:, cols - LANES // 2 :]
    grad[base:] = jnp.concatenate([last[: rows // 2], last[rows // 2 :]], axis=1).astype(grad.dtype)


def back_kernel(extent, half, *refs):
    pieces, feature_pieces = refs[:3], refs[3:6]
    weights, up_weights, unsort, sorted_act, slope, coarse_grad, dpre2, grads = refs[6:]
    chans3 = pieces[0].shape[0]
    columns, chans = feature_pieces[0].shape[0] // 2, feature_pieces[0].shape[2]
    ddown = fold_taps(dot(weights[...], coarse_stack(pieces)), chans3, LANES // 2)
    own_ddown = jnp.where(own_lanes(half[0], extent, ddown.shape), ddown, 0.0).astype(BF16)
    ddown = ddown.astype(BF16)
    spread = dot(up_weights[...], ddown).astype(BF16)
    rows = spread.shape[0] // 2
    total = None
    for tile in range(columns // 2):
        lanes = slice(tile * LANES, (tile + 1) * LANES)
        both = dot(jnp.concatenate([spread[:rows, lanes], spread[rows:, lanes]], axis=1), unsort[...])
        for member in range(2):
            column = tile + member * (columns // 2)
            dpre = both[:, member * LANES : (member + 1) * LANES] * slope[column]
            dpre = dpre.astype(BF16)
            parts = [dpre[place * chans : (place + 1) * chans] for place in range(4)]
            for place in range(4):
                dpre2[2 * column + place // 2, place % 2] = parts[place]
            place = column - (columns - extent) * half[0]
            inside = (place >= 0) & (place < extent)
            parts = [jnp.where(inside, part.astype(F32), 0.0) for part in parts]
            moved = jnp.concatenate([tap_stack(part, LANES) for part in parts], axis=1)
            term = dot_lanes(moved, fine_stack(feature_pieces, column))
            total = term if total is None else total + term
    base = coarse_grad.shape[0]
    grads[:base] = coarse_grad[...]
    grads[base:] = jnp.zeros((grads.shape[0] - base, LANES), grads.dtype)
    base = store_tiles(grads, base, total)
    grad_down = dot_lanes(sorted_act[...], own_ddown)
    rows = grad_down.shape[0] // 2
    grads[base : base + rows] = jnp.concatenate(
        [grad_down[:rows], grad_down[rows:]], axis=1
    ).astype(grads.dtype)


def input_kernel(half, *refs):
    pieces, (weights, out) = refs[:3], refs[3:]
    cells, chans = pieces[0].shape[0], pieces[0].shape[2]
    count = out.shape[0]
    for column in range(count // 2):
        stack = fine_stack(pieces, column, (half[0], cells - count, count))
        products = dot(weights[...], stack)
        for place in range(4):
            total = fold_taps(products[:, place * LANES : (place + 1) * LANES], chans, LANES)
            out[2 * column + place // 2, place % 2] = total.astype(BF16)


def assemble_kernel(fine_scale, coarse_scale, rows, fine, down, coarse):
    def pieces(start, count, width, scale):
        tile = rows[start : start + count].astype(F32) * scale
        return [
            (tile if lane == 0 else pltpu.roll(tile, LANES - lane, 1))[:, :width]
            for lane in range(0, LANES, width)
        ]

    chans, chans3 = fine.shape[1], coarse.shape[1]
    for tile in range(4):
        for h, part in enumerate(pieces(3 * tile * chans3, 3 * chans3, chans3, coarse_scale)):
            for c in range(3):
                coarse[6 * tile + 3 * h + c] = part[c * chans3 : (c + 1) * chans3]
    base = 12 * chans3
    low, high = pieces(base, 3 * chans3 // 2, chans3, coarse_scale)
    coarse[24] = low[:chans3]
    coarse[25] = jnp.concatenate([low[chans3:], high[: chans3 // 2]], axis=0)
    coarse[26] = high[chans3 // 2 :]
    base += 3 * chans3 // 2
    for tile in range(3):
        for h, part in enumerate(pieces(base, 3 * chans, chans, fine_scale)):
            for c in range(3):
                if 4 * tile + h < 9:
                    fine[3 * (4 * tile + h) + c] = part[c * chans : (c + 1) * chans]
        base += 3 * chans
    for last, part in enumerate(pieces(base, 4 * chans, chans3, coarse_scale)):
        for first in range(4):
            down[2 * first + last] = part[first * chans : (first + 1) * chans]


def tap_matrix(weights):
    taps, outs, ins = weights.shape
    return jnp.transpose(weights.reshape(9, 3, outs, ins), (1, 2, 0, 3)).reshape(3 * outs, 9 * ins)


def reversed_taps(weights):
    return jnp.transpose(weights[::-1], (0, 2, 1))


def sort_matrix():
    table = np.zeros((2 * LANES, 2 * LANES), np.float32)
    for sample in range(2):
        for z in range(LANES):
            table[sample * LANES + z, (z % 2) * LANES + sample * (LANES // 2) + z // 2] = 1.0
    return table


def trade(parts, axis, groups=None):
    return lax.all_to_all(
        parts, axis, split_axis=0, concat_axis=0, axis_index_groups=groups, tiled=True
    )


def share(part, axis, groups=None):
    count = lax.axis_size(axis) if groups is None else len(groups[0])
    return trade(jnp.broadcast_to(part[None], (count, *part.shape)), axis, groups)


def turned(block):
    rows, cols = lax.axis_size("grp"), lax.axis_size("sp")
    batch, shift = cols // 2, QUARTERS // 2
    pairs = []
    for row in range(rows):
        major, quarter = divmod((row - shift) % rows, QUARTERS)
        for col in range(cols):
            there = (QUARTERS * (col % batch) + quarter + shift) % rows
            pairs.append((row * cols + col, there * cols + col // batch * batch + major))
    return lax.ppermute(block, ("grp", "sp"), pairs)


def planes():
    rows, cols = lax.axis_size("grp"), lax.axis_size("sp")
    return [
        [row * cols + col for row in range(start, start + 4) for col in range(cols) if col & 2 == far]
        for start in range(0, rows, 4)
        for far in (0, 2)
    ]


def columns():
    rows, cols = lax.axis_size("grp"), lax.axis_size("sp")
    return [
        [row * cols + col + far for row in range(y, rows, 4) for far in (0, 2)]
        for y in range(4)
        for col in range(cols)
        if col & 2 == 0
    ]


def late():
    return (lax.axis_index("grp") % 4 < 2).astype(jnp.int32)


def for_plane(cells):
    lead = cells.shape[0] // 4
    parts = cells.reshape(lead, 2, 2, QUARTERS, 8, LANES)
    parts = jnp.roll(jnp.transpose(parts, (3, 0, 2, 1, 4, 5)), QUARTERS // 2, axis=0)
    blank = jnp.zeros_like(parts)
    low = upper_half() == 0
    both = [jnp.where(low, parts, blank), jnp.where(low, blank, parts)]
    return jnp.concatenate(both, axis=1).reshape(-1, 16, LANES)


def for_column(got):
    lead = lax.axis_size("sp") // 8
    parts = got.reshape(4, 2, lead, 2, 2, 8, LANES)
    parts = jnp.where(upper_half() == 0, parts[:, 0], parts[:, 1])
    parts = jnp.transpose(parts, (1, 2, 3, 0, 4, 5))
    parts = jnp.stack([parts, jnp.zeros_like(parts)], axis=1).reshape(4 * lead, 2, 32, LANES)
    steps = 4 * lead
    shift = 2 * far_side() + late()
    twice = jnp.concatenate([parts, parts], axis=0)
    return lax.dynamic_slice_in_dim(twice, steps - shift, steps, axis=0).reshape(-1, 32, LANES)


def from_column(got):
    parts = got.reshape(-1, 2, 32, LANES)
    steps = parts.shape[0]
    sample = (lax.axis_index("grp") // 4 - late()) % steps
    return jnp.where(sample // 2 % 2 == 0, parts[:, 0], parts[:, 1]).reshape(-1, LANES)


def far_side():
    return lax.axis_index("sp") // 2 % 2


def far_exchange(parts):
    near = far_side() == 0
    kept = jnp.where(near, parts[:, 0], parts[:, 1])
    sent = jnp.where(near, parts[:, 1], parts[:, 0])
    got = lax.ppermute(sent, "sp", [(col, col ^ 2) for col in range(lax.axis_size("sp"))])
    return jnp.stack([jnp.where(near, kept, got), jnp.where(near, got, kept)], axis=2)


def matched(parts, far, core):
    if parts.shape[0] > 1:
        parts = jnp.where(far == 0, parts, parts[::-1])
    return jnp.where(core == 0, parts, parts[:, ::-1])


def near_exchange(parts):
    cols, lead = lax.axis_size("sp"), parts.shape[0]
    place = lax.axis_index("sp")
    far, core = place // 4 % lead, place % 2
    parts = matched(parts, far, core)
    got = [
        [
            parts[x, c]
            if x == c == 0
            else lax.ppermute(parts[x, c], "sp", [(col, col ^ (4 * x + c)) for col in range(cols)])
            for c in (0, 1)
        ]
        for x in range(lead)
    ]
    return matched(jnp.stack([jnp.stack(row) for row in got]), far, core)


def local(features, weight_fine, weight_down, weight_coarse, cotangent):
    batch, chans, x_cells, y_cells, z_cells = features.shape
    chans3 = weight_down.shape[1]
    rows, cols = lax.axis_size("grp"), lax.axis_size("sp")
    width = batch * z_cells // 2
    extent = batch + reach()
    wider = extent * z_cells // 2
    fine_scale = 1.0 / math.sqrt(batch * x_cells * cols * y_cells * rows * z_cells)
    coarse_scale = 1.0 / math.sqrt(batch * x_cells * cols * y_cells * rows * z_cells // 8)
    shape = jax.ShapeDtypeStruct
    near = planes()
    unit = len(near[0]) * 8
    grad_rows = -(-(27 * chans3 // 2 + 9 * chans + 2 * chans3) // unit) * unit
    half = upper_half().astype(jnp.int32).reshape(1)

    sort = jnp.asarray(sort_matrix(), BF16)
    unsort = jnp.asarray(sort_matrix().T, BF16)
    parted = weight_down.reshape(2, 2, 2, chans3, chans)
    down_matrix = jnp.transpose(parted, (3, 2, 0, 1, 4)).reshape(chans3, 8 * chans)

    halves = [list(range(batch)), list(range(batch, cols))]
    own = trade(jnp.transpose(features, (0, 2, 3, 1, 4)), "sp", halves)
    own = own.reshape(batch * x_cells, y_cells, chans, LANES)

    block = (rows, width // 2 // rows, LANES)
    cells = pl.pallas_call(
        pack_kernel, out_shape=shape((width // 2, LANES), BF16), interpret=INTERPRET
    )(cotangent.reshape(chans3, width))
    cells = turned(cells).reshape(block)
    matrices = [
        tap_matrix(weight_fine),
        tap_matrix(reversed_taps(weight_fine)),
        tap_matrix(weight_coarse),
        tap_matrix(reversed_taps(weight_coarse)),
        down_matrix,
        down_matrix.T,
    ]
    own, cells, *matrices = lax.optimization_barrier((own, cells, *matrices))
    fine_matrix, fine_back, coarse_matrix, coarse_back, down_matrix, up_matrix = matrices
    own = joined(own, arrival(nearest(own, reach() * x_cells), 0, True))
    cells = jnp.roll(trade(cells, "grp"), -(QUARTERS // 2), axis=0).reshape(width // 2, LANES)
    upstream = joined(cells, arrival(nearest(cells, reach() * QUARTERS * block[1]), 0, True))

    feature_pieces = fine_pieces(own)
    down, sorted_act, slope = call(
        down_kernel,
        (
            shape((chans3, wider), BF16),
            shape((8 * chans, wider), BF16),
            shape((extent, 4 * chans, LANES), F32),
        ),
        half,
        *feature_pieces,
        fine_matrix,
        down_matrix,
        sort,
    )
    down_pieces = coarse_pieces(down)
    coarse, dpre3 = call(
        coarse_kernel,
        (shape(upstream.shape, BF16), shape((chans3, wider), BF16)),
        half,
        *down_pieces,
        coarse_matrix,
        upstream,
    )
    coarse_grad = call(
        partial(coarse_grad_kernel, batch),
        shape((27 * chans3 // 2, LANES), BF16),
        half,
        *down_pieces,
        dpre3,
    )
    dpre_pieces = coarse_pieces(dpre3)
    coarse_grad, *dpre_pieces = lax.optimization_barrier((coarse_grad, *dpre_pieces))

    dpre2, grads = call(
        partial(back_kernel, batch),
        (shape(own.shape, BF16), shape((grad_rows, LANES), BF16)),
        half,
        *dpre_pieces,
        *feature_pieces,
        coarse_back,
        up_matrix,
        unsort,
        sorted_act,
        slope,
        coarse_grad,
    )
    coarse = jnp.where(upper_half() == 0, coarse[: width // 2], coarse[-(width // 2) :])
    spread = fine_pieces(dpre2)
    grads, *spread[1:] = lax.optimization_barrier((grads, *spread[1:]))
    grads = grads.reshape(len(near[0]), -1, LANES)
    kept = grads.shape[1]
    coarse = for_plane(coarse.reshape(batch, QUARTERS, 8, LANES))
    mixed = trade(jnp.concatenate([grads, coarse], axis=1), ("grp", "sp"), near)
    part = jnp.sum(mixed[:, :kept].astype(F32), axis=0).astype(BF16)
    coarse = for_column(mixed[:, kept:])
    gradient = call(
        input_kernel,
        shape((batch * x_cells, *own.shape[1:]), BF16),
        half,
        *spread,
        fine_back,
    )
    part, gradient, coarse = lax.optimization_barrier((part, gradient, coarse))
    gradient = far_exchange(gradient.reshape(batch // 4, 2, 2, x_cells, y_cells, chans, LANES))
    part = jnp.broadcast_to(part[None], (coarse.shape[0], *part.shape))
    mixed = trade(jnp.concatenate([part, coarse], axis=1), ("grp", "sp"), columns())
    part = jnp.sum(mixed[:, :kept].astype(F32), axis=0).astype(BF16)
    coarse = from_column(mixed[:, kept:])
    grads = share(part, ("grp", "sp"), near).reshape(grad_rows, LANES)
    gradient = near_exchange(gradient)
    grads, gradient = lax.optimization_barrier((grads, gradient))
    grad_input = jnp.transpose(gradient, (0, 2, 1, 5, 3, 4, 6)).reshape(features.shape)

    result = pl.pallas_call(
        unpack_kernel, out_shape=shape((chans3, width), BF16), interpret=INTERPRET
    )(coarse)
    result = result.reshape(cotangent.shape)

    grad_fine, grad_down, grad_coarse = pl.pallas_call(
        partial(assemble_kernel, fine_scale, coarse_scale),
        out_shape=(
            shape(weight_fine.shape, F32),
            shape((8, chans, chans3), F32),
            shape(weight_coarse.shape, F32),
        ),
        interpret=INTERPRET,
    )(grads)
    return result, grad_input, grad_fine, jnp.swapaxes(grad_down, 1, 2), grad_coarse


def solution(mesh):
    placed = (P(None, None, "sp", "grp", None), P(), P(), P(), P("grp", None, "sp", None))
    return jax.shard_map(
        local,
        mesh=mesh,
        in_specs=placed,
        out_specs=(P("grp", None, "sp", None), P(None, None, "sp", "grp", None), P(), P(), P()),
        check_vma=False,
    )
```

```python
import math
from functools import partial

import jax
import jax.numpy as jnp
import numpy as np
from jax import lax
from jax.experimental import pallas as pl
from jax.experimental.pallas import tpu as pltpu
from jax.sharding import PartitionSpec as P

QUARTERS = 4
LANES = 128
STEPS = (-1, 0, 1)
F32 = jnp.float32
BF16 = jnp.bfloat16
INTERPRET = False


def call(kernel, outs, half, *operands):
    spaces = [pltpu.SMEM] + [pltpu.VMEM] * len(operands)
    return pl.pallas_call(
        kernel,
        out_shape=outs,
        in_specs=[pl.BlockSpec(memory_space=space) for space in spaces],
        compiler_params=pltpu.CompilerParams(vmem_limit_bytes=28 * 1024 * 1024),
        interpret=INTERPRET,
    )(half, *operands)


def arrival(block, step_y, across):
    rows, cols = lax.axis_size("grp"), lax.axis_size("sp")
    pairs = []
    for row in range(rows):
        for col in range(cols):
            if 0 <= row + step_y < rows:
                source = (col + cols // 2) % cols if across else col
                pairs.append(((row + step_y) * cols + source, row * cols + col))
    return lax.ppermute(block, ("grp", "sp"), pairs)


def upper_half():
    return lax.axis_index("sp") // (lax.axis_size("sp") // 2)


def reach():
    return min(4, lax.axis_size("sp") // 2)


def joined(own, other):
    low = jnp.concatenate([own, other], axis=0)
    return jnp.where(upper_half() == 0, low, jnp.concatenate([other, own], axis=0))


def nearest(block, count):
    return jnp.where(upper_half() == 0, block[-count:], block[:count])


def fine_pieces(block):
    return [block, arrival(block[:, 1:], -1, False), arrival(block[:, :1], 1, False)]


def coarse_pieces(block):
    return [block, arrival(block, -1, False), arrival(block, 1, False)]


def silu_slope(values, sigma):
    return sigma * (1.0 + values * (1.0 - sigma))


def dot(left, right):
    return lax.dot_general(left, right, (((1,), (0,)), ((), ())), preferred_element_type=F32)


def dot_lanes(left, right):
    return lax.dot_general(left, right, (((1,), (1,)), ((), ())), preferred_element_type=F32)


def shifted(values, step, span):
    if step == 0:
        return values
    place = lax.broadcasted_iota(jnp.int32, values.shape, 1) % span
    width = values.shape[1]
    moved = pltpu.roll(values, (-step) % width, 1)
    return jnp.where(place == (span - 1 if step > 0 else 0), 0.0, moved)


def fold_taps(products, chans, span):
    total = products[chans : 2 * chans]
    total = total + shifted(products[:chans], -1, span)
    return total + shifted(products[2 * chans :], 1, span)


def fine_stack(refs, column, shift=None):
    center, before, after = refs
    cells = center.shape[0]

    def cell(x, y):
        inside = None
        if shift is not None:
            half, skip, count = shift
            inside = half == 1 if x < 0 else half == 0 if x >= count else None
            x = jnp.clip(x + skip * half, 0, cells - 1)
        elif not 0 <= x < cells:
            return jnp.zeros(center.shape[2:], center.dtype)
        value = before[x, 0] if y < 0 else after[x, 0] if y > 1 else center[x, y]
        return value if inside is None else jnp.where(inside, value, jnp.zeros_like(value))

    return jnp.concatenate(
        [
            jnp.concatenate(
                [cell(2 * column + x + a, y + b) for x in (0, 1) for y in (0, 1)], axis=1
            )
            for a in STEPS
            for b in STEPS
        ],
        axis=0,
    )


def coarse_stack(refs):
    tiles = refs[0].shape[1] // LANES
    low = lax.broadcasted_iota(jnp.int32, (refs[0].shape[0], LANES), 1) < LANES // 2
    lined = []
    for ref in (refs[1], refs[0], refs[2]):
        own = [ref[:, tile * LANES : (tile + 1) * LANES] for tile in range(tiles)]
        first = jnp.where(low, own[-1].astype(F32), 0.0)
        last = jnp.where(low, 0.0, own[0].astype(F32))
        first, last = [pltpu.roll(tile, LANES // 2, 1).astype(BF16) for tile in (first, last)]
        lined.append([first, *own, last])
    return jnp.concatenate(
        [jnp.concatenate(lined[b][a : a + tiles], axis=1) for a in range(3) for b in range(3)],
        axis=0,
    )


def own_lanes(half, extent, shape):
    lane = lax.broadcasted_iota(jnp.int32, shape, 1)
    tiles = shape[1] // LANES
    x = lane // LANES + tiles * (lane % LANES // (LANES // 2)) - (2 * tiles - extent) * half
    return (x >= 0) & (x < extent)


def down_kernel(half, *refs):
    pieces, (weights, down_weights, sort, down, sorted_act, slope) = refs[:3], refs[3:]
    columns, chans = pieces[0].shape[0] // 2, pieces[0].shape[2]
    for tile in range(columns // 2):
        acts = []
        for column in (tile, tile + columns // 2):
            products = dot(weights[...], fine_stack(pieces, column))
            parts = []
            for place in range(4):
                pre = fold_taps(products[:, place * LANES : (place + 1) * LANES], chans, LANES)
                sigma = jax.nn.sigmoid(pre)
                slope[column, place * chans : (place + 1) * chans] = silu_slope(pre, sigma)
                parts.append((pre * sigma).astype(BF16))
            acts.append(jnp.concatenate(parts, axis=0))
        parted = dot(jnp.concatenate(acts, axis=1), sort[...]).astype(BF16)
        stacked = jnp.concatenate([parted[:, :LANES], parted[:, LANES:]], axis=0)
        lanes = slice(tile * LANES, (tile + 1) * LANES)
        sorted_act[:, lanes] = stacked
        down[:, lanes] = dot(down_weights[...], stacked).astype(BF16)


def coarse_kernel(half, *refs):
    pieces, (weights, upstream, out, dpre) = refs[:3], refs[3:]
    chans, width = pieces[0].shape
    pre = fold_taps(dot(weights[...], coarse_stack(pieces)), chans, LANES // 2)
    sigma = jax.nn.sigmoid(pre)
    act = pre * sigma
    slope = silu_slope(pre, sigma)
    tiles = width // LANES
    rows = LANES // 4
    for tile in range(tiles):
        lanes = slice(tile * LANES, (tile + 1) * LANES)
        ends = [tile * rows, (tile + tiles) * rows]
        packed = jnp.concatenate([upstream[end : end + rows] for end in ends], axis=0)
        dpre[:, lanes] = (unpacked(packed.astype(F32)) * slope[:, lanes]).astype(BF16)
        both = packed_cells(act[:, lanes]).astype(BF16)
        for member, end in enumerate(ends):
            out[end : end + rows] = both[member * rows : (member + 1) * rows]


def packed_cells(values):
    turned = jnp.concatenate([values, values], axis=0).T.reshape(LANES // 16, 2, 8, LANES)
    low = lax.broadcasted_iota(jnp.int32, (LANES // 16, 8, LANES), 2) < LANES // 2
    return jnp.where(low, turned[:, 0], turned[:, 1]).reshape(LANES // 2, LANES)


def unpacked(values):
    first = values.reshape(LANES // 16, 1, 8, LANES)
    second = pltpu.roll(values, LANES // 2, 1).reshape(LANES // 16, 1, 8, LANES)
    turned = jnp.concatenate([first, second], axis=1).reshape(LANES, LANES).T
    return turned[: LANES // 2]


def pack_kernel(values, out):
    for tile in range(values.shape[1] // LANES):
        part = values[:, tile * LANES : (tile + 1) * LANES].astype(F32)
        out[tile * LANES // 2 : (tile + 1) * LANES // 2] = packed_cells(part).astype(BF16)


def unpack_kernel(values, out):
    for tile in range(out.shape[1] // LANES):
        part = values[tile * LANES // 2 : (tile + 1) * LANES // 2].astype(F32)
        out[:, tile * LANES : (tile + 1) * LANES] = unpacked(part).astype(BF16)


def tap_stack(values, span):
    values = values.astype(F32)
    return jnp.concatenate([shifted(values, -step, span).astype(BF16) for step in STEPS], axis=0)


def store_tiles(ref, base, values):
    rows, cols = values.shape
    for start in range(0, cols, LANES):
        width = min(LANES, cols - start)
        ref[base : base + rows, :width] = values[:, start : start + width].astype(ref.dtype)
        base += rows
    return base


def coarse_grad_kernel(extent, half, *refs):
    pieces, (dpre, grad) = refs[:3], refs[3:]
    own = jnp.where(own_lanes(half[0], extent, dpre.shape), dpre[...].astype(F32), 0.0)
    products = dot_lanes(tap_stack(own, LANES // 2), coarse_stack(pieces))
    rows, cols = products.shape
    base = store_tiles(grad, 0, products[:, : cols - LANES // 2])
    last = products[:, cols - LANES // 2 :]
    grad[base:] = jnp.concatenate([last[: rows // 2], last[rows // 2 :]], axis=1).astype(grad.dtype)


def back_kernel(extent, half, *refs):
    pieces, feature_pieces = refs[:3], refs[3:6]
    weights, up_weights, unsort, sorted_act, slope, coarse_grad, dpre2, grads = refs[6:]
    chans3 = pieces[0].shape[0]
    columns, chans = feature_pieces[0].shape[0] // 2, feature_pieces[0].shape[2]
    ddown = fold_taps(dot(weights[...], coarse_stack(pieces)), chans3, LANES // 2)
    own_ddown = jnp.where(own_lanes(half[0], extent, ddown.shape), ddown, 0.0).astype(BF16)
    ddown = ddown.astype(BF16)
    spread = dot(up_weights[...], ddown).astype(BF16)
    rows = spread.shape[0] // 2
    total = None
    for tile in range(columns // 2):
        lanes = slice(tile * LANES, (tile + 1) * LANES)
        both = dot(jnp.concatenate([spread[:rows, lanes], spread[rows:, lanes]], axis=1), unsort[...])
        for member in range(2):
            column = tile + member * (columns // 2)
            dpre = both[:, member * LANES : (member + 1) * LANES] * slope[column]
            dpre = dpre.astype(BF16)
            parts = [dpre[place * chans : (place + 1) * chans] for place in range(4)]
            for place in range(4):
                dpre2[2 * column + place // 2, place % 2] = parts[place]
            place = column - (columns - extent) * half[0]
            inside = (place >= 0) & (place < extent)
            parts = [jnp.where(inside, part.astype(F32), 0.0) for part in parts]
            moved = jnp.concatenate([tap_stack(part, LANES) for part in parts], axis=1)
            term = dot_lanes(moved, fine_stack(feature_pieces, column))
            total = term if total is None else total + term
    base = coarse_grad.shape[0]
    grads[:base] = coarse_grad[...]
    grads[base:] = jnp.zeros((grads.shape[0] - base, LANES), grads.dtype)
    base = store_tiles(grads, base, total)
    grad_down = dot_lanes(sorted_act[...], own_ddown)
    rows = grad_down.shape[0] // 2
    grads[base : base + rows] = jnp.concatenate(
        [grad_down[:rows], grad_down[rows:]], axis=1
    ).astype(grads.dtype)


def input_kernel(half, *refs):
    pieces, (weights, out) = refs[:3], refs[3:]
    cells, chans = pieces[0].shape[0], pieces[0].shape[2]
    count = out.shape[0]
    for column in range(count // 2):
        stack = fine_stack(pieces, column, (half[0], cells - count, count))
        products = dot(weights[...], stack)
        for place in range(4):
            total = fold_taps(products[:, place * LANES : (place + 1) * LANES], chans, LANES)
            out[2 * column + place // 2, place % 2] = total.astype(BF16)


def assemble_kernel(fine_scale, coarse_scale, rows, fine, down, coarse):
    def pieces(start, count, width, scale):
        tile = rows[start : start + count].astype(F32) * scale
        return [
            (tile if lane == 0 else pltpu.roll(tile, LANES - lane, 1))[:, :width]
            for lane in range(0, LANES, width)
        ]

    chans, chans3 = fine.shape[1], coarse.shape[1]
    for tile in range(4):
        for h, part in enumerate(pieces(3 * tile * chans3, 3 * chans3, chans3, coarse_scale)):
            for c in range(3):
                coarse[6 * tile + 3 * h + c] = part[c * chans3 : (c + 1) * chans3]
    base = 12 * chans3
    low, high = pieces(base, 3 * chans3 // 2, chans3, coarse_scale)
    coarse[24] = low[:chans3]
    coarse[25] = jnp.concatenate([low[chans3:], high[: chans3 // 2]], axis=0)
    coarse[26] = high[chans3 // 2 :]
    base += 3 * chans3 // 2
    for tile in range(3):
        for h, part in enumerate(pieces(base, 3 * chans, chans, fine_scale)):
            for c in range(3):
                if 4 * tile + h < 9:
                    fine[3 * (4 * tile + h) + c] = part[c * chans : (c + 1) * chans]
        base += 3 * chans
    for last, part in enumerate(pieces(base, 4 * chans, chans3, coarse_scale)):
        for first in range(4):
            down[2 * first + last] = part[first * chans : (first + 1) * chans]


def tap_matrix(weights):
    taps, outs, ins = weights.shape
    return jnp.transpose(weights.reshape(9, 3, outs, ins), (1, 2, 0, 3)).reshape(3 * outs, 9 * ins)


def reversed_taps(weights):
    return jnp.transpose(weights[::-1], (0, 2, 1))


def sort_matrix():
    table = np.zeros((2 * LANES, 2 * LANES), np.float32)
    for sample in range(2):
        for z in range(LANES):
            table[sample * LANES + z, (z % 2) * LANES + sample * (LANES // 2) + z // 2] = 1.0
    return table


def trade(parts, axis, groups=None):
    return lax.all_to_all(
        parts, axis, split_axis=0, concat_axis=0, axis_index_groups=groups, tiled=True
    )


def share(part, axis, groups=None):
    count = lax.axis_size(axis) if groups is None else len(groups[0])
    return trade(jnp.broadcast_to(part[None], (count, *part.shape)), axis, groups)


def turned(block):
    rows, cols = lax.axis_size("grp"), lax.axis_size("sp")
    batch, shift = cols // 2, QUARTERS // 2
    pairs = []
    for row in range(rows):
        major, quarter = divmod((row - shift) % rows, QUARTERS)
        for col in range(cols):
            there = (QUARTERS * (col % batch) + quarter + shift) % rows
            pairs.append((row * cols + col, there * cols + col // batch * batch + major))
    return lax.ppermute(block, ("grp", "sp"), pairs)


def planes():
    rows, cols = lax.axis_size("grp"), lax.axis_size("sp")
    return [
        [row * cols + col for row in range(start, start + 4) for col in range(cols) if col & 2 == far]
        for start in range(0, rows, 4)
        for far in (0, 2)
    ]


def columns():
    rows, cols = lax.axis_size("grp"), lax.axis_size("sp")
    return [
        [row * cols + col + far for row in range(y, rows, 4) for far in (0, 2)]
        for y in range(4)
        for col in range(cols)
        if col & 2 == 0
    ]


def late():
    return (lax.axis_index("grp") % 4 < 2).astype(jnp.int32)


def for_plane(cells):
    lead = cells.shape[0] // 4
    parts = cells.reshape(lead, 2, 2, QUARTERS, 8, LANES)
    parts = jnp.roll(jnp.transpose(parts, (3, 0, 2, 1, 4, 5)), QUARTERS // 2, axis=0)
    blank = jnp.zeros_like(parts)
    low = upper_half() == 0
    both = [jnp.where(low, parts, blank), jnp.where(low, blank, parts)]
    return jnp.concatenate(both, axis=1).reshape(-1, 16, LANES)


def for_column(got):
    lead = lax.axis_size("sp") // 8
    parts = got.reshape(4, 2, lead, 2, 2, 8, LANES)
    parts = jnp.where(upper_half() == 0, parts[:, 0], parts[:, 1])
    parts = jnp.transpose(parts, (1, 2, 3, 0, 4, 5))
    parts = jnp.stack([parts, jnp.zeros_like(parts)], axis=1).reshape(4 * lead, 2, 32, LANES)
    steps = 4 * lead
    shift = 2 * far_side() + late()
    twice = jnp.concatenate([parts, parts], axis=0)
    return lax.dynamic_slice_in_dim(twice, steps - shift, steps, axis=0).reshape(-1, 32, LANES)


def from_column(got):
    parts = got.reshape(-1, 2, 32, LANES)
    steps = parts.shape[0]
    sample = (lax.axis_index("grp") // 4 - late()) % steps
    return jnp.where(sample // 2 % 2 == 0, parts[:, 0], parts[:, 1]).reshape(-1, LANES)


def following(value, other):
    return lax.optimization_barrier((value, other))[0]


def far_side():
    return lax.axis_index("sp") // 2 % 2


def far_exchange(parts):
    near = far_side() == 0
    kept = jnp.where(near, parts[:, 0], parts[:, 1])
    sent = jnp.where(near, parts[:, 1], parts[:, 0])
    got = lax.ppermute(sent, "sp", [(col, col ^ 2) for col in range(lax.axis_size("sp"))])
    return jnp.stack([jnp.where(near, kept, got), jnp.where(near, got, kept)], axis=2)


def near_exchange(parts):
    cols, lead = lax.axis_size("sp"), parts.shape[0]
    groups = [
        [start + 4 * far + core for far in range(lead) for core in (0, 1)]
        for half in range(0, cols, 4 * lead)
        for start in (half, half + 2)
    ]
    return trade(parts.reshape(2 * lead, *parts.shape[2:]), "sp", groups).reshape(parts.shape)


def local(features, weight_fine, weight_down, weight_coarse, cotangent):
    batch, chans, x_cells, y_cells, z_cells = features.shape
    chans3 = weight_down.shape[1]
    rows, cols = lax.axis_size("grp"), lax.axis_size("sp")
    width = batch * z_cells // 2
    extent = batch + reach()
    wider = extent * z_cells // 2
    fine_scale = 1.0 / math.sqrt(batch * x_cells * cols * y_cells * rows * z_cells)
    coarse_scale = 1.0 / math.sqrt(batch * x_cells * cols * y_cells * rows * z_cells // 8)
    shape = jax.ShapeDtypeStruct
    near = planes()
    unit = len(near[0]) * 8
    grad_rows = -(-(27 * chans3 // 2 + 9 * chans + 2 * chans3) // unit) * unit
    half = upper_half().astype(jnp.int32).reshape(1)

    sort = jnp.asarray(sort_matrix(), BF16)
    unsort = jnp.asarray(sort_matrix().T, BF16)
    parted = weight_down.reshape(2, 2, 2, chans3, chans)
    down_matrix = jnp.transpose(parted, (3, 2, 0, 1, 4)).reshape(chans3, 8 * chans)

    halves = [list(range(batch)), list(range(batch, cols))]
    own = trade(jnp.transpose(features, (0, 2, 3, 1, 4)), "sp", halves)
    own = own.reshape(batch * x_cells, y_cells, chans, LANES)

    block = (rows, width // 2 // rows, LANES)
    cells = pl.pallas_call(
        pack_kernel, out_shape=shape((width // 2, LANES), BF16), interpret=INTERPRET
    )(cotangent.reshape(chans3, width))
    cells = turned(cells).reshape(block)
    matrices = [
        tap_matrix(weight_fine),
        tap_matrix(reversed_taps(weight_fine)),
        tap_matrix(weight_coarse),
        tap_matrix(reversed_taps(weight_coarse)),
        down_matrix,
        down_matrix.T,
    ]
    own, cells, *matrices = lax.optimization_barrier((own, cells, *matrices))
    fine_matrix, fine_back, coarse_matrix, coarse_back, down_matrix, up_matrix = matrices
    own = joined(own, arrival(nearest(own, reach() * x_cells), 0, True))
    cells = jnp.roll(trade(cells, "grp"), -(QUARTERS // 2), axis=0).reshape(width // 2, LANES)

    feature_pieces = fine_pieces(own)
    down, sorted_act, slope = call(
        down_kernel,
        (
            shape((chans3, wider), BF16),
            shape((8 * chans, wider), BF16),
            shape((extent, 4 * chans, LANES), F32),
        ),
        half,
        *feature_pieces,
        fine_matrix,
        down_matrix,
        sort,
    )
    cells = following(cells, down)
    upstream = joined(cells, arrival(nearest(cells, reach() * QUARTERS * block[1]), 0, True))
    down_pieces = coarse_pieces(down)
    coarse, dpre3 = call(
        coarse_kernel,
        (shape(upstream.shape, BF16), shape((chans3, wider), BF16)),
        half,
        *down_pieces,
        coarse_matrix,
        upstream,
    )
    coarse_grad = call(
        partial(coarse_grad_kernel, batch),
        shape((27 * chans3 // 2, LANES), BF16),
        half,
        *down_pieces,
        dpre3,
    )
    dpre_pieces = coarse_pieces(dpre3)
    coarse_grad, *dpre_pieces = lax.optimization_barrier((coarse_grad, *dpre_pieces))

    dpre2, grads = call(
        partial(back_kernel, batch),
        (shape(own.shape, BF16), shape((grad_rows, LANES), BF16)),
        half,
        *dpre_pieces,
        *feature_pieces,
        coarse_back,
        up_matrix,
        unsort,
        sorted_act,
        slope,
        coarse_grad,
    )
    coarse = jnp.where(upper_half() == 0, coarse[: width // 2], coarse[-(width // 2) :])
    grads = grads.reshape(len(near[0]), -1, LANES)
    kept = grads.shape[1]
    coarse = for_plane(coarse.reshape(batch, QUARTERS, 8, LANES))
    mixed = trade(jnp.concatenate([grads, coarse], axis=1), ("grp", "sp"), near)
    part = jnp.sum(mixed[:, :kept].astype(F32), axis=0).astype(BF16)
    coarse = for_column(mixed[:, kept:])
    gradient = call(
        input_kernel,
        shape((batch * x_cells, *own.shape[1:]), BF16),
        half,
        *fine_pieces(dpre2),
        fine_back,
    )
    part, gradient, coarse = lax.optimization_barrier((part, gradient, coarse))
    part = jnp.broadcast_to(part[None], (coarse.shape[0], *part.shape))
    mixed = trade(jnp.concatenate([part, coarse], axis=1), ("grp", "sp"), columns())
    part = jnp.sum(mixed[:, :kept].astype(F32), axis=0).astype(BF16)
    coarse = from_column(mixed[:, kept:])
    gradient = following(gradient, part)
    gradient = far_exchange(gradient.reshape(batch // 4, 2, 2, x_cells, y_cells, chans, LANES))
    grads = share(part, ("grp", "sp"), near).reshape(grad_rows, LANES)
    grads, gradient = lax.optimization_barrier((grads, gradient))
    gradient = near_exchange(gradient)
    grad_input = jnp.transpose(gradient, (0, 2, 1, 5, 3, 4, 6)).reshape(features.shape)

    result = pl.pallas_call(
        unpack_kernel, out_shape=shape((chans3, width), BF16), interpret=INTERPRET
    )(coarse)
    result = result.reshape(cotangent.shape)

    grad_fine, grad_down, grad_coarse = pl.pallas_call(
        partial(assemble_kernel, fine_scale, coarse_scale),
        out_shape=(
            shape(weight_fine.shape, F32),
            shape((8, chans, chans3), F32),
            shape(weight_coarse.shape, F32),
        ),
        interpret=INTERPRET,
    )(grads)
    return result, grad_input, grad_fine, jnp.swapaxes(grad_down, 1, 2), grad_coarse


def solution(mesh):
    placed = (P(None, None, "sp", "grp", None), P(), P(), P(), P("grp", None, "sp", None))
    return jax.shard_map(
        local,
        mesh=mesh,
        in_specs=placed,
        out_specs=(P("grp", None, "sp", None), P(None, None, "sp", "grp", None), P(), P(), P()),
        check_vma=False,
    )
```

```python
import math
from functools import partial

import jax
import jax.numpy as jnp
import numpy as np
from jax import lax
from jax.experimental import pallas as pl
from jax.experimental.pallas import tpu as pltpu
from jax.sharding import PartitionSpec as P

QUARTERS = 4
LANES = 128
STEPS = (-1, 0, 1)
F32 = jnp.float32
BF16 = jnp.bfloat16
INTERPRET = False


def call(kernel, outs, half, *operands):
    spaces = [pltpu.SMEM] + [pltpu.VMEM] * len(operands)
    return pl.pallas_call(
        kernel,
        out_shape=outs,
        in_specs=[pl.BlockSpec(memory_space=space) for space in spaces],
        compiler_params=pltpu.CompilerParams(vmem_limit_bytes=28 * 1024 * 1024),
        interpret=INTERPRET,
    )(half, *operands)


def arrival(block, step_y, across):
    rows, cols = lax.axis_size("grp"), lax.axis_size("sp")
    pairs = []
    for row in range(rows):
        for col in range(cols):
            if 0 <= row + step_y < rows:
                source = (col + cols // 2) % cols if across else col
                pairs.append(((row + step_y) * cols + source, row * cols + col))
    return lax.ppermute(block, ("grp", "sp"), pairs)


def upper_half():
    return lax.axis_index("sp") // (lax.axis_size("sp") // 2)


def reach():
    return min(4, lax.axis_size("sp") // 2)


def joined(own, other):
    low = jnp.concatenate([own, other], axis=0)
    return jnp.where(upper_half() == 0, low, jnp.concatenate([other, own], axis=0))


def nearest(block, count):
    return jnp.where(upper_half() == 0, block[-count:], block[:count])


def fine_pieces(block):
    return [block, arrival(block[:, 1:], -1, False), arrival(block[:, :1], 1, False)]


def coarse_pieces(block):
    return [block, arrival(block, -1, False), arrival(block, 1, False)]


def silu_slope(values, sigma):
    return sigma * (1.0 + values * (1.0 - sigma))


def dot(left, right):
    return lax.dot_general(left, right, (((1,), (0,)), ((), ())), preferred_element_type=F32)


def dot_lanes(left, right):
    return lax.dot_general(left, right, (((1,), (1,)), ((), ())), preferred_element_type=F32)


def shifted(values, step, span):
    if step == 0:
        return values
    place = lax.broadcasted_iota(jnp.int32, values.shape, 1) % span
    width = values.shape[1]
    moved = pltpu.roll(values, (-step) % width, 1)
    return jnp.where(place == (span - 1 if step > 0 else 0), 0.0, moved)


def fold_taps(products, chans, span):
    total = products[chans : 2 * chans]
    total = total + shifted(products[:chans], -1, span)
    return total + shifted(products[2 * chans :], 1, span)


def fine_stack(refs, column, shift=None):
    center, before, after = refs
    cells = center.shape[0]

    def cell(x, y):
        inside = None
        if shift is not None:
            half, skip, count = shift
            inside = half == 1 if x < 0 else half == 0 if x >= count else None
            x = jnp.clip(x + skip * half, 0, cells - 1)
        elif not 0 <= x < cells:
            return jnp.zeros(center.shape[2:], center.dtype)
        value = before[x, 0] if y < 0 else after[x, 0] if y > 1 else center[x, y]
        return value if inside is None else jnp.where(inside, value, jnp.zeros_like(value))

    return jnp.concatenate(
        [
            jnp.concatenate(
                [cell(2 * column + x + a, y + b) for x in (0, 1) for y in (0, 1)], axis=1
            )
            for a in STEPS
            for b in STEPS
        ],
        axis=0,
    )


def coarse_stack(refs):
    tiles = refs[0].shape[1] // LANES
    low = lax.broadcasted_iota(jnp.int32, (refs[0].shape[0], LANES), 1) < LANES // 2
    lined = []
    for ref in (refs[1], refs[0], refs[2]):
        own = [ref[:, tile * LANES : (tile + 1) * LANES] for tile in range(tiles)]
        first = jnp.where(low, own[-1].astype(F32), 0.0)
        last = jnp.where(low, 0.0, own[0].astype(F32))
        first, last = [pltpu.roll(tile, LANES // 2, 1).astype(BF16) for tile in (first, last)]
        lined.append([first, *own, last])
    return jnp.concatenate(
        [jnp.concatenate(lined[b][a : a + tiles], axis=1) for a in range(3) for b in range(3)],
        axis=0,
    )


def own_lanes(half, extent, shape):
    lane = lax.broadcasted_iota(jnp.int32, shape, 1)
    tiles = shape[1] // LANES
    x = lane // LANES + tiles * (lane % LANES // (LANES // 2)) - (2 * tiles - extent) * half
    return (x >= 0) & (x < extent)


def down_kernel(half, *refs):
    pieces, (weights, down_weights, sort, down, sorted_act, slope) = refs[:3], refs[3:]
    columns, chans = pieces[0].shape[0] // 2, pieces[0].shape[2]
    for tile in range(columns // 2):
        acts = []
        for column in (tile, tile + columns // 2):
            products = dot(weights[...], fine_stack(pieces, column))
            parts = []
            for place in range(4):
                pre = fold_taps(products[:, place * LANES : (place + 1) * LANES], chans, LANES)
                sigma = jax.nn.sigmoid(pre)
                slope[column, place * chans : (place + 1) * chans] = silu_slope(pre, sigma)
                parts.append((pre * sigma).astype(BF16))
            acts.append(jnp.concatenate(parts, axis=0))
        parted = dot(jnp.concatenate(acts, axis=1), sort[...]).astype(BF16)
        stacked = jnp.concatenate([parted[:, :LANES], parted[:, LANES:]], axis=0)
        lanes = slice(tile * LANES, (tile + 1) * LANES)
        sorted_act[:, lanes] = stacked
        down[:, lanes] = dot(down_weights[...], stacked).astype(BF16)


def coarse_kernel(half, *refs):
    pieces, (weights, upstream, out, dpre) = refs[:3], refs[3:]
    chans, width = pieces[0].shape
    pre = fold_taps(dot(weights[...], coarse_stack(pieces)), chans, LANES // 2)
    sigma = jax.nn.sigmoid(pre)
    act = pre * sigma
    slope = silu_slope(pre, sigma)
    tiles = width // LANES
    rows = LANES // 4
    for tile in range(tiles):
        lanes = slice(tile * LANES, (tile + 1) * LANES)
        ends = [tile * rows, (tile + tiles) * rows]
        packed = jnp.concatenate([upstream[end : end + rows] for end in ends], axis=0)
        dpre[:, lanes] = (unpacked(packed.astype(F32)) * slope[:, lanes]).astype(BF16)
        both = packed_cells(act[:, lanes]).astype(BF16)
        for member, end in enumerate(ends):
            out[end : end + rows] = both[member * rows : (member + 1) * rows]


def packed_cells(values):
    turned = jnp.concatenate([values, values], axis=0).T.reshape(LANES // 16, 2, 8, LANES)
    low = lax.broadcasted_iota(jnp.int32, (LANES // 16, 8, LANES), 2) < LANES // 2
    return jnp.where(low, turned[:, 0], turned[:, 1]).reshape(LANES // 2, LANES)


def unpacked(values):
    first = values.reshape(LANES // 16, 1, 8, LANES)
    second = pltpu.roll(values, LANES // 2, 1).reshape(LANES // 16, 1, 8, LANES)
    turned = jnp.concatenate([first, second], axis=1).reshape(LANES, LANES).T
    return turned[: LANES // 2]


def pack_kernel(values, out):
    for tile in range(values.shape[1] // LANES):
        part = values[:, tile * LANES : (tile + 1) * LANES].astype(F32)
        out[tile * LANES // 2 : (tile + 1) * LANES // 2] = packed_cells(part).astype(BF16)


def unpack_kernel(values, out):
    for tile in range(out.shape[1] // LANES):
        part = values[tile * LANES // 2 : (tile + 1) * LANES // 2].astype(F32)
        out[:, tile * LANES : (tile + 1) * LANES] = unpacked(part).astype(BF16)


def tap_stack(values, span):
    values = values.astype(F32)
    return jnp.concatenate([shifted(values, -step, span).astype(BF16) for step in STEPS], axis=0)


def store_tiles(ref, base, values):
    rows, cols = values.shape
    for start in range(0, cols, LANES):
        width = min(LANES, cols - start)
        ref[base : base + rows, :width] = values[:, start : start + width].astype(ref.dtype)
        base += rows
    return base


def coarse_grad_kernel(extent, half, *refs):
    pieces, (dpre, grad) = refs[:3], refs[3:]
    own = jnp.where(own_lanes(half[0], extent, dpre.shape), dpre[...].astype(F32), 0.0)
    products = dot_lanes(tap_stack(own, LANES // 2), coarse_stack(pieces))
    rows, cols = products.shape
    base = store_tiles(grad, 0, products[:, : cols - LANES // 2])
    last = products[:, cols - LANES // 2 :]
    grad[base:] = jnp.concatenate([last[: rows // 2], last[rows // 2 :]], axis=1).astype(grad.dtype)


def back_kernel(extent, half, *refs):
    pieces, feature_pieces = refs[:3], refs[3:6]
    weights, up_weights, unsort, sorted_act, slope, coarse_grad, dpre2, grads = refs[6:]
    chans3 = pieces[0].shape[0]
    columns, chans = feature_pieces[0].shape[0] // 2, feature_pieces[0].shape[2]
    ddown = fold_taps(dot(weights[...], coarse_stack(pieces)), chans3, LANES // 2)
    own_ddown = jnp.where(own_lanes(half[0], extent, ddown.shape), ddown, 0.0).astype(BF16)
    ddown = ddown.astype(BF16)
    spread = dot(up_weights[...], ddown).astype(BF16)
    rows = spread.shape[0] // 2
    total = None
    for tile in range(columns // 2):
        lanes = slice(tile * LANES, (tile + 1) * LANES)
        both = dot(jnp.concatenate([spread[:rows, lanes], spread[rows:, lanes]], axis=1), unsort[...])
        for member in range(2):
            column = tile + member * (columns // 2)
            dpre = both[:, member * LANES : (member + 1) * LANES] * slope[column]
            dpre = dpre.astype(BF16)
            parts = [dpre[place * chans : (place + 1) * chans] for place in range(4)]
            for place in range(4):
                dpre2[2 * column + place // 2, place % 2] = parts[place]
            place = column - (columns - extent) * half[0]
            inside = (place >= 0) & (place < extent)
            parts = [jnp.where(inside, part.astype(F32), 0.0) for part in parts]
            moved = jnp.concatenate([tap_stack(part, LANES) for part in parts], axis=1)
            term = dot_lanes(moved, fine_stack(feature_pieces, column))
            total = term if total is None else total + term
    base = coarse_grad.shape[0]
    grads[:base] = coarse_grad[...]
    grads[base:] = jnp.zeros((grads.shape[0] - base, LANES), grads.dtype)
    base = store_tiles(grads, base, total)
    grad_down = dot_lanes(sorted_act[...], own_ddown)
    rows = grad_down.shape[0] // 2
    grads[base : base + rows] = jnp.concatenate(
        [grad_down[:rows], grad_down[rows:]], axis=1
    ).astype(grads.dtype)


def input_kernel(half, *refs):
    pieces, (weights, out) = refs[:3], refs[3:]
    cells, chans = pieces[0].shape[0], pieces[0].shape[2]
    count = out.shape[0]
    for column in range(count // 2):
        stack = fine_stack(pieces, column, (half[0], cells - count, count))
        products = dot(weights[...], stack)
        for place in range(4):
            total = fold_taps(products[:, place * LANES : (place + 1) * LANES], chans, LANES)
            out[2 * column + place // 2, place % 2] = total.astype(BF16)


def assemble_kernel(fine_scale, coarse_scale, rows, fine, down, coarse):
    def pieces(start, count, width, scale):
        tile = rows[start : start + count].astype(F32) * scale
        return [
            (tile if lane == 0 else pltpu.roll(tile, LANES - lane, 1))[:, :width]
            for lane in range(0, LANES, width)
        ]

    chans, chans3 = fine.shape[1], coarse.shape[1]
    for tile in range(4):
        for h, part in enumerate(pieces(3 * tile * chans3, 3 * chans3, chans3, coarse_scale)):
            for c in range(3):
                coarse[6 * tile + 3 * h + c] = part[c * chans3 : (c + 1) * chans3]
    base = 12 * chans3
    low, high = pieces(base, 3 * chans3 // 2, chans3, coarse_scale)
    coarse[24] = low[:chans3]
    coarse[25] = jnp.concatenate([low[chans3:], high[: chans3 // 2]], axis=0)
    coarse[26] = high[chans3 // 2 :]
    base += 3 * chans3 // 2
    for tile in range(3):
        for h, part in enumerate(pieces(base, 3 * chans, chans, fine_scale)):
            for c in range(3):
                if 4 * tile + h < 9:
                    fine[3 * (4 * tile + h) + c] = part[c * chans : (c + 1) * chans]
        base += 3 * chans
    for last, part in enumerate(pieces(base, 4 * chans, chans3, coarse_scale)):
        for first in range(4):
            down[2 * first + last] = part[first * chans : (first + 1) * chans]


def tap_matrix(weights):
    taps, outs, ins = weights.shape
    return jnp.transpose(weights.reshape(9, 3, outs, ins), (1, 2, 0, 3)).reshape(3 * outs, 9 * ins)


def reversed_taps(weights):
    return jnp.transpose(weights[::-1], (0, 2, 1))


def sort_matrix():
    table = np.zeros((2 * LANES, 2 * LANES), np.float32)
    for sample in range(2):
        for z in range(LANES):
            table[sample * LANES + z, (z % 2) * LANES + sample * (LANES // 2) + z // 2] = 1.0
    return table


def trade(parts, axis, groups=None):
    return lax.all_to_all(
        parts, axis, split_axis=0, concat_axis=0, axis_index_groups=groups, tiled=True
    )


def share(part, axis, groups=None):
    count = lax.axis_size(axis) if groups is None else len(groups[0])
    return trade(jnp.broadcast_to(part[None], (count, *part.shape)), axis, groups)


def turned(block):
    rows, cols = lax.axis_size("grp"), lax.axis_size("sp")
    batch, shift = cols // 2, QUARTERS // 2
    pairs = []
    for row in range(rows):
        major, quarter = divmod((row - shift) % rows, QUARTERS)
        for col in range(cols):
            there = (QUARTERS * (col % batch) + quarter + shift) % rows
            pairs.append((row * cols + col, there * cols + col // batch * batch + major))
    return lax.ppermute(block, ("grp", "sp"), pairs)


def planes():
    rows, cols = lax.axis_size("grp"), lax.axis_size("sp")
    return [
        [row * cols + col for row in range(start, start + 4) for col in range(cols) if col & 2 == far]
        for start in range(0, rows, 4)
        for far in (0, 2)
    ]


def columns():
    rows, cols = lax.axis_size("grp"), lax.axis_size("sp")
    return [
        [row * cols + col + far for row in range(y, rows, 4) for far in (0, 2)]
        for y in range(4)
        for col in range(cols)
        if col & 2 == 0
    ]


def late():
    return (lax.axis_index("grp") % 4 < 2).astype(jnp.int32)


def for_plane(cells):
    lead = cells.shape[0] // 4
    parts = cells.reshape(lead, 2, 2, QUARTERS, 8, LANES)
    parts = jnp.roll(jnp.transpose(parts, (3, 0, 2, 1, 4, 5)), QUARTERS // 2, axis=0)
    blank = jnp.zeros_like(parts)
    low = upper_half() == 0
    both = [jnp.where(low, parts, blank), jnp.where(low, blank, parts)]
    return jnp.concatenate(both, axis=1).reshape(-1, 16, LANES)


def for_column(got):
    lead = lax.axis_size("sp") // 8
    parts = got.reshape(4, 2, lead, 2, 2, 8, LANES)
    parts = jnp.where(upper_half() == 0, parts[:, 0], parts[:, 1])
    parts = jnp.transpose(parts, (1, 2, 3, 0, 4, 5))
    parts = jnp.stack([parts, jnp.zeros_like(parts)], axis=1).reshape(4 * lead, 2, 32, LANES)
    steps = 4 * lead
    shift = 2 * far_side() + late()
    twice = jnp.concatenate([parts, parts], axis=0)
    return lax.dynamic_slice_in_dim(twice, steps - shift, steps, axis=0).reshape(-1, 32, LANES)


def from_column(got):
    parts = got.reshape(-1, 2, 32, LANES)
    steps = parts.shape[0]
    sample = (lax.axis_index("grp") // 4 - late()) % steps
    return jnp.where(sample // 2 % 2 == 0, parts[:, 0], parts[:, 1]).reshape(-1, LANES)


def far_side():
    return lax.axis_index("sp") // 2 % 2


def matched(parts, far, core):
    if parts.shape[0] > 1:
        parts = jnp.where(far == 0, parts, parts[::-1])
    return jnp.where(core == 0, parts, parts[:, ::-1])


def near_exchange(parts):
    cols, lead = lax.axis_size("sp"), parts.shape[0]
    place = lax.axis_index("sp")
    far, core = place // 4 % lead, place % 2
    parts = matched(parts, far, core)
    got = [
        [
            parts[x, c]
            if x == c == 0
            else lax.ppermute(parts[x, c], "sp", [(col, col ^ (4 * x + c)) for col in range(cols)])
            for c in (0, 1)
        ]
        for x in range(lead)
    ]
    return matched(jnp.stack([jnp.stack(row) for row in got]), far, core)


def far_exchange(parts):
    near = far_side() == 0
    kept = jnp.where(near, parts[:, :, 0], parts[:, :, 1])
    sent = jnp.where(near, parts[:, :, 1], parts[:, :, 0])
    got = lax.ppermute(sent, "sp", [(col, col ^ 2) for col in range(lax.axis_size("sp"))])
    return jnp.stack([jnp.where(near, kept, got), jnp.where(near, got, kept)], axis=2)


def local(features, weight_fine, weight_down, weight_coarse, cotangent):
    batch, chans, x_cells, y_cells, z_cells = features.shape
    chans3 = weight_down.shape[1]
    rows, cols = lax.axis_size("grp"), lax.axis_size("sp")
    width = batch * z_cells // 2
    extent = batch + reach()
    wider = extent * z_cells // 2
    fine_scale = 1.0 / math.sqrt(batch * x_cells * cols * y_cells * rows * z_cells)
    coarse_scale = 1.0 / math.sqrt(batch * x_cells * cols * y_cells * rows * z_cells // 8)
    shape = jax.ShapeDtypeStruct
    near = planes()
    unit = len(near[0]) * 8
    grad_rows = -(-(27 * chans3 // 2 + 9 * chans + 2 * chans3) // unit) * unit
    half = upper_half().astype(jnp.int32).reshape(1)

    sort = jnp.asarray(sort_matrix(), BF16)
    unsort = jnp.asarray(sort_matrix().T, BF16)
    parted = weight_down.reshape(2, 2, 2, chans3, chans)
    down_matrix = jnp.transpose(parted, (3, 2, 0, 1, 4)).reshape(chans3, 8 * chans)

    halves = [list(range(batch)), list(range(batch, cols))]
    own = trade(jnp.transpose(features, (0, 2, 3, 1, 4)), "sp", halves)
    own = own.reshape(batch * x_cells, y_cells, chans, LANES)

    block = (rows, width // 2 // rows, LANES)
    cells = pl.pallas_call(
        pack_kernel, out_shape=shape((width // 2, LANES), BF16), interpret=INTERPRET
    )(cotangent.reshape(chans3, width))
    cells = turned(cells).reshape(block)
    matrices = [
        tap_matrix(weight_fine),
        tap_matrix(reversed_taps(weight_fine)),
        tap_matrix(weight_coarse),
        tap_matrix(reversed_taps(weight_coarse)),
        down_matrix,
        down_matrix.T,
    ]
    own, cells, *matrices = lax.optimization_barrier((own, cells, *matrices))
    fine_matrix, fine_back, coarse_matrix, coarse_back, down_matrix, up_matrix = matrices
    own = joined(own, arrival(nearest(own, reach() * x_cells), 0, True))
    cells = jnp.roll(trade(cells, "grp"), -(QUARTERS // 2), axis=0).reshape(width // 2, LANES)
    upstream = joined(cells, arrival(nearest(cells, reach() * QUARTERS * block[1]), 0, True))

    feature_pieces = fine_pieces(own)
    down, sorted_act, slope = call(
        down_kernel,
        (
            shape((chans3, wider), BF16),
            shape((8 * chans, wider), BF16),
            shape((extent, 4 * chans, LANES), F32),
        ),
        half,
        *feature_pieces,
        fine_matrix,
        down_matrix,
        sort,
    )
    down_pieces = coarse_pieces(down)
    coarse, dpre3 = call(
        coarse_kernel,
        (shape(upstream.shape, BF16), shape((chans3, wider), BF16)),
        half,
        *down_pieces,
        coarse_matrix,
        upstream,
    )
    coarse_grad = call(
        partial(coarse_grad_kernel, batch),
        shape((27 * chans3 // 2, LANES), BF16),
        half,
        *down_pieces,
        dpre3,
    )
    dpre_pieces = coarse_pieces(dpre3)
    coarse_grad, *dpre_pieces = lax.optimization_barrier((coarse_grad, *dpre_pieces))

    dpre2, grads = call(
        partial(back_kernel, batch),
        (shape(own.shape, BF16), shape((grad_rows, LANES), BF16)),
        half,
        *dpre_pieces,
        *feature_pieces,
        coarse_back,
        up_matrix,
        unsort,
        sorted_act,
        slope,
        coarse_grad,
    )
    coarse = jnp.where(upper_half() == 0, coarse[: width // 2], coarse[-(width // 2) :])
    grads = grads.reshape(len(near[0]), -1, LANES)
    kept = grads.shape[1]
    coarse = for_plane(coarse.reshape(batch, QUARTERS, 8, LANES))
    mixed = trade(jnp.concatenate([grads, coarse], axis=1), ("grp", "sp"), near)
    part = jnp.sum(mixed[:, :kept].astype(F32), axis=0).astype(BF16)
    coarse = for_column(mixed[:, kept:])
    spread = fine_pieces(dpre2)
    part, coarse, *spread[1:] = lax.optimization_barrier((part, coarse, *spread[1:]))
    gradient = call(
        input_kernel,
        shape((batch * x_cells, *own.shape[1:]), BF16),
        half,
        *spread,
        fine_back,
    )
    gradient = gradient.reshape(batch // 4, 2, 2, x_cells, y_cells, chans, LANES)
    gradient = far_exchange(near_exchange(jnp.swapaxes(gradient, 1, 2)))
    part = jnp.broadcast_to(part[None], (coarse.shape[0], *part.shape))
    mixed = trade(jnp.concatenate([part, coarse], axis=1), ("grp", "sp"), columns())
    part = jnp.sum(mixed[:, :kept].astype(F32), axis=0).astype(BF16)
    coarse = from_column(mixed[:, kept:])
    grads = share(part, ("grp", "sp"), near).reshape(grad_rows, LANES)
    grads, gradient = lax.optimization_barrier((grads, gradient))
    grad_input = jnp.transpose(gradient, (0, 2, 1, 5, 3, 4, 6)).reshape(features.shape)

    result = pl.pallas_call(
        unpack_kernel, out_shape=shape((chans3, width), BF16), interpret=INTERPRET
    )(coarse)
    result = result.reshape(cotangent.shape)

    grad_fine, grad_down, grad_coarse = pl.pallas_call(
        partial(assemble_kernel, fine_scale, coarse_scale),
        out_shape=(
            shape(weight_fine.shape, F32),
            shape((8, chans, chans3), F32),
            shape(weight_coarse.shape, F32),
        ),
        interpret=INTERPRET,
    )(grads)
    return result, grad_input, grad_fine, jnp.swapaxes(grad_down, 1, 2), grad_coarse


def solution(mesh):
    placed = (P(None, None, "sp", "grp", None), P(), P(), P(), P("grp", None, "sp", None))
    return jax.shard_map(
        local,
        mesh=mesh,
        in_specs=placed,
        out_specs=(P("grp", None, "sp", None), P(None, None, "sp", "grp", None), P(), P(), P()),
        check_vma=False,
    )
```

```python
import math
from functools import partial

import jax
import jax.numpy as jnp
import numpy as np
from jax import lax
from jax.experimental import pallas as pl
from jax.experimental.pallas import tpu as pltpu
from jax.sharding import PartitionSpec as P

QUARTERS = 4
LANES = 128
STEPS = (-1, 0, 1)
F32 = jnp.float32
BF16 = jnp.bfloat16
INTERPRET = False


def call(kernel, outs, half, *operands):
    spaces = [pltpu.SMEM] + [pltpu.VMEM] * len(operands)
    return pl.pallas_call(
        kernel,
        out_shape=outs,
        in_specs=[pl.BlockSpec(memory_space=space) for space in spaces],
        compiler_params=pltpu.CompilerParams(vmem_limit_bytes=28 * 1024 * 1024),
        interpret=INTERPRET,
    )(half, *operands)


def arrival(block, step_y, across):
    rows, cols = lax.axis_size("grp"), lax.axis_size("sp")
    pairs = []
    for row in range(rows):
        for col in range(cols):
            if 0 <= row + step_y < rows:
                source = (col + cols // 2) % cols if across else col
                pairs.append(((row + step_y) * cols + source, row * cols + col))
    return lax.ppermute(block, ("grp", "sp"), pairs)


def upper_half():
    return lax.axis_index("sp") // (lax.axis_size("sp") // 2)


def reach():
    return min(4, lax.axis_size("sp") // 2)


def joined(own, other):
    low = jnp.concatenate([own, other], axis=0)
    return jnp.where(upper_half() == 0, low, jnp.concatenate([other, own], axis=0))


def nearest(block, count):
    return jnp.where(upper_half() == 0, block[-count:], block[:count])


def fine_pieces(block):
    return [block, arrival(block[:, 1:], -1, False), arrival(block[:, :1], 1, False)]


def last_pieces(block, count):
    there = jnp.where(upper_half() == 0, block[: count + 1], block[-(count + 1) :])
    return [block, arrival(there[:, 1:], -1, False), arrival(there[:, :1], 1, False)]


def coarse_pieces(block):
    return [block, arrival(block, -1, False), arrival(block, 1, False)]


def silu_slope(values, sigma):
    return sigma * (1.0 + values * (1.0 - sigma))


def dot(left, right):
    return lax.dot_general(left, right, (((1,), (0,)), ((), ())), preferred_element_type=F32)


def dot_lanes(left, right):
    return lax.dot_general(left, right, (((1,), (1,)), ((), ())), preferred_element_type=F32)


def shifted(values, step, span):
    if step == 0:
        return values
    place = lax.broadcasted_iota(jnp.int32, values.shape, 1) % span
    width = values.shape[1]
    moved = pltpu.roll(values, (-step) % width, 1)
    return jnp.where(place == (span - 1 if step > 0 else 0), 0.0, moved)


def fold_taps(products, chans, span):
    total = products[chans : 2 * chans]
    total = total + shifted(products[:chans], -1, span)
    return total + shifted(products[2 * chans :], 1, span)


def fine_stack(refs, column, shift=None):
    center, before, after = refs
    cells = center.shape[0]

    def cell(x, y):
        inside = None
        if shift is not None:
            half, skip, count = shift
            inside = half == 1 if x < 0 else half == 0 if x >= count else None
            lag = 0 if before.shape[0] == cells else skip - 1
            beside = jnp.clip(x + (skip - lag) * half, 0, before.shape[0] - 1)
            x = jnp.clip(x + skip * half, 0, cells - 1)
        elif not 0 <= x < cells:
            return jnp.zeros(center.shape[2:], center.dtype)
        else:
            beside = x
        value = before[beside, 0] if y < 0 else after[beside, 0] if y > 1 else center[x, y]
        return value if inside is None else jnp.where(inside, value, jnp.zeros_like(value))

    return jnp.concatenate(
        [
            jnp.concatenate(
                [cell(2 * column + x + a, y + b) for x in (0, 1) for y in (0, 1)], axis=1
            )
            for a in STEPS
            for b in STEPS
        ],
        axis=0,
    )


def coarse_stack(refs):
    tiles = refs[0].shape[1] // LANES
    low = lax.broadcasted_iota(jnp.int32, (refs[0].shape[0], LANES), 1) < LANES // 2
    lined = []
    for ref in (refs[1], refs[0], refs[2]):
        own = [ref[:, tile * LANES : (tile + 1) * LANES] for tile in range(tiles)]
        first = jnp.where(low, own[-1].astype(F32), 0.0)
        last = jnp.where(low, 0.0, own[0].astype(F32))
        first, last = [pltpu.roll(tile, LANES // 2, 1).astype(BF16) for tile in (first, last)]
        lined.append([first, *own, last])
    return jnp.concatenate(
        [jnp.concatenate(lined[b][a : a + tiles], axis=1) for a in range(3) for b in range(3)],
        axis=0,
    )


def own_lanes(half, extent, shape):
    lane = lax.broadcasted_iota(jnp.int32, shape, 1)
    tiles = shape[1] // LANES
    x = lane // LANES + tiles * (lane % LANES // (LANES // 2)) - (2 * tiles - extent) * half
    return (x >= 0) & (x < extent)


def down_kernel(half, *refs):
    pieces, (weights, down_weights, sort, down, sorted_act, slope) = refs[:3], refs[3:]
    columns, chans = pieces[0].shape[0] // 2, pieces[0].shape[2]
    for tile in range(columns // 2):
        acts = []
        for column in (tile, tile + columns // 2):
            products = dot(weights[...], fine_stack(pieces, column))
            parts = []
            for place in range(4):
                pre = fold_taps(products[:, place * LANES : (place + 1) * LANES], chans, LANES)
                sigma = jax.nn.sigmoid(pre)
                slope[column, place * chans : (place + 1) * chans] = silu_slope(pre, sigma)
                parts.append((pre * sigma).astype(BF16))
            acts.append(jnp.concatenate(parts, axis=0))
        parted = dot(jnp.concatenate(acts, axis=1), sort[...]).astype(BF16)
        stacked = jnp.concatenate([parted[:, :LANES], parted[:, LANES:]], axis=0)
        lanes = slice(tile * LANES, (tile + 1) * LANES)
        sorted_act[:, lanes] = stacked
        down[:, lanes] = dot(down_weights[...], stacked).astype(BF16)


def coarse_kernel(half, *refs):
    pieces, (weights, upstream, out, dpre) = refs[:3], refs[3:]
    chans, width = pieces[0].shape
    pre = fold_taps(dot(weights[...], coarse_stack(pieces)), chans, LANES // 2)
    sigma = jax.nn.sigmoid(pre)
    act = pre * sigma
    slope = silu_slope(pre, sigma)
    tiles = width // LANES
    rows = LANES // 4
    for tile in range(tiles):
        lanes = slice(tile * LANES, (tile + 1) * LANES)
        ends = [tile * rows, (tile + tiles) * rows]
        packed = jnp.concatenate([upstream[end : end + rows] for end in ends], axis=0)
        dpre[:, lanes] = (unpacked(packed.astype(F32)) * slope[:, lanes]).astype(BF16)
        both = packed_cells(act[:, lanes]).astype(BF16)
        for member, end in enumerate(ends):
            out[end : end + rows] = both[member * rows : (member + 1) * rows]


def packed_cells(values):
    turned = jnp.concatenate([values, values], axis=0).T.reshape(LANES // 16, 2, 8, LANES)
    low = lax.broadcasted_iota(jnp.int32, (LANES // 16, 8, LANES), 2) < LANES // 2
    return jnp.where(low, turned[:, 0], turned[:, 1]).reshape(LANES // 2, LANES)


def unpacked(values):
    first = values.reshape(LANES // 16, 1, 8, LANES)
    second = pltpu.roll(values, LANES // 2, 1).reshape(LANES // 16, 1, 8, LANES)
    turned = jnp.concatenate([first, second], axis=1).reshape(LANES, LANES).T
    return turned[: LANES // 2]


def pack_kernel(values, out):
    for tile in range(values.shape[1] // LANES):
        part = values[:, tile * LANES : (tile + 1) * LANES].astype(F32)
        out[tile * LANES // 2 : (tile + 1) * LANES // 2] = packed_cells(part).astype(BF16)


def unpack_kernel(values, out):
    for tile in range(out.shape[1] // LANES):
        part = values[tile * LANES // 2 : (tile + 1) * LANES // 2].astype(F32)
        out[:, tile * LANES : (tile + 1) * LANES] = unpacked(part).astype(BF16)


def tap_stack(values, span):
    values = values.astype(F32)
    return jnp.concatenate([shifted(values, -step, span).astype(BF16) for step in STEPS], axis=0)


def store_tiles(ref, base, values):
    rows, cols = values.shape
    for start in range(0, cols, LANES):
        width = min(LANES, cols - start)
        ref[base : base + rows, :width] = values[:, start : start + width].astype(ref.dtype)
        base += rows
    return base


def coarse_grad_kernel(extent, half, *refs):
    pieces, (dpre, grad) = refs[:3], refs[3:]
    own = jnp.where(own_lanes(half[0], extent, dpre.shape), dpre[...].astype(F32), 0.0)
    products = dot_lanes(tap_stack(own, LANES // 2), coarse_stack(pieces))
    rows, cols = products.shape
    base = store_tiles(grad, 0, products[:, : cols - LANES // 2])
    last = products[:, cols - LANES // 2 :]
    grad[base:] = jnp.concatenate([last[: rows // 2], last[rows // 2 :]], axis=1).astype(grad.dtype)


def back_kernel(extent, half, *refs):
    pieces, feature_pieces = refs[:3], refs[3:6]
    weights, up_weights, unsort, sorted_act, slope, coarse_grad, dpre2, grads = refs[6:]
    chans3 = pieces[0].shape[0]
    columns, chans = feature_pieces[0].shape[0] // 2, feature_pieces[0].shape[2]
    ddown = fold_taps(dot(weights[...], coarse_stack(pieces)), chans3, LANES // 2)
    own_ddown = jnp.where(own_lanes(half[0], extent, ddown.shape), ddown, 0.0).astype(BF16)
    ddown = ddown.astype(BF16)
    spread = dot(up_weights[...], ddown).astype(BF16)
    rows = spread.shape[0] // 2
    for tile in range(columns // 2):
        lanes = slice(tile * LANES, (tile + 1) * LANES)
        both = dot(jnp.concatenate([spread[:rows, lanes], spread[rows:, lanes]], axis=1), unsort[...])
        for member in range(2):
            column = tile + member * (columns // 2)
            dpre = both[:, member * LANES : (member + 1) * LANES] * slope[column]
            dpre = dpre.astype(BF16)
            parts = [dpre[place * chans : (place + 1) * chans] for place in range(4)]
            for place in range(4):
                dpre2[2 * column + place // 2, place % 2] = parts[place]
    total = None
    skip = columns - extent
    for place in range(extent):
        column = place + skip * half[0]
        parts = [dpre2[2 * column + x, y] for x in (0, 1) for y in (0, 1)]
        moved = jnp.concatenate([tap_stack(part, LANES) for part in parts], axis=1)
        stack = fine_stack(feature_pieces, place, (half[0], 2 * skip, 2 * extent))
        term = dot_lanes(moved, stack)
        total = term if total is None else total + term
    base = coarse_grad.shape[0]
    grads[:base] = coarse_grad[...]
    grads[base:] = jnp.zeros((grads.shape[0] - base, LANES), grads.dtype)
    base = store_tiles(grads, base, total)
    grad_down = dot_lanes(sorted_act[...], own_ddown)
    rows = grad_down.shape[0] // 2
    grads[base : base + rows] = jnp.concatenate(
        [grad_down[:rows], grad_down[rows:]], axis=1
    ).astype(grads.dtype)


def input_kernel(half, *refs):
    pieces, (weights, out) = refs[:3], refs[3:]
    cells, chans = pieces[0].shape[0], pieces[0].shape[2]
    count = out.shape[0]
    for column in range(count // 2):
        stack = fine_stack(pieces, column, (half[0], cells - count, count))
        products = dot(weights[...], stack)
        for place in range(4):
            total = fold_taps(products[:, place * LANES : (place + 1) * LANES], chans, LANES)
            out[2 * column + place // 2, place % 2] = total.astype(BF16)


def assemble_kernel(fine_scale, coarse_scale, rows, fine, down, coarse):
    def pieces(start, count, width, scale):
        tile = rows[start : start + count].astype(F32) * scale
        return [
            (tile if lane == 0 else pltpu.roll(tile, LANES - lane, 1))[:, :width]
            for lane in range(0, LANES, width)
        ]

    chans, chans3 = fine.shape[1], coarse.shape[1]
    for tile in range(4):
        for h, part in enumerate(pieces(3 * tile * chans3, 3 * chans3, chans3, coarse_scale)):
            for c in range(3):
                coarse[6 * tile + 3 * h + c] = part[c * chans3 : (c + 1) * chans3]
    base = 12 * chans3
    low, high = pieces(base, 3 * chans3 // 2, chans3, coarse_scale)
    coarse[24] = low[:chans3]
    coarse[25] = jnp.concatenate([low[chans3:], high[: chans3 // 2]], axis=0)
    coarse[26] = high[chans3 // 2 :]
    base += 3 * chans3 // 2
    for tile in range(3):
        for h, part in enumerate(pieces(base, 3 * chans, chans, fine_scale)):
            for c in range(3):
                if 4 * tile + h < 9:
                    fine[3 * (4 * tile + h) + c] = part[c * chans : (c + 1) * chans]
        base += 3 * chans
    for last, part in enumerate(pieces(base, 4 * chans, chans3, coarse_scale)):
        for first in range(4):
            down[2 * first + last] = part[first * chans : (first + 1) * chans]


def tap_matrix(weights):
    taps, outs, ins = weights.shape
    return jnp.transpose(weights.reshape(9, 3, outs, ins), (1, 2, 0, 3)).reshape(3 * outs, 9 * ins)


def reversed_taps(weights):
    return jnp.transpose(weights[::-1], (0, 2, 1))


def sort_matrix():
    table = np.zeros((2 * LANES, 2 * LANES), np.float32)
    for sample in range(2):
        for z in range(LANES):
            table[sample * LANES + z, (z % 2) * LANES + sample * (LANES // 2) + z // 2] = 1.0
    return table


def trade(parts, axis, groups=None):
    return lax.all_to_all(
        parts, axis, split_axis=0, concat_axis=0, axis_index_groups=groups, tiled=True
    )


def share(part, axis, groups=None):
    count = lax.axis_size(axis) if groups is None else len(groups[0])
    return trade(jnp.broadcast_to(part[None], (count, *part.shape)), axis, groups)


def turned(block):
    rows, cols = lax.axis_size("grp"), lax.axis_size("sp")
    batch, shift = cols // 2, QUARTERS // 2
    pairs = []
    for row in range(rows):
        major, quarter = divmod((row - shift) % rows, QUARTERS)
        for col in range(cols):
            there = (QUARTERS * (col % batch) + quarter + shift) % rows
            pairs.append((row * cols + col, there * cols + col // batch * batch + major))
    return lax.ppermute(block, ("grp", "sp"), pairs)


def planes():
    rows, cols = lax.axis_size("grp"), lax.axis_size("sp")
    return [
        [row * cols + col for row in range(start, start + 4) for col in range(cols) if col & 2 == far]
        for start in range(0, rows, 4)
        for far in (0, 2)
    ]


def columns():
    rows, cols = lax.axis_size("grp"), lax.axis_size("sp")
    return [
        [row * cols + col + far for row in range(y, rows, 4) for far in (0, 2)]
        for y in range(4)
        for col in range(cols)
        if col & 2 == 0
    ]


def late():
    return (lax.axis_index("grp") % 4 < 2).astype(jnp.int32)


def for_plane(cells):
    lead = cells.shape[0] // 4
    parts = cells.reshape(lead, 2, 2, QUARTERS, 8, LANES)
    parts = jnp.roll(jnp.transpose(parts, (3, 0, 2, 1, 4, 5)), QUARTERS // 2, axis=0)
    blank = jnp.zeros_like(parts)
    low = upper_half() == 0
    both = [jnp.where(low, parts, blank), jnp.where(low, blank, parts)]
    return jnp.concatenate(both, axis=1).reshape(-1, 16, LANES)


def for_column(got):
    lead = lax.axis_size("sp") // 8
    parts = got.reshape(4, 2, lead, 2, 2, 8, LANES)
    parts = jnp.where(upper_half() == 0, parts[:, 0], parts[:, 1])
    parts = jnp.transpose(parts, (1, 2, 3, 0, 4, 5))
    parts = jnp.stack([parts, jnp.zeros_like(parts)], axis=1).reshape(4 * lead, 2, 32, LANES)
    steps = 4 * lead
    shift = 2 * far_side() + late()
    twice = jnp.concatenate([parts, parts], axis=0)
    return lax.dynamic_slice_in_dim(twice, steps - shift, steps, axis=0).reshape(-1, 32, LANES)


def from_column(got):
    parts = got.reshape(-1, 2, 32, LANES)
    steps = parts.shape[0]
    sample = (lax.axis_index("grp") // 4 - late()) % steps
    return jnp.where(sample // 2 % 2 == 0, parts[:, 0], parts[:, 1]).reshape(-1, LANES)


def far_side():
    return lax.axis_index("sp") // 2 % 2


def far_exchange(parts):
    near = far_side() == 0
    kept = jnp.where(near, parts[:, 0], parts[:, 1])
    sent = jnp.where(near, parts[:, 1], parts[:, 0])
    got = lax.ppermute(sent, "sp", [(col, col ^ 2) for col in range(lax.axis_size("sp"))])
    return jnp.stack([jnp.where(near, kept, got), jnp.where(near, got, kept)], axis=2)


def near_exchange(parts):
    cols, lead = lax.axis_size("sp"), parts.shape[0]
    groups = [
        [start + 4 * far + core for far in range(lead) for core in (0, 1)]
        for half in range(0, cols, 4 * lead)
        for start in (half, half + 2)
    ]
    return trade(parts.reshape(2 * lead, *parts.shape[2:]), "sp", groups).reshape(parts.shape)


def local(features, weight_fine, weight_down, weight_coarse, cotangent):
    batch, chans, x_cells, y_cells, z_cells = features.shape
    chans3 = weight_down.shape[1]
    rows, cols = lax.axis_size("grp"), lax.axis_size("sp")
    width = batch * z_cells // 2
    extent = batch + reach()
    wider = extent * z_cells // 2
    fine_scale = 1.0 / math.sqrt(batch * x_cells * cols * y_cells * rows * z_cells)
    coarse_scale = 1.0 / math.sqrt(batch * x_cells * cols * y_cells * rows * z_cells // 8)
    shape = jax.ShapeDtypeStruct
    near = planes()
    unit = len(near[0]) * 8
    grad_rows = -(-(27 * chans3 // 2 + 9 * chans + 2 * chans3) // unit) * unit
    half = upper_half().astype(jnp.int32).reshape(1)

    sort = jnp.asarray(sort_matrix(), BF16)
    unsort = jnp.asarray(sort_matrix().T, BF16)
    parted = weight_down.reshape(2, 2, 2, chans3, chans)
    down_matrix = jnp.transpose(parted, (3, 2, 0, 1, 4)).reshape(chans3, 8 * chans)

    halves = [list(range(batch)), list(range(batch, cols))]
    own = trade(jnp.transpose(features, (0, 2, 3, 1, 4)), "sp", halves)
    own = own.reshape(batch * x_cells, y_cells, chans, LANES)

    block = (rows, width // 2 // rows, LANES)
    cells = pl.pallas_call(
        pack_kernel, out_shape=shape((width // 2, LANES), BF16), interpret=INTERPRET
    )(cotangent.reshape(chans3, width))
    cells = turned(cells).reshape(block)
    matrices = [
        tap_matrix(weight_fine),
        tap_matrix(reversed_taps(weight_fine)),
        tap_matrix(weight_coarse),
        tap_matrix(reversed_taps(weight_coarse)),
        down_matrix,
        down_matrix.T,
    ]
    own, cells, *matrices = lax.optimization_barrier((own, cells, *matrices))
    fine_matrix, fine_back, coarse_matrix, coarse_back, down_matrix, up_matrix = matrices
    own = joined(own, arrival(nearest(own, reach() * x_cells), 0, True))
    cells = jnp.roll(trade(cells, "grp"), -(QUARTERS // 2), axis=0).reshape(width // 2, LANES)
    upstream = joined(cells, arrival(nearest(cells, reach() * QUARTERS * block[1]), 0, True))

    feature_pieces = fine_pieces(own)
    down, sorted_act, slope = call(
        down_kernel,
        (
            shape((chans3, wider), BF16),
            shape((8 * chans, wider), BF16),
            shape((extent, 4 * chans, LANES), F32),
        ),
        half,
        *feature_pieces,
        fine_matrix,
        down_matrix,
        sort,
    )
    down_pieces = coarse_pieces(down)
    coarse, dpre3 = call(
        coarse_kernel,
        (shape(upstream.shape, BF16), shape((chans3, wider), BF16)),
        half,
        *down_pieces,
        coarse_matrix,
        upstream,
    )
    coarse_grad = call(
        partial(coarse_grad_kernel, batch),
        shape((27 * chans3 // 2, LANES), BF16),
        half,
        *down_pieces,
        dpre3,
    )
    dpre_pieces = coarse_pieces(dpre3)
    coarse_grad, *dpre_pieces = lax.optimization_barrier((coarse_grad, *dpre_pieces))

    dpre2, grads = call(
        partial(back_kernel, batch),
        (shape(own.shape, BF16), shape((grad_rows, LANES), BF16)),
        half,
        *dpre_pieces,
        *feature_pieces,
        coarse_back,
        up_matrix,
        unsort,
        sorted_act,
        slope,
        coarse_grad,
    )
    coarse = jnp.where(upper_half() == 0, coarse[: width // 2], coarse[-(width // 2) :])
    grads = grads.reshape(len(near[0]), -1, LANES)
    kept = grads.shape[1]
    coarse = for_plane(coarse.reshape(batch, QUARTERS, 8, LANES))
    mixed = trade(jnp.concatenate([grads, coarse], axis=1), ("grp", "sp"), near)
    part = jnp.sum(mixed[:, :kept].astype(F32), axis=0).astype(BF16)
    coarse = for_column(mixed[:, kept:])
    gradient = call(
        input_kernel,
        shape((batch * x_cells, *own.shape[1:]), BF16),
        half,
        *last_pieces(dpre2, batch * x_cells),
        fine_back,
    )
    part, gradient, coarse = lax.optimization_barrier((part, gradient, coarse))
    gradient = far_exchange(gradient.reshape(batch // 4, 2, 2, x_cells, y_cells, chans, LANES))
    part = jnp.broadcast_to(part[None], (coarse.shape[0], *part.shape))
    mixed = trade(jnp.concatenate([part, coarse], axis=1), ("grp", "sp"), columns())
    part = jnp.sum(mixed[:, :kept].astype(F32), axis=0).astype(BF16)
    coarse = from_column(mixed[:, kept:])
    grads = share(part, ("grp", "sp"), near).reshape(grad_rows, LANES)
    grads, gradient = lax.optimization_barrier((grads, gradient))
    gradient = near_exchange(gradient)
    grad_input = jnp.transpose(gradient, (0, 2, 1, 5, 3, 4, 6)).reshape(features.shape)

    result = pl.pallas_call(
        unpack_kernel, out_shape=shape((chans3, width), BF16), interpret=INTERPRET
    )(coarse)
    result = result.reshape(cotangent.shape)

    grad_fine, grad_down, grad_coarse = pl.pallas_call(
        partial(assemble_kernel, fine_scale, coarse_scale),
        out_shape=(
            shape(weight_fine.shape, F32),
            shape((8, chans, chans3), F32),
            shape(weight_coarse.shape, F32),
        ),
        interpret=INTERPRET,
    )(grads)
    return result, grad_input, grad_fine, jnp.swapaxes(grad_down, 1, 2), grad_coarse


def solution(mesh):
    placed = (P(None, None, "sp", "grp", None), P(), P(), P(), P("grp", None, "sp", None))
    return jax.shard_map(
        local,
        mesh=mesh,
        in_specs=placed,
        out_specs=(P("grp", None, "sp", None), P(None, None, "sp", "grp", None), P(), P(), P()),
        check_vma=False,
    )
```

```python
import math
from functools import partial

import jax
import jax.numpy as jnp
import numpy as np
from jax import lax
from jax.experimental import pallas as pl
from jax.experimental.pallas import tpu as pltpu
from jax.sharding import PartitionSpec as P

QUARTERS = 4
LANES = 128
STEPS = (-1, 0, 1)
F32 = jnp.float32
BF16 = jnp.bfloat16
INTERPRET = False


def call(kernel, outs, half, *operands):
    spaces = [pltpu.SMEM] + [pltpu.VMEM] * len(operands)
    return pl.pallas_call(
        kernel,
        out_shape=outs,
        in_specs=[pl.BlockSpec(memory_space=space) for space in spaces],
        compiler_params=pltpu.CompilerParams(vmem_limit_bytes=28 * 1024 * 1024),
        interpret=INTERPRET,
    )(half, *operands)


def arrival(block, step_y, across):
    rows, cols = lax.axis_size("grp"), lax.axis_size("sp")
    pairs = []
    for row in range(rows):
        for col in range(cols):
            if 0 <= row + step_y < rows:
                source = (col + cols // 2) % cols if across else col
                pairs.append(((row + step_y) * cols + source, row * cols + col))
    return lax.ppermute(block, ("grp", "sp"), pairs)


def upper_half():
    return lax.axis_index("sp") // (lax.axis_size("sp") // 2)


def reach():
    return min(4, lax.axis_size("sp") // 2)


def joined(own, other):
    low = jnp.concatenate([own, other], axis=0)
    return jnp.where(upper_half() == 0, low, jnp.concatenate([other, own], axis=0))


def nearest(block, count):
    return jnp.where(upper_half() == 0, block[-count:], block[:count])


def fine_pieces(block):
    return [block, arrival(block[:, 1:], -1, False), arrival(block[:, :1], 1, False)]


def last_pieces(block, count):
    there = jnp.where(upper_half() == 0, block[: count + 1], block[-(count + 1) :])
    return [block, arrival(there[:, 1:], -1, False), arrival(there[:, :1], 1, False)]


def coarse_pieces(block):
    return [block, arrival(block, -1, False), arrival(block, 1, False)]


def silu_slope(values, sigma):
    return sigma * (1.0 + values * (1.0 - sigma))


def dot(left, right):
    return lax.dot_general(left, right, (((1,), (0,)), ((), ())), preferred_element_type=F32)


def dot_lanes(left, right):
    return lax.dot_general(left, right, (((1,), (1,)), ((), ())), preferred_element_type=F32)


def shifted(values, step, span):
    if step == 0:
        return values
    place = lax.broadcasted_iota(jnp.int32, values.shape, 1) % span
    width = values.shape[1]
    moved = pltpu.roll(values, (-step) % width, 1)
    return jnp.where(place == (span - 1 if step > 0 else 0), 0.0, moved)


def fold_taps(products, chans, span):
    total = products[chans : 2 * chans]
    total = total + shifted(products[:chans], -1, span)
    return total + shifted(products[2 * chans :], 1, span)


def fine_stack(refs, column, shift=None):
    center, before, after = refs
    cells = center.shape[0]

    def cell(x, y):
        inside = None
        if shift is not None:
            half, skip, count = shift
            inside = half == 1 if x < 0 else half == 0 if x >= count else None
            lag = 0 if before.shape[0] == cells else skip - 1
            beside = jnp.clip(x + (skip - lag) * half, 0, before.shape[0] - 1)
            x = jnp.clip(x + skip * half, 0, cells - 1)
        elif not 0 <= x < cells:
            return jnp.zeros(center.shape[2:], center.dtype)
        else:
            beside = x
        value = before[beside, 0] if y < 0 else after[beside, 0] if y > 1 else center[x, y]
        return value if inside is None else jnp.where(inside, value, jnp.zeros_like(value))

    return jnp.concatenate(
        [
            jnp.concatenate(
                [cell(2 * column + x + a, y + b) for x in (0, 1) for y in (0, 1)], axis=1
            )
            for a in STEPS
            for b in STEPS
        ],
        axis=0,
    )


def coarse_stack(refs):
    tiles = refs[0].shape[1] // LANES
    low = lax.broadcasted_iota(jnp.int32, (refs[0].shape[0], LANES), 1) < LANES // 2
    lined = []
    for ref in (refs[1], refs[0], refs[2]):
        own = [ref[:, tile * LANES : (tile + 1) * LANES] for tile in range(tiles)]
        first = jnp.where(low, own[-1].astype(F32), 0.0)
        last = jnp.where(low, 0.0, own[0].astype(F32))
        first, last = [pltpu.roll(tile, LANES // 2, 1).astype(BF16) for tile in (first, last)]
        lined.append([first, *own, last])
    return jnp.concatenate(
        [jnp.concatenate(lined[b][a : a + tiles], axis=1) for a in range(3) for b in range(3)],
        axis=0,
    )


def own_lanes(half, extent, shape):
    lane = lax.broadcasted_iota(jnp.int32, shape, 1)
    tiles = shape[1] // LANES
    x = lane // LANES + tiles * (lane % LANES // (LANES // 2)) - (2 * tiles - extent) * half
    return (x >= 0) & (x < extent)


def down_kernel(half, *refs):
    pieces, (weights, down_weights, sort, down, sorted_act, slope) = refs[:3], refs[3:]
    columns, chans = pieces[0].shape[0] // 2, pieces[0].shape[2]
    for tile in range(columns // 2):
        acts = []
        for column in (tile, tile + columns // 2):
            products = dot(weights[...], fine_stack(pieces, column))
            parts = []
            for place in range(4):
                pre = fold_taps(products[:, place * LANES : (place + 1) * LANES], chans, LANES)
                sigma = jax.nn.sigmoid(pre)
                slope[column, place * chans : (place + 1) * chans] = silu_slope(pre, sigma)
                parts.append((pre * sigma).astype(BF16))
            acts.append(jnp.concatenate(parts, axis=0))
        parted = dot(jnp.concatenate(acts, axis=1), sort[...]).astype(BF16)
        stacked = jnp.concatenate([parted[:, :LANES], parted[:, LANES:]], axis=0)
        lanes = slice(tile * LANES, (tile + 1) * LANES)
        sorted_act[:, lanes] = stacked
        down[:, lanes] = dot(down_weights[...], stacked).astype(BF16)


def coarse_kernel(half, *refs):
    pieces, (weights, upstream, out, dpre) = refs[:3], refs[3:]
    chans, width = pieces[0].shape
    pre = fold_taps(dot(weights[...], coarse_stack(pieces)), chans, LANES // 2)
    sigma = jax.nn.sigmoid(pre)
    act = pre * sigma
    slope = silu_slope(pre, sigma)
    tiles = width // LANES
    rows = LANES // 4
    for tile in range(tiles):
        lanes = slice(tile * LANES, (tile + 1) * LANES)
        ends = [tile * rows, (tile + tiles) * rows]
        packed = jnp.concatenate([upstream[end : end + rows] for end in ends], axis=0)
        dpre[:, lanes] = (unpacked(packed.astype(F32)) * slope[:, lanes]).astype(BF16)
        both = packed_cells(act[:, lanes]).astype(BF16)
        for member, end in enumerate(ends):
            out[end : end + rows] = both[member * rows : (member + 1) * rows]


def packed_cells(values):
    turned = jnp.concatenate([values, values], axis=0).T.reshape(LANES // 16, 2, 8, LANES)
    low = lax.broadcasted_iota(jnp.int32, (LANES // 16, 8, LANES), 2) < LANES // 2
    return jnp.where(low, turned[:, 0], turned[:, 1]).reshape(LANES // 2, LANES)


def unpacked(values):
    first = values.reshape(LANES // 16, 1, 8, LANES)
    second = pltpu.roll(values, LANES // 2, 1).reshape(LANES // 16, 1, 8, LANES)
    turned = jnp.concatenate([first, second], axis=1).reshape(LANES, LANES).T
    return turned[: LANES // 2]


def pack_kernel(values, out):
    for tile in range(values.shape[1] // LANES):
        part = values[:, tile * LANES : (tile + 1) * LANES].astype(F32)
        out[tile * LANES // 2 : (tile + 1) * LANES // 2] = packed_cells(part).astype(BF16)


def unpack_kernel(values, out):
    for tile in range(out.shape[1] // LANES):
        part = values[tile * LANES // 2 : (tile + 1) * LANES // 2].astype(F32)
        out[:, tile * LANES : (tile + 1) * LANES] = unpacked(part).astype(BF16)


def tap_stack(values, span):
    values = values.astype(F32)
    return jnp.concatenate([shifted(values, -step, span).astype(BF16) for step in STEPS], axis=0)


def store_tiles(ref, base, values):
    rows, cols = values.shape
    for start in range(0, cols, LANES):
        width = min(LANES, cols - start)
        ref[base : base + rows, :width] = values[:, start : start + width].astype(ref.dtype)
        base += rows
    return base


def coarse_grad_kernel(extent, half, *refs):
    pieces, (dpre, grad) = refs[:3], refs[3:]
    own = jnp.where(own_lanes(half[0], extent, dpre.shape), dpre[...].astype(F32), 0.0)
    products = dot_lanes(tap_stack(own, LANES // 2), coarse_stack(pieces))
    rows, cols = products.shape
    base = store_tiles(grad, 0, products[:, : cols - LANES // 2])
    last = products[:, cols - LANES // 2 :]
    grad[base:] = jnp.concatenate([last[: rows // 2], last[rows // 2 :]], axis=1).astype(grad.dtype)


def back_kernel(extent, half, *refs):
    pieces, feature_pieces = refs[:3], refs[3:6]
    weights, up_weights, unsort, sorted_act, slope, coarse_grad, dpre2, grads = refs[6:]
    chans3 = pieces[0].shape[0]
    columns, chans = feature_pieces[0].shape[0] // 2, feature_pieces[0].shape[2]
    ddown = fold_taps(dot(weights[...], coarse_stack(pieces)), chans3, LANES // 2)
    own_ddown = jnp.where(own_lanes(half[0], extent, ddown.shape), ddown, 0.0).astype(BF16)
    ddown = ddown.astype(BF16)
    spread = dot(up_weights[...], ddown).astype(BF16)
    rows = spread.shape[0] // 2
    for tile in range(columns // 2):
        lanes = slice(tile * LANES, (tile + 1) * LANES)
        both = dot(jnp.concatenate([spread[:rows, lanes], spread[rows:, lanes]], axis=1), unsort[...])
        for member in range(2):
            column = tile + member * (columns // 2)
            dpre = both[:, member * LANES : (member + 1) * LANES] * slope[column]
            dpre = dpre.astype(BF16)
            parts = [dpre[place * chans : (place + 1) * chans] for place in range(4)]
            for place in range(4):
                dpre2[2 * column + place // 2, place % 2] = parts[place]
    total = None
    skip = columns - extent
    for place in range(extent):
        column = place + skip * half[0]
        parts = [dpre2[2 * column + x, y] for x in (0, 1) for y in (0, 1)]
        moved = jnp.concatenate([tap_stack(part, LANES) for part in parts], axis=1)
        stack = fine_stack(feature_pieces, place, (half[0], 2 * skip, 2 * extent))
        term = dot_lanes(moved, stack)
        total = term if total is None else total + term
    base = coarse_grad.shape[0]
    grads[:base] = coarse_grad[...]
    grads[base:] = jnp.zeros((grads.shape[0] - base, LANES), grads.dtype)
    base = store_tiles(grads, base, total)
    grad_down = dot_lanes(sorted_act[...], own_ddown)
    rows = grad_down.shape[0] // 2
    grads[base : base + rows] = jnp.concatenate(
        [grad_down[:rows], grad_down[rows:]], axis=1
    ).astype(grads.dtype)


def input_kernel(half, *refs):
    pieces, (weights, out) = refs[:3], refs[3:]
    cells, chans = pieces[0].shape[0], pieces[0].shape[2]
    count = out.shape[0]
    for column in range(count // 2):
        stack = fine_stack(pieces, column, (half[0], cells - count, count))
        products = dot(weights[...], stack)
        for place in range(4):
            total = fold_taps(products[:, place * LANES : (place + 1) * LANES], chans, LANES)
            out[2 * column + place // 2, place % 2] = total.astype(BF16)


def assemble_kernel(fine_scale, coarse_scale, rows, fine, down, coarse):
    def pieces(start, count, width, scale):
        tile = rows[start : start + count].astype(F32) * scale
        return [
            (tile if lane == 0 else pltpu.roll(tile, LANES - lane, 1))[:, :width]
            for lane in range(0, LANES, width)
        ]

    chans, chans3 = fine.shape[1], coarse.shape[1]
    for tile in range(4):
        for h, part in enumerate(pieces(3 * tile * chans3, 3 * chans3, chans3, coarse_scale)):
            for c in range(3):
                coarse[6 * tile + 3 * h + c] = part[c * chans3 : (c + 1) * chans3]
    base = 12 * chans3
    low, high = pieces(base, 3 * chans3 // 2, chans3, coarse_scale)
    coarse[24] = low[:chans3]
    coarse[25] = jnp.concatenate([low[chans3:], high[: chans3 // 2]], axis=0)
    coarse[26] = high[chans3 // 2 :]
    base += 3 * chans3 // 2
    for tile in range(3):
        for h, part in enumerate(pieces(base, 3 * chans, chans, fine_scale)):
            for c in range(3):
                if 4 * tile + h < 9:
                    fine[3 * (4 * tile + h) + c] = part[c * chans : (c + 1) * chans]
        base += 3 * chans
    for last, part in enumerate(pieces(base, 4 * chans, chans3, coarse_scale)):
        for first in range(4):
            down[2 * first + last] = part[first * chans : (first + 1) * chans]


def tap_matrix(weights):
    taps, outs, ins = weights.shape
    return jnp.transpose(weights.reshape(9, 3, outs, ins), (1, 2, 0, 3)).reshape(3 * outs, 9 * ins)


def reversed_taps(weights):
    return jnp.transpose(weights[::-1], (0, 2, 1))


def sort_matrix():
    table = np.zeros((2 * LANES, 2 * LANES), np.float32)
    for sample in range(2):
        for z in range(LANES):
            table[sample * LANES + z, (z % 2) * LANES + sample * (LANES // 2) + z // 2] = 1.0
    return table


def trade(parts, axis, groups=None):
    return lax.all_to_all(
        parts, axis, split_axis=0, concat_axis=0, axis_index_groups=groups, tiled=True
    )


def share(part, axis, groups=None):
    count = lax.axis_size(axis) if groups is None else len(groups[0])
    return trade(jnp.broadcast_to(part[None], (count, *part.shape)), axis, groups)


def turned(block):
    rows, cols = lax.axis_size("grp"), lax.axis_size("sp")
    batch, shift = cols // 2, QUARTERS // 2
    pairs = []
    for row in range(rows):
        major, quarter = divmod((row - shift) % rows, QUARTERS)
        for col in range(cols):
            there = (QUARTERS * (col % batch) + quarter + shift) % rows
            pairs.append((row * cols + col, there * cols + col // batch * batch + major))
    return lax.ppermute(block, ("grp", "sp"), pairs)


def planes():
    rows, cols = lax.axis_size("grp"), lax.axis_size("sp")
    return [
        [row * cols + col for row in range(start, start + 4) for col in range(cols) if col & 2 == far]
        for start in range(0, rows, 4)
        for far in (0, 2)
    ]


def columns():
    rows, cols = lax.axis_size("grp"), lax.axis_size("sp")
    return [
        [row * cols + col + far for row in range(y, rows, 4) for far in (0, 2)]
        for y in range(4)
        for col in range(cols)
        if col & 2 == 0
    ]


def late():
    return (lax.axis_index("grp") % 4 < 2).astype(jnp.int32)


def for_plane(cells):
    lead = cells.shape[0] // 4
    parts = cells.reshape(lead, 2, 2, QUARTERS, 8, LANES)
    parts = jnp.roll(jnp.transpose(parts, (3, 0, 2, 1, 4, 5)), QUARTERS // 2, axis=0)
    blank = jnp.zeros_like(parts)
    low = upper_half() == 0
    both = [jnp.where(low, parts, blank), jnp.where(low, blank, parts)]
    return jnp.concatenate(both, axis=1).reshape(-1, 16, LANES)


def for_column(got):
    lead = lax.axis_size("sp") // 8
    parts = got.reshape(4, 2, lead, 2, 2, 8, LANES)
    parts = jnp.where(upper_half() == 0, parts[:, 0], parts[:, 1])
    parts = jnp.transpose(parts, (1, 2, 3, 0, 4, 5))
    parts = jnp.stack([parts, jnp.zeros_like(parts)], axis=1).reshape(4 * lead, 2, 32, LANES)
    steps = 4 * lead
    shift = 2 * far_side() + late()
    twice = jnp.concatenate([parts, parts], axis=0)
    return lax.dynamic_slice_in_dim(twice, steps - shift, steps, axis=0).reshape(-1, 32, LANES)


def from_column(got):
    parts = got.reshape(-1, 2, 32, LANES)
    steps = parts.shape[0]
    sample = (lax.axis_index("grp") // 4 - late()) % steps
    return jnp.where(sample // 2 % 2 == 0, parts[:, 0], parts[:, 1]).reshape(-1, LANES)


def far_side():
    return lax.axis_index("sp") // 2 % 2


def far_exchange(parts):
    near = far_side() == 0
    kept = jnp.where(near, parts[:, 0], parts[:, 1])
    sent = jnp.where(near, parts[:, 1], parts[:, 0])
    got = lax.ppermute(sent, "sp", [(col, col ^ 2) for col in range(lax.axis_size("sp"))])
    return jnp.stack([jnp.where(near, kept, got), jnp.where(near, got, kept)], axis=2)


def near_exchange(parts):
    cols, lead = lax.axis_size("sp"), parts.shape[0]
    groups = [
        [start + 4 * far + core for far in range(lead) for core in (0, 1)]
        for half in range(0, cols, 4 * lead)
        for start in (half, half + 2)
    ]
    return trade(parts.reshape(2 * lead, *parts.shape[2:]), "sp", groups).reshape(parts.shape)


def local(features, weight_fine, weight_down, weight_coarse, cotangent):
    batch, chans, x_cells, y_cells, z_cells = features.shape
    chans3 = weight_down.shape[1]
    rows, cols = lax.axis_size("grp"), lax.axis_size("sp")
    width = batch * z_cells // 2
    extent = batch + reach()
    wider = extent * z_cells // 2
    fine_scale = 1.0 / math.sqrt(batch * x_cells * cols * y_cells * rows * z_cells)
    coarse_scale = 1.0 / math.sqrt(batch * x_cells * cols * y_cells * rows * z_cells // 8)
    shape = jax.ShapeDtypeStruct
    near = planes()
    unit = len(near[0]) * 8
    grad_rows = -(-(27 * chans3 // 2 + 9 * chans + 2 * chans3) // unit) * unit
    half = upper_half().astype(jnp.int32).reshape(1)

    sort = jnp.asarray(sort_matrix(), BF16)
    unsort = jnp.asarray(sort_matrix().T, BF16)
    parted = weight_down.reshape(2, 2, 2, chans3, chans)
    down_matrix = jnp.transpose(parted, (3, 2, 0, 1, 4)).reshape(chans3, 8 * chans)

    halves = [list(range(batch)), list(range(batch, cols))]
    own = trade(jnp.transpose(features, (0, 2, 3, 1, 4)), "sp", halves)
    own = own.reshape(batch * x_cells, y_cells, chans, LANES)

    block = (rows, width // 2 // rows, LANES)
    cells = pl.pallas_call(
        pack_kernel, out_shape=shape((width // 2, LANES), BF16), interpret=INTERPRET
    )(cotangent.reshape(chans3, width))
    cells = turned(cells).reshape(block)
    matrices = [
        tap_matrix(weight_fine),
        tap_matrix(reversed_taps(weight_fine)),
        tap_matrix(weight_coarse),
        tap_matrix(reversed_taps(weight_coarse)),
        down_matrix,
        down_matrix.T,
    ]
    own, cells, *matrices = lax.optimization_barrier((own, cells, *matrices))
    fine_matrix, fine_back, coarse_matrix, coarse_back, down_matrix, up_matrix = matrices
    own = joined(own, arrival(nearest(own, reach() * x_cells), 0, True))
    cells = jnp.roll(trade(cells, "grp"), -(QUARTERS // 2), axis=0).reshape(width // 2, LANES)
    upstream = joined(cells, arrival(nearest(cells, reach() * QUARTERS * block[1]), 0, True))

    feature_pieces = fine_pieces(own)
    down, sorted_act, slope = call(
        down_kernel,
        (
            shape((chans3, wider), BF16),
            shape((8 * chans, wider), BF16),
            shape((extent, 4 * chans, LANES), F32),
        ),
        half,
        *feature_pieces,
        fine_matrix,
        down_matrix,
        sort,
    )
    down_pieces = coarse_pieces(down)
    coarse, dpre3 = call(
        coarse_kernel,
        (shape(upstream.shape, BF16), shape((chans3, wider), BF16)),
        half,
        *down_pieces,
        coarse_matrix,
        upstream,
    )
    coarse_grad = call(
        partial(coarse_grad_kernel, batch),
        shape((27 * chans3 // 2, LANES), BF16),
        half,
        *down_pieces,
        dpre3,
    )
    dpre_pieces = coarse_pieces(dpre3)
    coarse_grad, *dpre_pieces = lax.optimization_barrier((coarse_grad, *dpre_pieces))

    dpre2, grads = call(
        partial(back_kernel, batch),
        (shape(own.shape, BF16), shape((grad_rows, LANES), BF16)),
        half,
        *dpre_pieces,
        *feature_pieces,
        coarse_back,
        up_matrix,
        unsort,
        sorted_act,
        slope,
        coarse_grad,
    )
    coarse = jnp.where(upper_half() == 0, coarse[: width // 2], coarse[-(width // 2) :])
    grads = grads.reshape(len(near[0]), -1, LANES)
    kept = grads.shape[1]
    coarse = for_plane(coarse.reshape(batch, QUARTERS, 8, LANES))
    mixed = trade(jnp.concatenate([grads, coarse], axis=1), ("grp", "sp"), near)
    part = jnp.sum(mixed[:, :kept].astype(F32), axis=0).astype(BF16)
    coarse = for_column(mixed[:, kept:])
    spread = last_pieces(dpre2, batch * x_cells)
    part, coarse, *spread[1:] = lax.optimization_barrier((part, coarse, *spread[1:]))
    gradient = call(
        input_kernel,
        shape((batch * x_cells, *own.shape[1:]), BF16),
        half,
        *spread,
        fine_back,
    )
    gradient = far_exchange(gradient.reshape(batch // 4, 2, 2, x_cells, y_cells, chans, LANES))
    part = jnp.broadcast_to(part[None], (coarse.shape[0], *part.shape))
    mixed = trade(jnp.concatenate([part, coarse], axis=1), ("grp", "sp"), columns())
    part = jnp.sum(mixed[:, :kept].astype(F32), axis=0).astype(BF16)
    coarse = from_column(mixed[:, kept:])
    grads = share(part, ("grp", "sp"), near).reshape(grad_rows, LANES)
    grads, gradient = lax.optimization_barrier((grads, gradient))
    gradient = near_exchange(gradient)
    grad_input = jnp.transpose(gradient, (0, 2, 1, 5, 3, 4, 6)).reshape(features.shape)

    result = pl.pallas_call(
        unpack_kernel, out_shape=shape((chans3, width), BF16), interpret=INTERPRET
    )(coarse)
    result = result.reshape(cotangent.shape)

    grad_fine, grad_down, grad_coarse = pl.pallas_call(
        partial(assemble_kernel, fine_scale, coarse_scale),
        out_shape=(
            shape(weight_fine.shape, F32),
            shape((8, chans, chans3), F32),
            shape(weight_coarse.shape, F32),
        ),
        interpret=INTERPRET,
    )(grads)
    return result, grad_input, grad_fine, jnp.swapaxes(grad_down, 1, 2), grad_coarse


def solution(mesh):
    placed = (P(None, None, "sp", "grp", None), P(), P(), P(), P("grp", None, "sp", None))
    return jax.shard_map(
        local,
        mesh=mesh,
        in_specs=placed,
        out_specs=(P("grp", None, "sp", None), P(None, None, "sp", "grp", None), P(), P(), P()),
        check_vma=False,
    )
```

```python
import math
from functools import partial

import jax
import jax.numpy as jnp
import numpy as np
from jax import lax
from jax.experimental import pallas as pl
from jax.experimental.pallas import tpu as pltpu
from jax.sharding import PartitionSpec as P

QUARTERS = 4
LANES = 128
STEPS = (-1, 0, 1)
F32 = jnp.float32
BF16 = jnp.bfloat16
INTERPRET = False


def call(kernel, outs, half, *operands):
    spaces = [pltpu.SMEM] + [pltpu.VMEM] * len(operands)
    return pl.pallas_call(
        kernel,
        out_shape=outs,
        in_specs=[pl.BlockSpec(memory_space=space) for space in spaces],
        compiler_params=pltpu.CompilerParams(vmem_limit_bytes=28 * 1024 * 1024),
        interpret=INTERPRET,
    )(half, *operands)


def arrival(block, step_y, across):
    rows, cols = lax.axis_size("grp"), lax.axis_size("sp")
    pairs = []
    for row in range(rows):
        for col in range(cols):
            if 0 <= row + step_y < rows:
                source = (col + cols // 2) % cols if across else col
                pairs.append(((row + step_y) * cols + source, row * cols + col))
    return lax.ppermute(block, ("grp", "sp"), pairs)


def upper_half():
    return lax.axis_index("sp") // (lax.axis_size("sp") // 2)


def reach():
    return min(4, lax.axis_size("sp") // 2)


def joined(own, other):
    low = jnp.concatenate([own, other], axis=0)
    return jnp.where(upper_half() == 0, low, jnp.concatenate([other, own], axis=0))


def nearest(block, count):
    return jnp.where(upper_half() == 0, block[-count:], block[:count])


def fine_pieces(block):
    return [block, arrival(block[:, 1:], -1, False), arrival(block[:, :1], 1, False)]


def last_pieces(block, count):
    there = jnp.where(upper_half() == 0, block[: count + 1], block[-(count + 1) :])
    return [block, arrival(there[:, 1:], -1, False), arrival(there[:, :1], 1, False)]


def coarse_pieces(block):
    return [block, arrival(block, -1, False), arrival(block, 1, False)]


def silu_slope(values, sigma):
    return sigma * (1.0 + values * (1.0 - sigma))


def dot(left, right):
    return lax.dot_general(left, right, (((1,), (0,)), ((), ())), preferred_element_type=F32)


def dot_lanes(left, right):
    return lax.dot_general(left, right, (((1,), (1,)), ((), ())), preferred_element_type=F32)


def shifted(values, step, span):
    if step == 0:
        return values
    place = lax.broadcasted_iota(jnp.int32, values.shape, 1) % span
    width = values.shape[1]
    moved = pltpu.roll(values, (-step) % width, 1)
    return jnp.where(place == (span - 1 if step > 0 else 0), 0.0, moved)


def fold_taps(products, chans, span):
    total = products[chans : 2 * chans]
    total = total + shifted(products[:chans], -1, span)
    return total + shifted(products[2 * chans :], 1, span)


def fine_stack(refs, column, shift=None):
    center, before, after = refs
    cells = center.shape[0]

    def cell(x, y):
        inside = None
        if shift is not None:
            half, skip, count = shift
            inside = half == 1 if x < 0 else half == 0 if x >= count else None
            lag = 0 if before.shape[0] == cells else skip - 1
            beside = jnp.clip(x + (skip - lag) * half, 0, before.shape[0] - 1)
            x = jnp.clip(x + skip * half, 0, cells - 1)
        elif not 0 <= x < cells:
            return jnp.zeros(center.shape[2:], center.dtype)
        else:
            beside = x
        value = before[beside, 0] if y < 0 else after[beside, 0] if y > 1 else center[x, y]
        return value if inside is None else jnp.where(inside, value, jnp.zeros_like(value))

    return jnp.concatenate(
        [
            jnp.concatenate(
                [cell(2 * column + x + a, y + b) for x in (0, 1) for y in (0, 1)], axis=1
            )
            for a in STEPS
            for b in STEPS
        ],
        axis=0,
    )


def coarse_stack(refs):
    tiles = refs[0].shape[1] // LANES
    low = lax.broadcasted_iota(jnp.int32, (refs[0].shape[0], LANES), 1) < LANES // 2
    lined = []
    for ref in (refs[1], refs[0], refs[2]):
        own = [ref[:, tile * LANES : (tile + 1) * LANES] for tile in range(tiles)]
        first = jnp.where(low, own[-1].astype(F32), 0.0)
        last = jnp.where(low, 0.0, own[0].astype(F32))
        first, last = [pltpu.roll(tile, LANES // 2, 1).astype(BF16) for tile in (first, last)]
        lined.append([first, *own, last])
    return jnp.concatenate(
        [jnp.concatenate(lined[b][a : a + tiles], axis=1) for a in range(3) for b in range(3)],
        axis=0,
    )


def own_lanes(half, extent, shape):
    lane = lax.broadcasted_iota(jnp.int32, shape, 1)
    tiles = shape[1] // LANES
    x = lane // LANES + tiles * (lane % LANES // (LANES // 2)) - (2 * tiles - extent) * half
    return (x >= 0) & (x < extent)


def down_kernel(half, *refs):
    pieces, (weights, down_weights, sort, down, sorted_act, slope) = refs[:3], refs[3:]
    columns, chans = pieces[0].shape[0] // 2, pieces[0].shape[2]
    for tile in range(columns // 2):
        acts = []
        for column in (tile, tile + columns // 2):
            products = dot(weights[...], fine_stack(pieces, column))
            parts = []
            for place in range(4):
                pre = fold_taps(products[:, place * LANES : (place + 1) * LANES], chans, LANES)
                sigma = jax.nn.sigmoid(pre)
                slope[column, place * chans : (place + 1) * chans] = silu_slope(pre, sigma)
                parts.append((pre * sigma).astype(BF16))
            acts.append(jnp.concatenate(parts, axis=0))
        parted = dot(jnp.concatenate(acts, axis=1), sort[...]).astype(BF16)
        stacked = jnp.concatenate([parted[:, :LANES], parted[:, LANES:]], axis=0)
        lanes = slice(tile * LANES, (tile + 1) * LANES)
        sorted_act[:, lanes] = stacked
        down[:, lanes] = dot(down_weights[...], stacked).astype(BF16)


def coarse_kernel(half, *refs):
    pieces, (weights, upstream, out, dpre) = refs[:3], refs[3:]
    chans, width = pieces[0].shape
    pre = fold_taps(dot(weights[...], coarse_stack(pieces)), chans, LANES // 2)
    sigma = jax.nn.sigmoid(pre)
    act = pre * sigma
    slope = silu_slope(pre, sigma)
    tiles = width // LANES
    rows = LANES // 4
    for tile in range(tiles):
        lanes = slice(tile * LANES, (tile + 1) * LANES)
        ends = [tile * rows, (tile + tiles) * rows]
        packed = jnp.concatenate([upstream[end : end + rows] for end in ends], axis=0)
        dpre[:, lanes] = (unpacked(packed.astype(F32)) * slope[:, lanes]).astype(BF16)
        both = packed_cells(act[:, lanes]).astype(BF16)
        for member, end in enumerate(ends):
            out[end : end + rows] = both[member * rows : (member + 1) * rows]


def packed_cells(values):
    turned = jnp.concatenate([values, values], axis=0).T.reshape(LANES // 16, 2, 8, LANES)
    low = lax.broadcasted_iota(jnp.int32, (LANES // 16, 8, LANES), 2) < LANES // 2
    return jnp.where(low, turned[:, 0], turned[:, 1]).reshape(LANES // 2, LANES)


def unpacked(values):
    first = values.reshape(LANES // 16, 1, 8, LANES)
    second = pltpu.roll(values, LANES // 2, 1).reshape(LANES // 16, 1, 8, LANES)
    turned = jnp.concatenate([first, second], axis=1).reshape(LANES, LANES).T
    return turned[: LANES // 2]


def pack_kernel(values, out):
    for tile in range(values.shape[1] // LANES):
        part = values[:, tile * LANES : (tile + 1) * LANES].astype(F32)
        out[tile * LANES // 2 : (tile + 1) * LANES // 2] = packed_cells(part).astype(BF16)


def unpack_kernel(values, out):
    for tile in range(out.shape[1] // LANES):
        part = values[tile * LANES // 2 : (tile + 1) * LANES // 2].astype(F32)
        out[:, tile * LANES : (tile + 1) * LANES] = unpacked(part).astype(BF16)


def tap_stack(values, span):
    values = values.astype(F32)
    return jnp.concatenate([shifted(values, -step, span).astype(BF16) for step in STEPS], axis=0)


def store_tiles(ref, base, values):
    rows, cols = values.shape
    for start in range(0, cols, LANES):
        width = min(LANES, cols - start)
        ref[base : base + rows, :width] = values[:, start : start + width].astype(ref.dtype)
        base += rows
    return base


def coarse_grad_kernel(extent, half, *refs):
    pieces, (dpre, grad) = refs[:3], refs[3:]
    own = jnp.where(own_lanes(half[0], extent, dpre.shape), dpre[...].astype(F32), 0.0)
    products = dot_lanes(tap_stack(own, LANES // 2), coarse_stack(pieces))
    rows, cols = products.shape
    base = store_tiles(grad, 0, products[:, : cols - LANES // 2])
    last = products[:, cols - LANES // 2 :]
    grad[base:] = jnp.concatenate([last[: rows // 2], last[rows // 2 :]], axis=1).astype(grad.dtype)


def back_kernel(extent, half, *refs):
    pieces, feature_pieces = refs[:3], refs[3:6]
    weights, up_weights, unsort, sorted_act, slope, coarse_grad, dpre2, grads = refs[6:]
    chans3 = pieces[0].shape[0]
    columns, chans = feature_pieces[0].shape[0] // 2, feature_pieces[0].shape[2]
    ddown = fold_taps(dot(weights[...], coarse_stack(pieces)), chans3, LANES // 2)
    own_ddown = jnp.where(own_lanes(half[0], extent, ddown.shape), ddown, 0.0).astype(BF16)
    ddown = ddown.astype(BF16)
    spread = dot(up_weights[...], ddown).astype(BF16)
    rows = spread.shape[0] // 2
    for tile in range(columns // 2):
        lanes = slice(tile * LANES, (tile + 1) * LANES)
        both = dot(jnp.concatenate([spread[:rows, lanes], spread[rows:, lanes]], axis=1), unsort[...])
        for member in range(2):
            column = tile + member * (columns // 2)
            dpre = both[:, member * LANES : (member + 1) * LANES] * slope[column]
            dpre = dpre.astype(BF16)
            parts = [dpre[place * chans : (place + 1) * chans] for place in range(4)]
            for place in range(4):
                dpre2[2 * column + place // 2, place % 2] = parts[place]
    total = None
    skip = columns - extent
    for place in range(extent):
        column = place + skip * half[0]
        parts = [dpre2[2 * column + x, y] for x in (0, 1) for y in (0, 1)]
        moved = jnp.concatenate([tap_stack(part, LANES) for part in parts], axis=1)
        stack = fine_stack(feature_pieces, place, (half[0], 2 * skip, 2 * extent))
        term = dot_lanes(moved, stack)
        total = term if total is None else total + term
    base = coarse_grad.shape[0]
    grads[:base] = coarse_grad[...]
    grads[base:] = jnp.zeros((grads.shape[0] - base, LANES), grads.dtype)
    base = store_tiles(grads, base, total)
    grad_down = dot_lanes(sorted_act[...], own_ddown)
    rows = grad_down.shape[0] // 2
    grads[base : base + rows] = jnp.concatenate(
        [grad_down[:rows], grad_down[rows:]], axis=1
    ).astype(grads.dtype)


def input_kernel(half, *refs):
    pieces, (weights, out) = refs[:3], refs[3:]
    cells, chans = pieces[0].shape[0], pieces[0].shape[2]
    count = out.shape[0]
    for column in range(count // 2):
        stack = fine_stack(pieces, column, (half[0], cells - count, count))
        products = dot(weights[...], stack)
        for place in range(4):
            total = fold_taps(products[:, place * LANES : (place + 1) * LANES], chans, LANES)
            out[2 * column + place // 2, place % 2] = total.astype(BF16)


def assemble_kernel(fine_scale, coarse_scale, rows, fine, down, coarse):
    def pieces(start, count, width, scale):
        tile = rows[start : start + count].astype(F32) * scale
        return [
            (tile if lane == 0 else pltpu.roll(tile, LANES - lane, 1))[:, :width]
            for lane in range(0, LANES, width)
        ]

    chans, chans3 = fine.shape[1], coarse.shape[1]
    for tile in range(4):
        for h, part in enumerate(pieces(3 * tile * chans3, 3 * chans3, chans3, coarse_scale)):
            for c in range(3):
                coarse[6 * tile + 3 * h + c] = part[c * chans3 : (c + 1) * chans3]
    base = 12 * chans3
    low, high = pieces(base, 3 * chans3 // 2, chans3, coarse_scale)
    coarse[24] = low[:chans3]
    coarse[25] = jnp.concatenate([low[chans3:], high[: chans3 // 2]], axis=0)
    coarse[26] = high[chans3 // 2 :]
    base += 3 * chans3 // 2
    for tile in range(3):
        for h, part in enumerate(pieces(base, 3 * chans, chans, fine_scale)):
            for c in range(3):
                if 4 * tile + h < 9:
                    fine[3 * (4 * tile + h) + c] = part[c * chans : (c + 1) * chans]
        base += 3 * chans
    for last, part in enumerate(pieces(base, 4 * chans, chans3, coarse_scale)):
        for first in range(4):
            down[2 * first + last] = part[first * chans : (first + 1) * chans]


def tap_matrix(weights):
    taps, outs, ins = weights.shape
    return jnp.transpose(weights.reshape(9, 3, outs, ins), (1, 2, 0, 3)).reshape(3 * outs, 9 * ins)


def reversed_taps(weights):
    return jnp.transpose(weights[::-1], (0, 2, 1))


def sort_matrix():
    table = np.zeros((2 * LANES, 2 * LANES), np.float32)
    for sample in range(2):
        for z in range(LANES):
            table[sample * LANES + z, (z % 2) * LANES + sample * (LANES // 2) + z // 2] = 1.0
    return table


def trade(parts, axis, groups=None):
    return lax.all_to_all(
        parts, axis, split_axis=0, concat_axis=0, axis_index_groups=groups, tiled=True
    )


def share(part, axis, groups=None):
    count = lax.axis_size(axis) if groups is None else len(groups[0])
    return trade(jnp.broadcast_to(part[None], (count, *part.shape)), axis, groups)


def turned(block):
    rows, cols = lax.axis_size("grp"), lax.axis_size("sp")
    batch, shift = cols // 2, QUARTERS // 2
    pairs = []
    for row in range(rows):
        major, quarter = divmod((row - shift) % rows, QUARTERS)
        for col in range(cols):
            there = (QUARTERS * (col % batch) + quarter + shift) % rows
            pairs.append((row * cols + col, there * cols + col // batch * batch + major))
    return lax.ppermute(block, ("grp", "sp"), pairs)


def planes():
    rows, cols = lax.axis_size("grp"), lax.axis_size("sp")
    return [
        [row * cols + col for row in range(start, start + 4) for col in range(cols) if col & 2 == far]
        for start in range(0, rows, 4)
        for far in (0, 2)
    ]


def columns():
    rows, cols = lax.axis_size("grp"), lax.axis_size("sp")
    return [
        [row * cols + col + far for row in range(y, rows, 4) for far in (0, 2)]
        for y in range(4)
        for col in range(cols)
        if col & 2 == 0
    ]


def late():
    return (lax.axis_index("grp") % 4 < 2).astype(jnp.int32)


def for_plane(cells):
    lead = cells.shape[0] // 4
    parts = cells.reshape(lead, 2, 2, QUARTERS, 8, LANES)
    parts = jnp.roll(jnp.transpose(parts, (3, 0, 2, 1, 4, 5)), QUARTERS // 2, axis=0)
    blank = jnp.zeros_like(parts)
    low = upper_half() == 0
    both = [jnp.where(low, parts, blank), jnp.where(low, blank, parts)]
    return jnp.concatenate(both, axis=1).reshape(-1, 16, LANES)


def for_column(got):
    lead = lax.axis_size("sp") // 8
    parts = got.reshape(4, 2, lead, 2, 2, 8, LANES)
    parts = jnp.where(upper_half() == 0, parts[:, 0], parts[:, 1])
    parts = jnp.transpose(parts, (1, 2, 3, 0, 4, 5))
    parts = jnp.stack([parts, jnp.zeros_like(parts)], axis=1).reshape(4 * lead, 2, 32, LANES)
    steps = 4 * lead
    shift = 2 * far_side() + late()
    twice = jnp.concatenate([parts, parts], axis=0)
    return lax.dynamic_slice_in_dim(twice, steps - shift, steps, axis=0).reshape(-1, 32, LANES)


def from_column(got):
    parts = got.reshape(-1, 2, 32, LANES)
    steps = parts.shape[0]
    sample = (lax.axis_index("grp") // 4 - late()) % steps
    return jnp.where(sample // 2 % 2 == 0, parts[:, 0], parts[:, 1]).reshape(-1, LANES)


def far_side():
    return lax.axis_index("sp") // 2 % 2


def far_exchange(parts):
    near = far_side() == 0
    kept = jnp.where(near, parts[:, 0], parts[:, 1])
    sent = jnp.where(near, parts[:, 1], parts[:, 0])
    got = lax.ppermute(sent, "sp", [(col, col ^ 2) for col in range(lax.axis_size("sp"))])
    return jnp.stack([jnp.where(near, kept, got), jnp.where(near, got, kept)], axis=2)


def near_exchange(parts):
    cols, lead = lax.axis_size("sp"), parts.shape[0]
    groups = [
        [start + 4 * far + core for far in range(lead) for core in (0, 1)]
        for half in range(0, cols, 4 * lead)
        for start in (half, half + 2)
    ]
    return trade(parts.reshape(2 * lead, *parts.shape[2:]), "sp", groups).reshape(parts.shape)


def local(features, weight_fine, weight_down, weight_coarse, cotangent):
    batch, chans, x_cells, y_cells, z_cells = features.shape
    chans3 = weight_down.shape[1]
    rows, cols = lax.axis_size("grp"), lax.axis_size("sp")
    width = batch * z_cells // 2
    extent = batch + reach()
    wider = extent * z_cells // 2
    fine_scale = 1.0 / math.sqrt(batch * x_cells * cols * y_cells * rows * z_cells)
    coarse_scale = 1.0 / math.sqrt(batch * x_cells * cols * y_cells * rows * z_cells // 8)
    shape = jax.ShapeDtypeStruct
    near = planes()
    unit = len(near[0]) * 8
    grad_rows = -(-(27 * chans3 // 2 + 9 * chans + 2 * chans3) // unit) * unit
    half = upper_half().astype(jnp.int32).reshape(1)

    sort = jnp.asarray(sort_matrix(), BF16)
    unsort = jnp.asarray(sort_matrix().T, BF16)
    parted = weight_down.reshape(2, 2, 2, chans3, chans)
    down_matrix = jnp.transpose(parted, (3, 2, 0, 1, 4)).reshape(chans3, 8 * chans)

    halves = [list(range(batch)), list(range(batch, cols))]
    own = trade(jnp.transpose(features, (0, 2, 3, 1, 4)), "sp", halves)
    own = own.reshape(batch * x_cells, y_cells, chans, LANES)

    block = (rows, width // 2 // rows, LANES)
    cells = pl.pallas_call(
        pack_kernel, out_shape=shape((width // 2, LANES), BF16), interpret=INTERPRET
    )(cotangent.reshape(chans3, width))
    cells = turned(cells).reshape(block)
    matrices = [
        tap_matrix(weight_fine),
        tap_matrix(reversed_taps(weight_fine)),
        tap_matrix(weight_coarse),
        tap_matrix(reversed_taps(weight_coarse)),
        down_matrix,
        down_matrix.T,
    ]
    own, cells, *matrices = lax.optimization_barrier((own, cells, *matrices))
    fine_matrix, fine_back, coarse_matrix, coarse_back, down_matrix, up_matrix = matrices
    own = joined(own, arrival(nearest(own, reach() * x_cells), 0, True))
    cells = jnp.roll(trade(cells, "grp"), -(QUARTERS // 2), axis=0).reshape(width // 2, LANES)
    upstream = joined(cells, arrival(nearest(cells, reach() * QUARTERS * block[1]), 0, True))

    feature_pieces = fine_pieces(own)
    down, sorted_act, slope = call(
        down_kernel,
        (
            shape((chans3, wider), BF16),
            shape((8 * chans, wider), BF16),
            shape((extent, 4 * chans, LANES), F32),
        ),
        half,
        *feature_pieces,
        fine_matrix,
        down_matrix,
        sort,
    )
    down_pieces = coarse_pieces(down)
    coarse, dpre3 = call(
        coarse_kernel,
        (shape(upstream.shape, BF16), shape((chans3, wider), BF16)),
        half,
        *down_pieces,
        coarse_matrix,
        upstream,
    )
    coarse_grad = call(
        partial(coarse_grad_kernel, batch),
        shape((27 * chans3 // 2, LANES), BF16),
        half,
        *down_pieces,
        dpre3,
    )
    dpre_pieces = coarse_pieces(dpre3)
    coarse_grad, *dpre_pieces = lax.optimization_barrier((coarse_grad, *dpre_pieces))

    dpre2, grads = call(
        partial(back_kernel, batch),
        (shape(own.shape, BF16), shape((grad_rows, LANES), BF16)),
        half,
        *dpre_pieces,
        *feature_pieces,
        coarse_back,
        up_matrix,
        unsort,
        sorted_act,
        slope,
        coarse_grad,
    )
    coarse = jnp.where(upper_half() == 0, coarse[: width // 2], coarse[-(width // 2) :])
    grads = grads.reshape(len(near[0]), -1, LANES)
    kept = grads.shape[1]
    coarse = for_plane(coarse.reshape(batch, QUARTERS, 8, LANES))
    mixed = trade(jnp.concatenate([grads, coarse], axis=1), ("grp", "sp"), near)
    part = jnp.sum(mixed[:, :kept].astype(F32), axis=0).astype(BF16)
    coarse = for_column(mixed[:, kept:])
    spread = last_pieces(dpre2, batch * x_cells)
    part, coarse, *spread[1:] = lax.optimization_barrier((part, coarse, *spread[1:]))
    gradient = call(
        input_kernel,
        shape((batch * x_cells, *own.shape[1:]), BF16),
        half,
        *spread,
        fine_back,
    )
    gradient = far_exchange(gradient.reshape(batch // 4, 2, 2, x_cells, y_cells, chans, LANES))
    part = jnp.broadcast_to(part[None], (coarse.shape[0], *part.shape))
    mixed = trade(jnp.concatenate([part, coarse], axis=1), ("grp", "sp"), columns())
    part = jnp.sum(mixed[:, :kept].astype(F32), axis=0).astype(BF16)
    coarse = from_column(mixed[:, kept:])
    grads = share(part, ("grp", "sp"), near).reshape(grad_rows, LANES)
    result = pl.pallas_call(
        unpack_kernel, out_shape=shape((chans3, width), BF16), interpret=INTERPRET
    )(coarse)
    grads, gradient, result = lax.optimization_barrier((grads, gradient, result))
    gradient = near_exchange(gradient)
    grad_input = jnp.transpose(gradient, (0, 2, 1, 5, 3, 4, 6)).reshape(features.shape)

    result = result.reshape(cotangent.shape)

    grad_fine, grad_down, grad_coarse = pl.pallas_call(
        partial(assemble_kernel, fine_scale, coarse_scale),
        out_shape=(
            shape(weight_fine.shape, F32),
            shape((8, chans, chans3), F32),
            shape(weight_coarse.shape, F32),
        ),
        interpret=INTERPRET,
    )(grads)
    return result, grad_input, grad_fine, jnp.swapaxes(grad_down, 1, 2), grad_coarse


def solution(mesh):
    placed = (P(None, None, "sp", "grp", None), P(), P(), P(), P("grp", None, "sp", None))
    return jax.shard_map(
        local,
        mesh=mesh,
        in_specs=placed,
        out_specs=(P("grp", None, "sp", None), P(None, None, "sp", "grp", None), P(), P(), P()),
        check_vma=False,
    )
```
